512 devices in a mesh: space: 32 (over y_lo, z, core), grain: 16 (over x, y_hi).
Axes of the slice: x: 4, y: 8 (y_hi: 4, y_lo: 2; y = y_hi * 2 + y_lo), z: 8, core: 2. Of those that a mesh axis runs over, the one named last changes fastest.
Arguments:
- grain_ids: int32 [3, 512, 2048], P(None, 'space'), may hold values from 0 to 95
- group_of: int32 [96], P('grain'), may hold values from 0 to 3
- group_mobility: float32 [4], replicated, may hold values from 0.3 to 1.5
- seed_noise: float32 [96, 3, 512, 2048], P('grain', None, 'space'), may hold values from -0.25 to 0.25
- concentration: float32 [3, 512, 2048], P(None, 'space'), may hold values from 0.1 to 0.7
Outputs:
- order_params: float32 [96, 3, 512, 2048], P('grain', None, 'space')
- solute: float32 [3, 512, 2048], P(None, 'space')
The draws below stay inside these ranges and needn't reach their ends.
All inputs are finite; a program needn't handle non-finite values.
Results may differ from the reference program's by a relative error of at most 0.0001.
Values sent between devices are 32-bit elements; how exact they have to be, the bound alone decides.
No kernel may reach another device: no remote copies, remote signals or barrier semaphores. Data moves between devices by JAX's collectives and lax.ppermute only.
A program may use at most 64 MiB of HBM per device.

```python
import math
import jax
import jax.numpy as jnp

GRAINS = 96
PLANES = 3
NY = 2048
NX = 512
GROUPS = 4
STEPS = 2


def place_ends(array, stream_key, least, top_value):
    index_at = [jax.random.randint(jax.random.fold_in(stream_key, axis), (), 0, length) for axis, length in enumerate(array.shape)]
    widest = array.shape.index(max(array.shape))
    next_to = index_at[:widest] + [(index_at[widest] + 1) % array.shape[widest]] + index_at[widest + 1:]
    return array.at[tuple(index_at)].set(least).at[tuple(next_to)].set(top_value)


def steps_of(own_key, shape, cuts, low, largest):
    gain, own = 1.0, jax.random.fold_in(own_key, 6)
    for dim, blocks in cuts:
        draws = jnp.exp(jax.random.uniform(jax.random.fold_in(own, dim), (blocks,), jnp.float32, low / len(cuts), largest / len(cuts)))
        gain = gain * jnp.repeat(draws, shape[dim] // blocks).reshape([-1 if axis == dim else 1 for axis in range(len(shape))])
    return gain


def setup_inputs(seed: int = 0) -> dict:
    streams_of = jax.random.split(jax.random.key(seed), 6)
    grain_ids = place_ends(jax.random.randint(streams_of[0], (PLANES, NX, NY), 0, GRAINS), jax.random.fold_in(streams_of[0], 1), 0, GRAINS - 1).astype(jnp.int32)
    group_of = place_ends(jax.random.randint(streams_of[1], (GRAINS,), 0, GROUPS), jax.random.fold_in(streams_of[1], 1), 0, GROUPS - 1).astype(jnp.int32)
    group_mobility = jnp.clip(jnp.exp(jax.random.uniform(streams_of[2], (GROUPS,), jnp.float32, math.log(0.3), math.log(1.5))), 0.3, 1.5)
    seed_noise = jnp.clip(jax.random.uniform(streams_of[3], (GRAINS, PLANES, NX, NY), jnp.float32, -0.25, 0.25) * steps_of(streams_of[3], (GRAINS, PLANES, NX, NY), ((0, 16), (2, 32)), -0.4, 0.0), -0.25, 0.25)
    concentration = jnp.clip(0.1 + 0.59999999 * jax.random.uniform(streams_of[4], (PLANES, NX, NY), jnp.float32) ** steps_of(streams_of[4], (PLANES, NX, NY), ((1, 32),), -0.2, 0.2), 0.1, 0.7)
    return dict(grain_ids=grain_ids, group_of=group_of, group_mobility=group_mobility, seed_noise=seed_noise, concentration=concentration)


coef_quad = 1.0
coef_quart = 1.0
cross_gamma = 1.5
gradient_kappa = 0.5
solute_beta = 0.6
bulk_stiff = 1.0
solute_mean = 0.4
solute_kappa = 0.25
solute_mobility = 0.3
time_step = 0.1


def laplace(field):
    along_x = jnp.roll(field, 1, -2) + jnp.roll(field, -1, -2)
    along_y = jnp.roll(field, 1, -1) + jnp.roll(field, -1, -1)
    edged = jnp.concatenate([field[..., :1, :, :], field, field[..., -1:, :, :]], axis=-3)
    along_z = edged[..., 2:, :, :] + edged[..., :-2, :, :]
    return along_x + along_y + along_z - 6.0 * field


def reference(grain_ids, group_of, group_mobility, seed_noise, concentration):
    grains = jnp.arange(GRAINS, dtype=jnp.int32)
    eta = (grain_ids[None] == grains[:, None, None, None]).astype(jnp.float32) * 0.9 + seed_noise
    mobility = group_mobility[group_of]
    solute = concentration
    for step in range(STEPS):
        square = eta * eta
        sum_two = jnp.sum(square, 0)
        sum_four = jnp.sum(square * square, 0)
        potential = 2.0 * bulk_stiff * (solute - solute_mean) - solute_beta * (sum_two * sum_two - sum_four) - solute_kappa * laplace(solute)
        force = -coef_quad * eta + coef_quart * eta * square + eta * (sum_two[None] - square) * (2.0 * cross_gamma - 4.0 * solute_beta * solute)[None] - gradient_kappa * laplace(eta)
        new_solute = solute + time_step * solute_mobility * laplace(potential)
        eta = eta - time_step * mobility[:, None, None, None] * force
        solute = new_solute
    return eta, solute
```

```python
import jax
import jax.numpy as jnp
from jax import lax
from jax.experimental import pallas as pl
from jax.experimental.pallas import tpu as pltpu
from jax.sharding import Mesh, PartitionSpec as P

GRAINS, PLANES, ROWS, COLS, LANES = 6, 3, 16, 2048, 128
BLOCKS = COLS // LANES
SPACE = ("yl", "z", "core")
GRAIN = ("x", "yh")

coef_quad = 1.0
coef_quart = 1.0
cross_gamma = 1.5
gradient_kappa = 0.5
solute_beta = 0.6
bulk_stiff = 1.0
solute_mean = 0.4
solute_kappa = 0.25
solute_mobility = 0.3
time_step = 0.1

F32 = jnp.float32
VMEM_LIMIT = 48 * 1024 * 1024


def shape(*dims):
    return jax.ShapeDtypeStruct(dims, F32)


def params():
    return pltpu.CompilerParams(vmem_limit_bytes=VMEM_LIMIT)


def whole(*dims):
    return pl.BlockSpec(dims, lambda *_: (0,) * len(dims))


def smem():
    return pl.BlockSpec(memory_space=pltpu.SMEM)


def along_columns(value):
    return pltpu.roll(value, 1, 1) + pltpu.roll(value, COLS - 1, 1)


def beside(planes):
    return (planes[0] + planes[1], planes[0] + planes[2], planes[1] + planes[2])


def column_block(block):
    return slice(block * LANES, (block + 1) * LANES)


def first_sums(first_ref, noise_ref, ids_ref, solute_ref, sums_ref, next_ref, prev_ref):
    for plane in range(PLANES):
        ids = ids_ref[plane]
        two = four = None
        for grain in range(GRAINS):
            seed = jnp.where(ids == first_ref[0] + grain, 0.9, 0.0).astype(F32)
            eta = seed + noise_ref[grain, plane]
            row = grain * PLANES + plane
            prev_ref[row : row + 1, :] = eta[:1]
            next_ref[row : row + 1, :] = eta[ROWS - 1 :]
            square = eta * eta
            two = square if two is None else two + square
            four = square * square if four is None else four + square * square
        for block in range(sums_ref.shape[0]):
            sums_ref[block, plane] = two[:, column_block(block)]
            sums_ref[block, PLANES + plane] = four[:, column_block(block)]
        row = GRAINS * PLANES + 3 * plane
        prev_ref[row : row + 3, :] = solute_ref[plane, :3]
        next_ref[row : row + 3, :] = solute_ref[plane, ROWS - 3 :]


def call_first_sums(first, noise, ids, solute):
    width = 512
    edge = GRAINS * PLANES + 3 * PLANES
    return pl.pallas_call(
        first_sums,
        grid=(COLS // width,),
        in_specs=[
            smem(),
            pl.BlockSpec((GRAINS, PLANES, ROWS, width), lambda i: (0, 0, 0, i)),
            pl.BlockSpec((PLANES, ROWS, width), lambda i: (0, 0, i)),
            pl.BlockSpec((PLANES, ROWS, width), lambda i: (0, 0, i)),
        ],
        out_specs=[
            pl.BlockSpec((width // LANES, 2 * PLANES, ROWS, LANES), lambda i: (i, 0, 0, 0)),
            pl.BlockSpec((edge, width), lambda i: (0, i)),
            pl.BlockSpec((edge, width), lambda i: (0, i)),
        ],
        out_shape=[
            shape(BLOCKS, 2 * PLANES, ROWS, LANES),
            shape(edge, COLS),
            shape(edge, COLS),
        ],
        compiler_params=params(),
        name="first_sums",
    )(first, noise, ids, solute)


def factors(sums_ref, solute_ref, base_ref, slope_ref):
    for plane in range(PLANES):
        for block in range(BLOCKS):
            columns = column_block(block)
            cross = 2.0 * cross_gamma - 4.0 * solute_beta * solute_ref[plane, :, columns]
            base_ref[plane, :, columns] = (
                coef_quad - 6.0 * gradient_kappa - sums_ref[block, plane] * cross
            )
            slope_ref[plane, :, columns] = cross - coef_quart


def stepped(planes, above, below, rate, base_ref, slope_ref):
    rows = lax.broadcasted_iota(jnp.int32, (ROWS, COLS), 0)
    out = []
    for plane, across in zip(range(PLANES), beside(planes)):
        eta = planes[plane]
        up = jnp.where(rows == 0, above[plane], pltpu.roll(eta, 1, 0))
        down = jnp.where(rows == ROWS - 1, below[plane], pltpu.roll(eta, ROWS - 1, 0))
        around = up + down + along_columns(eta) + across
        bracket = base_ref[plane] + slope_ref[plane] * (eta * eta)
        out.append(eta + rate * (eta * bracket + gradient_kappa * around))
    return out


def halo_rows(ref, grain):
    return [ref[pl.ds(grain * PLANES + plane, 1), :] for plane in range(PLANES)]


def first_step(
    first_ref, group_ref, mobility_ref, noise_ref, ids_ref, solute_ref, sums_ref, above_ref, below_ref,
    eta_ref, next_sums_ref, next_ref, prev_ref, base_ref, slope_ref,
):
    grain = pl.program_id(0)

    @pl.when(grain == 0)
    def _():
        factors(sums_ref, solute_ref, base_ref, slope_ref)
        for plane in range(PLANES):
            row = GRAINS * PLANES + 2 * plane
            for block in range(BLOCKS):
                columns = column_block(block)
                two, four = sums_ref[block, plane], sums_ref[block, PLANES + plane]
                bulk = solute_beta * (two * two - four)
                prev_ref[row : row + 2, columns] = bulk[:2]
                next_ref[row : row + 2, columns] = bulk[ROWS - 2 :]

    rate = time_step * mobility_ref[group_ref[grain]]
    planes = [
        jnp.where(ids_ref[plane] == first_ref[0] + grain, 0.9, 0.0).astype(F32) + noise_ref[0, plane]
        for plane in range(PLANES)
    ]
    out = stepped(planes, halo_rows(above_ref, grain), halo_rows(below_ref, grain), rate, base_ref, slope_ref)
    for plane in range(PLANES):
        eta = out[plane]
        eta_ref[0, plane] = eta
        row = pl.ds(grain * PLANES + plane, 1)
        prev_ref[row, :] = eta[:1]
        next_ref[row, :] = eta[ROWS - 1 :]
    for plane in range(PLANES):
        square = out[plane] * out[plane]
        fourth = square * square

        @pl.when(grain == 0)
        def _():
            for block in range(BLOCKS):
                next_sums_ref[block, plane] = square[:, column_block(block)]
                next_sums_ref[block, PLANES + plane] = fourth[:, column_block(block)]

        @pl.when(grain != 0)
        def _():
            for block in range(BLOCKS):
                next_sums_ref[block, plane] += square[:, column_block(block)]
                next_sums_ref[block, PLANES + plane] += fourth[:, column_block(block)]


def call_first_step(first, groups, mobility, noise, ids, solute, sums, above, below):
    edge = GRAINS * PLANES + 2 * PLANES
    grain_block = pl.BlockSpec((1, PLANES, ROWS, COLS), lambda i: (i, 0, 0, 0))
    return pl.pallas_call(
        first_step,
        grid=(GRAINS,),
        in_specs=[
            smem(), smem(), smem(), grain_block,
            whole(*ids.shape), whole(*solute.shape), whole(*sums.shape),
            whole(*above.shape), whole(*below.shape),
        ],
        out_specs=[grain_block, whole(*sums.shape), whole(edge, COLS), whole(edge, COLS)],
        out_shape=[shape(*noise.shape), shape(*sums.shape), shape(edge, COLS), shape(edge, COLS)],
        scratch_shapes=[pltpu.VMEM(solute.shape, F32)] * 2,
        compiler_params=params(),
        name="first_step",
    )(first, groups, mobility, noise, ids, solute, sums, above, below)


PAD = 8
DEEP = ROWS + 2 * PAD


def laplace(planes):
    height = planes[0].shape[0]
    return [
        pltpu.roll(value, 1, 0) + pltpu.roll(value, height - 1, 0) + along_columns(value) + across - 6.0 * value
        for value, across in zip(planes, beside(planes))
    ]


def solute_step(
    solute_ref, sums_ref, above_ref, below_ref, mid_above_ref, mid_below_ref,
    out_ref, part_ref, deep_ref, bulk_ref,
):
    for plane in range(PLANES):
        for ref in (deep_ref, bulk_ref):
            ref[plane, :PAD] = jnp.zeros((PAD, COLS), F32)
            ref[plane, PAD + ROWS :] = jnp.zeros((PAD, COLS), F32)
        row = GRAINS * PLANES + 3 * plane
        deep_ref[plane, PAD - 3 : PAD] = above_ref[row : row + 3, :]
        deep_ref[plane, PAD : PAD + ROWS] = solute_ref[plane]
        deep_ref[plane, PAD + ROWS : PAD + ROWS + 3] = below_ref[row : row + 3, :]
        row = GRAINS * PLANES + 2 * plane
        bulk_ref[plane, PAD - 2 : PAD] = mid_above_ref[row : row + 2, :]
        bulk_ref[plane, PAD + ROWS : PAD + ROWS + 2] = mid_below_ref[row : row + 2, :]
        for block in range(BLOCKS):
            two, four = sums_ref[block, plane], sums_ref[block, PLANES + plane]
            bulk_ref[plane, PAD : PAD + ROWS, column_block(block)] = solute_beta * (two * two - four)
    solute = [deep_ref[plane] for plane in range(PLANES)]
    potential = [
        2.0 * bulk_stiff * (solute[plane] - solute_mean) - bulk_ref[plane] - solute_kappa * lap
        for plane, lap in enumerate(laplace(solute))
    ]
    moved = [
        solute[plane] + time_step * solute_mobility * lap for plane, lap in enumerate(laplace(potential))
    ]
    for plane, lap in enumerate(laplace(moved)):
        part = 2.0 * bulk_stiff * (moved[plane] - solute_mean) - solute_kappa * lap
        out_ref[plane] = moved[plane][PAD : PAD + ROWS]
        part_ref[plane] = part[PAD : PAD + ROWS]


def call_solute_step(solute, sums, above, below, mid_above, mid_below):
    return pl.pallas_call(
        solute_step,
        out_shape=[shape(*solute.shape)] * 2,
        scratch_shapes=[pltpu.VMEM((PLANES, DEEP, COLS), F32)] * 2,
        compiler_params=params(),
        name="solute_step",
    )(solute, sums, above, below, mid_above, mid_below)


def second_potential(part_ref, sums_ref, out_ref, next_ref, prev_ref):
    for plane in range(PLANES):
        for block in range(BLOCKS):
            columns = column_block(block)
            two, four = sums_ref[block, plane], sums_ref[block, PLANES + plane]
            potential = part_ref[plane, :, columns] - solute_beta * (two * two - four)
            out_ref[plane, :, columns] = potential
            prev_ref[plane : plane + 1, columns] = potential[:1]
            next_ref[plane : plane + 1, columns] = potential[ROWS - 1 :]


def call_second_potential(part, sums):
    return pl.pallas_call(
        second_potential,
        out_shape=[shape(*part.shape), shape(PLANES, COLS), shape(PLANES, COLS)],
        compiler_params=params(),
        name="second_potential",
    )(part, sums)


def second_step(
    group_ref, mobility_ref, old_ref, solute_ref, sums_ref, above_ref, below_ref, eta_ref, base_ref, slope_ref
):
    grain = pl.program_id(0)

    @pl.when(grain == 0)
    def _():
        factors(sums_ref, solute_ref, base_ref, slope_ref)

    rate = time_step * mobility_ref[group_ref[grain]]
    planes = [old_ref[0, plane] for plane in range(PLANES)]
    out = stepped(planes, halo_rows(above_ref, grain), halo_rows(below_ref, grain), rate, base_ref, slope_ref)
    for plane in range(PLANES):
        eta_ref[0, plane] = out[plane]


def call_second_step(groups, mobility, eta, solute, sums, above, below):
    grain_block = pl.BlockSpec((1, PLANES, ROWS, COLS), lambda i: (i, 0, 0, 0))
    return pl.pallas_call(
        second_step,
        grid=(GRAINS,),
        in_specs=[
            smem(), smem(), grain_block, whole(*solute.shape), whole(*sums.shape),
            whole(*above.shape), whole(*below.shape),
        ],
        out_specs=grain_block,
        out_shape=shape(*eta.shape),
        scratch_shapes=[pltpu.VMEM(solute.shape, F32)] * 2,
        compiler_params=params(),
        cost_estimate=pl.CostEstimate(flops=20_000_000, bytes_accessed=10_000_000, transcendentals=0),
        name="second_step",
    )(groups, mobility, eta, solute, sums, above, below)


def solute_end(solute_ref, potential_ref, above_ref, below_ref, out_ref):
    rows = lax.broadcasted_iota(jnp.int32, (ROWS, COLS), 0)
    planes = [potential_ref[plane] for plane in range(PLANES)]
    for plane, across in enumerate(beside(planes)):
        value = planes[plane]
        up = jnp.where(rows == 0, above_ref[plane : plane + 1, :], pltpu.roll(value, 1, 0))
        down = jnp.where(rows == ROWS - 1, below_ref[plane : plane + 1, :], pltpu.roll(value, ROWS - 1, 0))
        lap = up + down + along_columns(value) + across - 6.0 * value
        out_ref[plane] = solute_ref[plane] + time_step * solute_mobility * lap


def call_solute_end(solute, potential, above, below):
    return pl.pallas_call(
        solute_end,
        out_shape=shape(*solute.shape),
        compiler_params=params(),
        name="solute_end",
    )(solute, potential, above, below)


def exchange(to_next, to_prev, count):
    above = lax.ppermute(to_next, SPACE, [(i, (i + 1) % count) for i in range(count)])
    below = lax.ppermute(to_prev, SPACE, [((i + 1) % count, i) for i in range(count)])
    return above, below


def total(sums):
    along, across = lax.axis_size("x"), lax.axis_size("yh")
    parts = sums.reshape((along, across) + sums.shape[1:])
    parts = jnp.sum(lax.all_to_all(parts, "x", 0, 0, tiled=True), 0)
    parts = jnp.sum(lax.all_to_all(parts, "yh", 0, 0, tiled=True), 0)
    parts = lax.all_gather(parts, "yh", axis=0)
    return lax.all_gather(parts, "x", axis=0).reshape(sums.shape)


def shards(grain_ids, group_of, group_mobility, seed_noise, concentration):
    count = lax.axis_size("yl") * lax.axis_size("z") * lax.axis_size("core")
    first = (lax.axis_index(GRAIN) * GRAINS).astype(jnp.int32).reshape(1)
    sums, to_next, to_prev = call_first_sums(first, seed_noise, grain_ids, concentration)
    above, below = exchange(to_next, to_prev, count)
    sums = total(sums)
    eta, next_sums, to_next, to_prev = call_first_step(
        first, group_of, group_mobility, seed_noise, grain_ids, concentration, sums, above, below
    )
    mid_above, mid_below = exchange(to_next, to_prev, count)
    next_sums = total(next_sums)
    solute, part = call_solute_step(concentration, sums, above, below, mid_above, mid_below)
    potential, to_next, to_prev = call_second_potential(part, next_sums)
    end_above, end_below = exchange(to_next, to_prev, count)
    eta = call_second_step(group_of, group_mobility, eta, solute, next_sums, mid_above, mid_below)
    solute = call_solute_end(solute, potential, end_above, end_below)
    return eta, solute


def solution(mesh):
    fine = Mesh(mesh.devices.reshape(2, 8, 2, 4, 4), SPACE + GRAIN)
    placed = (
        P(None, SPACE, None),
        P(GRAIN),
        P(),
        P(GRAIN, None, SPACE, None),
        P(None, SPACE, None),
    )
    return jax.shard_map(
        shards,
        mesh=fine,
        in_specs=placed,
        out_specs=(P(GRAIN, None, SPACE, None), P(None, SPACE, None)),
        check_vma=False,
    )
```

```python
import jax
import jax.numpy as jnp
from jax import lax
from jax.experimental import pallas as pl
from jax.experimental.pallas import tpu as pltpu
from jax.sharding import Mesh, PartitionSpec as P

GRAINS, PLANES, ROWS, COLS, LANES = 6, 3, 16, 2048, 128
BLOCKS = COLS // LANES
SPACE = ("yl", "z", "core")
GRAIN = ("x", "yh")

coef_quad = 1.0
coef_quart = 1.0
cross_gamma = 1.5
gradient_kappa = 0.5
solute_beta = 0.6
bulk_stiff = 1.0
solute_mean = 0.4
solute_kappa = 0.25
solute_mobility = 0.3
time_step = 0.1

F32 = jnp.float32
MIB = 1024 * 1024


def shape(*dims):
    return jax.ShapeDtypeStruct(dims, F32)


def params(mib=16):
    return pltpu.CompilerParams(vmem_limit_bytes=mib * MIB)


def whole(*dims):
    return pl.BlockSpec(dims, lambda *_: (0,) * len(dims))


def smem():
    return pl.BlockSpec(memory_space=pltpu.SMEM)


def along_columns(value):
    return pltpu.roll(value, 1, 1) + pltpu.roll(value, COLS - 1, 1)


def beside(planes):
    return (planes[0] + planes[1], planes[0] + planes[2], planes[1] + planes[2])


def column_block(block):
    return slice(block * LANES, (block + 1) * LANES)


def first_sums(first_ref, noise_ref, ids_ref, solute_ref, sums_ref, next_ref, prev_ref):
    for plane in range(PLANES):
        ids = ids_ref[plane]
        two = four = None
        for grain in range(GRAINS):
            seed = jnp.where(ids == first_ref[0] + grain, 0.9, 0.0).astype(F32)
            eta = seed + noise_ref[grain, plane]
            row = grain * PLANES + plane
            prev_ref[row : row + 1, :] = eta[:1]
            next_ref[row : row + 1, :] = eta[ROWS - 1 :]
            square = eta * eta
            two = square if two is None else two + square
            four = square * square if four is None else four + square * square
        for block in range(sums_ref.shape[0]):
            sums_ref[block, plane] = two[:, column_block(block)]
            sums_ref[block, PLANES + plane] = four[:, column_block(block)]
        row = GRAINS * PLANES + 3 * plane
        prev_ref[row : row + 3, :] = solute_ref[plane, :3]
        next_ref[row : row + 3, :] = solute_ref[plane, ROWS - 3 :]


def call_first_sums(first, noise, ids, solute):
    width = 512
    edge = GRAINS * PLANES + 3 * PLANES
    return pl.pallas_call(
        first_sums,
        grid=(COLS // width,),
        in_specs=[
            smem(),
            pl.BlockSpec((GRAINS, PLANES, ROWS, width), lambda i: (0, 0, 0, i)),
            pl.BlockSpec((PLANES, ROWS, width), lambda i: (0, 0, i)),
            pl.BlockSpec((PLANES, ROWS, width), lambda i: (0, 0, i)),
        ],
        out_specs=[
            pl.BlockSpec((width // LANES, 2 * PLANES, ROWS, LANES), lambda i: (i, 0, 0, 0)),
            pl.BlockSpec((edge, width), lambda i: (0, i)),
            pl.BlockSpec((edge, width), lambda i: (0, i)),
        ],
        out_shape=[
            shape(BLOCKS, 2 * PLANES, ROWS, LANES),
            shape(edge, COLS),
            shape(edge, COLS),
        ],
        compiler_params=params(60),
        name="first_sums",
    )(first, noise, ids, solute)


def factors(sums_ref, solute_ref, base_ref, slope_ref):
    for plane in range(PLANES):
        for block in range(BLOCKS):
            columns = column_block(block)
            cross = 2.0 * cross_gamma - 4.0 * solute_beta * solute_ref[plane, :, columns]
            base_ref[plane, :, columns] = (
                coef_quad - 6.0 * gradient_kappa - sums_ref[block, plane] * cross
            )
            slope_ref[plane, :, columns] = cross - coef_quart


def stepped(planes, above, below, rate, base_ref, slope_ref):
    rows = lax.broadcasted_iota(jnp.int32, (ROWS, COLS), 0)
    out = []
    for plane, across in zip(range(PLANES), beside(planes)):
        eta = planes[plane]
        up = jnp.where(rows == 0, above[plane], pltpu.roll(eta, 1, 0))
        down = jnp.where(rows == ROWS - 1, below[plane], pltpu.roll(eta, ROWS - 1, 0))
        around = up + down + along_columns(eta) + across
        bracket = base_ref[plane] + slope_ref[plane] * (eta * eta)
        out.append(eta + rate * (eta * bracket + gradient_kappa * around))
    return out


def halo_rows(ref, grain):
    return [ref[pl.ds(grain * PLANES + plane, 1), :] for plane in range(PLANES)]


def first_step(
    first_ref, group_ref, mobility_ref, noise_ref, ids_ref, solute_ref, sums_ref, above_ref, below_ref,
    eta_ref, next_sums_ref, next_ref, prev_ref, base_ref, slope_ref,
):
    grain = pl.program_id(0)

    @pl.when(grain == 0)
    def _():
        factors(sums_ref, solute_ref, base_ref, slope_ref)
        for plane in range(PLANES):
            row = GRAINS * PLANES + 2 * plane
            for block in range(BLOCKS):
                columns = column_block(block)
                two, four = sums_ref[block, plane], sums_ref[block, PLANES + plane]
                bulk = solute_beta * (two * two - four)
                prev_ref[row : row + 2, columns] = bulk[:2]
                next_ref[row : row + 2, columns] = bulk[ROWS - 2 :]

    rate = time_step * mobility_ref[group_ref[grain]]
    planes = [
        jnp.where(ids_ref[plane] == first_ref[0] + grain, 0.9, 0.0).astype(F32) + noise_ref[0, plane]
        for plane in range(PLANES)
    ]
    out = stepped(planes, halo_rows(above_ref, grain), halo_rows(below_ref, grain), rate, base_ref, slope_ref)
    for plane in range(PLANES):
        eta = out[plane]
        eta_ref[0, plane] = eta
        row = pl.ds(grain * PLANES + plane, 1)
        prev_ref[row, :] = eta[:1]
        next_ref[row, :] = eta[ROWS - 1 :]
    for plane in range(PLANES):
        square = out[plane] * out[plane]
        fourth = square * square

        @pl.when(grain == 0)
        def _():
            for block in range(BLOCKS):
                next_sums_ref[block, plane] = square[:, column_block(block)]
                next_sums_ref[block, PLANES + plane] = fourth[:, column_block(block)]

        @pl.when(grain != 0)
        def _():
            for block in range(BLOCKS):
                next_sums_ref[block, plane] += square[:, column_block(block)]
                next_sums_ref[block, PLANES + plane] += fourth[:, column_block(block)]


def call_first_step(first, groups, mobility, noise, ids, solute, sums, above, below):
    edge = GRAINS * PLANES + 2 * PLANES
    grain_block = pl.BlockSpec((1, PLANES, ROWS, COLS), lambda i: (i, 0, 0, 0))
    return pl.pallas_call(
        first_step,
        grid=(GRAINS,),
        in_specs=[
            smem(), smem(), smem(), grain_block,
            whole(*ids.shape), whole(*solute.shape), whole(*sums.shape),
            whole(*above.shape), whole(*below.shape),
        ],
        out_specs=[grain_block, whole(*sums.shape), whole(edge, COLS), whole(edge, COLS)],
        out_shape=[shape(*noise.shape), shape(*sums.shape), shape(edge, COLS), shape(edge, COLS)],
        scratch_shapes=[pltpu.VMEM(solute.shape, F32)] * 2,
        compiler_params=params(),
        name="first_step",
    )(first, groups, mobility, noise, ids, solute, sums, above, below)


PAD = 8
DEEP = ROWS + 2 * PAD


def laplace(planes):
    height = planes[0].shape[0]
    return [
        pltpu.roll(value, 1, 0) + pltpu.roll(value, height - 1, 0) + along_columns(value) + across - 6.0 * value
        for value, across in zip(planes, beside(planes))
    ]


def solute_step(
    solute_ref, sums_ref, above_ref, below_ref, mid_above_ref, mid_below_ref,
    out_ref, part_ref, deep_ref, bulk_ref,
):
    for plane in range(PLANES):
        for ref in (deep_ref, bulk_ref):
            ref[plane, :PAD] = jnp.zeros((PAD, COLS), F32)
            ref[plane, PAD + ROWS :] = jnp.zeros((PAD, COLS), F32)
        row = GRAINS * PLANES + 3 * plane
        deep_ref[plane, PAD - 3 : PAD] = above_ref[row : row + 3, :]
        deep_ref[plane, PAD : PAD + ROWS] = solute_ref[plane]
        deep_ref[plane, PAD + ROWS : PAD + ROWS + 3] = below_ref[row : row + 3, :]
        row = GRAINS * PLANES + 2 * plane
        bulk_ref[plane, PAD - 2 : PAD] = mid_above_ref[row : row + 2, :]
        bulk_ref[plane, PAD + ROWS : PAD + ROWS + 2] = mid_below_ref[row : row + 2, :]
        for block in range(BLOCKS):
            two, four = sums_ref[block, plane], sums_ref[block, PLANES + plane]
            bulk_ref[plane, PAD : PAD + ROWS, column_block(block)] = solute_beta * (two * two - four)
    solute = [deep_ref[plane] for plane in range(PLANES)]
    potential = [
        2.0 * bulk_stiff * (solute[plane] - solute_mean) - bulk_ref[plane] - solute_kappa * lap
        for plane, lap in enumerate(laplace(solute))
    ]
    moved = [
        solute[plane] + time_step * solute_mobility * lap for plane, lap in enumerate(laplace(potential))
    ]
    for plane, lap in enumerate(laplace(moved)):
        part = 2.0 * bulk_stiff * (moved[plane] - solute_mean) - solute_kappa * lap
        out_ref[plane] = moved[plane][PAD : PAD + ROWS]
        part_ref[plane] = part[PAD : PAD + ROWS]


def call_solute_step(solute, sums, above, below, mid_above, mid_below):
    return pl.pallas_call(
        solute_step,
        out_shape=[shape(*solute.shape)] * 2,
        scratch_shapes=[pltpu.VMEM((PLANES, DEEP, COLS), F32)] * 2,
        compiler_params=params(),
        name="solute_step",
    )(solute, sums, above, below, mid_above, mid_below)


def second_potential(part_ref, sums_ref, out_ref, next_ref, prev_ref):
    for plane in range(PLANES):
        for block in range(BLOCKS):
            columns = column_block(block)
            two, four = sums_ref[block, plane], sums_ref[block, PLANES + plane]
            potential = part_ref[plane, :, columns] - solute_beta * (two * two - four)
            out_ref[plane, :, columns] = potential
            prev_ref[plane : plane + 1, columns] = potential[:1]
            next_ref[plane : plane + 1, columns] = potential[ROWS - 1 :]


def call_second_potential(part, sums):
    return pl.pallas_call(
        second_potential,
        out_shape=[shape(*part.shape), shape(PLANES, COLS), shape(PLANES, COLS)],
        compiler_params=params(),
        name="second_potential",
    )(part, sums)


def second_step(
    group_ref, mobility_ref, old_ref, solute_ref, sums_ref, above_ref, below_ref, eta_ref, base_ref, slope_ref
):
    grain = pl.program_id(0)

    @pl.when(grain == 0)
    def _():
        factors(sums_ref, solute_ref, base_ref, slope_ref)

    rate = time_step * mobility_ref[group_ref[grain]]
    planes = [old_ref[0, plane] for plane in range(PLANES)]
    out = stepped(planes, halo_rows(above_ref, grain), halo_rows(below_ref, grain), rate, base_ref, slope_ref)
    for plane in range(PLANES):
        eta_ref[0, plane] = out[plane]


def call_second_step(groups, mobility, eta, solute, sums, above, below):
    grain_block = pl.BlockSpec((1, PLANES, ROWS, COLS), lambda i: (i, 0, 0, 0))
    return pl.pallas_call(
        second_step,
        grid=(GRAINS,),
        in_specs=[
            smem(), smem(), grain_block, whole(*solute.shape), whole(*sums.shape),
            whole(*above.shape), whole(*below.shape),
        ],
        out_specs=grain_block,
        out_shape=shape(*eta.shape),
        scratch_shapes=[pltpu.VMEM(solute.shape, F32)] * 2,
        compiler_params=params(),
        cost_estimate=pl.CostEstimate(flops=20_000_000, bytes_accessed=10_000_000, transcendentals=0),
        name="second_step",
    )(groups, mobility, eta, solute, sums, above, below)


def solute_end(solute_ref, potential_ref, above_ref, below_ref, out_ref):
    rows = lax.broadcasted_iota(jnp.int32, (ROWS, COLS), 0)
    planes = [potential_ref[plane] for plane in range(PLANES)]
    for plane, across in enumerate(beside(planes)):
        value = planes[plane]
        up = jnp.where(rows == 0, above_ref[plane : plane + 1, :], pltpu.roll(value, 1, 0))
        down = jnp.where(rows == ROWS - 1, below_ref[plane : plane + 1, :], pltpu.roll(value, ROWS - 1, 0))
        lap = up + down + along_columns(value) + across - 6.0 * value
        out_ref[plane] = solute_ref[plane] + time_step * solute_mobility * lap


def call_solute_end(solute, potential, above, below):
    return pl.pallas_call(
        solute_end,
        out_shape=shape(*solute.shape),
        compiler_params=params(),
        name="solute_end",
    )(solute, potential, above, below)


def exchange(to_next, to_prev, count):
    above = lax.ppermute(to_next, SPACE, [(i, (i + 1) % count) for i in range(count)])
    below = lax.ppermute(to_prev, SPACE, [((i + 1) % count, i) for i in range(count)])
    return above, below


def spread(value, axis):
    copies = jnp.broadcast_to(value[None], (lax.axis_size(axis),) + value.shape)
    return lax.all_to_all(copies, axis, 0, 0, tiled=True)


def total(sums):
    along = lax.axis_size("x")
    parts = sums.reshape((along, BLOCKS // along) + sums.shape[1:])
    parts = jnp.sum(lax.all_to_all(parts, "x", 0, 0, tiled=True), 0)
    parts = jnp.sum(spread(parts, "yh"), 0)
    return spread(parts, "x").reshape(sums.shape)


def shards(grain_ids, group_of, group_mobility, seed_noise, concentration):
    count = lax.axis_size("yl") * lax.axis_size("z") * lax.axis_size("core")
    first = (lax.axis_index(GRAIN) * GRAINS).astype(jnp.int32).reshape(1)
    sums, to_next, to_prev = call_first_sums(first, seed_noise, grain_ids, concentration)
    above, below = exchange(to_next, to_prev, count)
    sums = total(sums)
    eta, next_sums, to_next, to_prev = call_first_step(
        first, group_of, group_mobility, seed_noise, grain_ids, concentration, sums, above, below
    )
    mid_above, mid_below = exchange(to_next, to_prev, count)
    next_sums = total(next_sums)
    solute, part = call_solute_step(concentration, sums, above, below, mid_above, mid_below)
    potential, to_next, to_prev = call_second_potential(part, next_sums)
    end_above, end_below = exchange(to_next, to_prev, count)
    eta = call_second_step(group_of, group_mobility, eta, solute, next_sums, mid_above, mid_below)
    solute = call_solute_end(solute, potential, end_above, end_below)
    return eta, solute


def solution(mesh):
    fine = Mesh(mesh.devices.reshape(2, 8, 2, 4, 4), SPACE + GRAIN)
    placed = (
        P(None, SPACE, None),
        P(GRAIN),
        P(),
        P(GRAIN, None, SPACE, None),
        P(None, SPACE, None),
    )
    return jax.shard_map(
        shards,
        mesh=fine,
        in_specs=placed,
        out_specs=(P(GRAIN, None, SPACE, None), P(None, SPACE, None)),
        check_vma=False,
    )
```

```python
import jax
import jax.numpy as jnp
from jax import lax
from jax.experimental import pallas as pl
from jax.experimental.pallas import tpu as pltpu
from jax.sharding import Mesh, PartitionSpec as P

GRAINS, PLANES, ROWS, COLS, LANES = 6, 3, 16, 2048, 128
BLOCKS = COLS // LANES
SPACE = ("yl", "z", "core")
GRAIN = ("x", "yh")

coef_quad = 1.0
coef_quart = 1.0
cross_gamma = 1.5
gradient_kappa = 0.5
solute_beta = 0.6
bulk_stiff = 1.0
solute_mean = 0.4
solute_kappa = 0.25
solute_mobility = 0.3
time_step = 0.1

F32 = jnp.float32
MIB = 1024 * 1024


def shape(*dims):
    return jax.ShapeDtypeStruct(dims, F32)


def hbm(*dims):
    return pltpu.HBM(dims, F32)


def from_hbm(*arrays):
    return [pltpu.with_memory_space_constraint(array, pltpu.HBM) for array in arrays]


def params(mib=16):
    return pltpu.CompilerParams(vmem_limit_bytes=mib * MIB)


def whole(*dims):
    return pl.BlockSpec(dims, lambda *_: (0,) * len(dims))


def smem():
    return pl.BlockSpec(memory_space=pltpu.SMEM)


def along_columns(value):
    return pltpu.roll(value, 1, 1) + pltpu.roll(value, COLS - 1, 1)


def beside(planes):
    return (planes[0] + planes[1], planes[0] + planes[2], planes[1] + planes[2])


def column_block(block):
    return slice(block * LANES, (block + 1) * LANES)


def first_sums(first_ref, noise_ref, ids_ref, solute_ref, sums_ref, next_ref, prev_ref):
    for plane in range(PLANES):
        ids = ids_ref[plane]
        two = four = None
        for grain in range(GRAINS):
            seed = jnp.where(ids == first_ref[0] + grain, 0.9, 0.0).astype(F32)
            eta = seed + noise_ref[grain, plane]
            row = grain * PLANES + plane
            prev_ref[row : row + 1, :] = eta[:1]
            next_ref[row : row + 1, :] = eta[ROWS - 1 :]
            square = eta * eta
            two = square if two is None else two + square
            four = square * square if four is None else four + square * square
        for block in range(sums_ref.shape[0]):
            sums_ref[block, plane] = two[:, column_block(block)]
            sums_ref[block, PLANES + plane] = four[:, column_block(block)]
        row = GRAINS * PLANES + 3 * plane
        prev_ref[row : row + 3, :] = solute_ref[plane, :3]
        next_ref[row : row + 3, :] = solute_ref[plane, ROWS - 3 :]


def call_first_sums(first, noise, ids, solute):
    width = 512
    edge = GRAINS * PLANES + 3 * PLANES
    return pl.pallas_call(
        first_sums,
        grid=(COLS // width,),
        in_specs=[
            smem(),
            pl.BlockSpec((GRAINS, PLANES, ROWS, width), lambda i: (0, 0, 0, i)),
            pl.BlockSpec((PLANES, ROWS, width), lambda i: (0, 0, i)),
            pl.BlockSpec((PLANES, ROWS, width), lambda i: (0, 0, i)),
        ],
        out_specs=[
            pl.BlockSpec((width // LANES, 2 * PLANES, ROWS, LANES), lambda i: (i, 0, 0, 0)),
            pl.BlockSpec((edge, width), lambda i: (0, i)),
            pl.BlockSpec((edge, width), lambda i: (0, i)),
        ],
        out_shape=[
            shape(BLOCKS, 2 * PLANES, ROWS, LANES),
            shape(edge, COLS),
            shape(edge, COLS),
        ],
        compiler_params=params(60),
        name="first_sums",
    )(first, *from_hbm(noise, ids, solute))


def factors(sums_ref, solute_ref, base_ref, slope_ref):
    for plane in range(PLANES):
        for block in range(BLOCKS):
            columns = column_block(block)
            cross = 2.0 * cross_gamma - 4.0 * solute_beta * solute_ref[plane, :, columns]
            base_ref[plane, :, columns] = (
                coef_quad - 6.0 * gradient_kappa - sums_ref[block, plane] * cross
            )
            slope_ref[plane, :, columns] = cross - coef_quart


def stepped(planes, above, below, rate, base_ref, slope_ref):
    rows = lax.broadcasted_iota(jnp.int32, (ROWS, COLS), 0)
    out = []
    for plane, across in zip(range(PLANES), beside(planes)):
        eta = planes[plane]
        up = jnp.where(rows == 0, above[plane], pltpu.roll(eta, 1, 0))
        down = jnp.where(rows == ROWS - 1, below[plane], pltpu.roll(eta, ROWS - 1, 0))
        around = up + down + along_columns(eta) + across
        bracket = base_ref[plane] + slope_ref[plane] * (eta * eta)
        out.append(eta + rate * (eta * bracket + gradient_kappa * around))
    return out


def halo_rows(ref, grain):
    return [ref[pl.ds(grain * PLANES + plane, 1), :] for plane in range(PLANES)]


def first_step(
    first_ref, group_ref, mobility_ref, noise_ref, ids_ref, solute_ref, sums_ref, bulk_ref, above_ref, below_ref,
    eta_ref, next_sums_ref, next_ref, prev_ref, base_ref, slope_ref,
):
    grain = pl.program_id(0)

    @pl.when(grain == 0)
    def _():
        factors(sums_ref, solute_ref, base_ref, slope_ref)
        for plane in range(PLANES):
            for block in range(BLOCKS):
                next_sums_ref[block, 2 * PLANES + plane] = bulk_ref[plane]

    rate = time_step * mobility_ref[group_ref[grain]]
    planes = [
        jnp.where(ids_ref[plane] == first_ref[0] + grain, 0.9, 0.0).astype(F32) + noise_ref[0, plane]
        for plane in range(PLANES)
    ]
    out = stepped(planes, halo_rows(above_ref, grain), halo_rows(below_ref, grain), rate, base_ref, slope_ref)
    for plane in range(PLANES):
        eta = out[plane]
        eta_ref[0, plane] = eta
        row = pl.ds(grain * PLANES + plane, 1)
        prev_ref[row, :] = eta[:1]
        next_ref[row, :] = eta[ROWS - 1 :]
    for plane in range(PLANES):
        square = out[plane] * out[plane]
        fourth = square * square

        @pl.when(grain == 0)
        def _():
            for block in range(BLOCKS):
                next_sums_ref[block, plane] = square[:, column_block(block)]
                next_sums_ref[block, PLANES + plane] = fourth[:, column_block(block)]

        @pl.when(grain != 0)
        def _():
            for block in range(BLOCKS):
                next_sums_ref[block, plane] += square[:, column_block(block)]
                next_sums_ref[block, PLANES + plane] += fourth[:, column_block(block)]


def call_first_step(first, groups, mobility, noise, ids, solute, sums, bulk, above, below):
    edge = GRAINS * PLANES
    grain_block = pl.BlockSpec((1, PLANES, ROWS, COLS), lambda i: (i, 0, 0, 0))
    parts = (BLOCKS, 3 * PLANES, ROWS, LANES)
    return pl.pallas_call(
        first_step,
        grid=(GRAINS,),
        in_specs=[
            smem(), smem(), smem(), grain_block,
            whole(*ids.shape), whole(*solute.shape), whole(*sums.shape), whole(*bulk.shape),
            whole(*above.shape), whole(*below.shape),
        ],
        out_specs=[grain_block, whole(*parts), whole(edge, COLS), whole(edge, COLS)],
        out_shape=[hbm(*noise.shape), shape(*parts), hbm(edge, COLS), hbm(edge, COLS)],
        scratch_shapes=[pltpu.VMEM(solute.shape, F32)] * 2,
        compiler_params=params(),
        name="first_step",
    )(first, groups, mobility, *from_hbm(noise, ids, solute), sums, *from_hbm(bulk, above, below))


def added(parts_ref, row):
    values = [parts_ref[part, row] for part in range(parts_ref.shape[0])]
    while len(values) > 1:
        values = [left + right for left, right in zip(values[::2], values[1::2])]
    return values[0]


def first_owner(parts_ref, copies_ref, bulk_ref):
    for plane in range(PLANES):
        two, four = added(parts_ref, plane), added(parts_ref, PLANES + plane)
        bulk_ref[plane] = solute_beta * (two * two - four)
        for copy in range(copies_ref.shape[0]):
            copies_ref[copy, plane] = two


def call_first_owner(parts):
    return pl.pallas_call(
        first_owner,
        out_shape=[hbm(BLOCKS, PLANES, ROWS, LANES), hbm(PLANES, ROWS, LANES)],
        compiler_params=params(),
        name="first_owner",
    )(parts)


def second_owner(parts_ref, eta_next_ref, eta_prev_ref, copies_ref, next_ref, prev_ref):
    for plane in range(PLANES):
        two, four = added(parts_ref, plane), added(parts_ref, PLANES + plane)
        bulk = solute_beta * (two * two - four)
        for copy in range(copies_ref.shape[0]):
            copies_ref[copy, plane] = two
            copies_ref[copy, PLANES + plane] = bulk
    edge = eta_next_ref.shape[0]
    next_ref[:edge] = eta_next_ref[...]
    prev_ref[:edge] = eta_prev_ref[...]
    for plane in range(PLANES):
        row = edge + 2 * plane
        for block in range(BLOCKS):
            columns = column_block(block)
            prev_ref[row : row + 2, columns] = parts_ref[block, 2 * PLANES + plane, :2]
            next_ref[row : row + 2, columns] = parts_ref[block, 2 * PLANES + plane, ROWS - 2 :]


def call_second_owner(parts, eta_next, eta_prev):
    edge = eta_next.shape[0] + 2 * PLANES
    return pl.pallas_call(
        second_owner,
        out_shape=[hbm(BLOCKS, 2 * PLANES, ROWS, LANES), hbm(edge, COLS), hbm(edge, COLS)],
        compiler_params=params(),
        name="second_owner",
    )(parts, *from_hbm(eta_next, eta_prev))


PAD = 8
DEEP = ROWS + 2 * PAD


def laplace(planes):
    height = planes[0].shape[0]
    return [
        pltpu.roll(value, 1, 0) + pltpu.roll(value, height - 1, 0) + along_columns(value) + across - 6.0 * value
        for value, across in zip(planes, beside(planes))
    ]


def solute_step(
    solute_ref, parts_ref, above_ref, below_ref, mid_above_ref, mid_below_ref,
    out_ref, part_ref, deep_ref, bulk_ref,
):
    for plane in range(PLANES):
        for ref in (deep_ref, bulk_ref):
            ref[plane, :PAD] = jnp.zeros((PAD, COLS), F32)
            ref[plane, PAD + ROWS :] = jnp.zeros((PAD, COLS), F32)
        row = GRAINS * PLANES + 3 * plane
        deep_ref[plane, PAD - 3 : PAD] = above_ref[row : row + 3, :]
        deep_ref[plane, PAD : PAD + ROWS] = solute_ref[plane]
        deep_ref[plane, PAD + ROWS : PAD + ROWS + 3] = below_ref[row : row + 3, :]
        row = GRAINS * PLANES + 2 * plane
        bulk_ref[plane, PAD - 2 : PAD] = mid_above_ref[row : row + 2, :]
        bulk_ref[plane, PAD + ROWS : PAD + ROWS + 2] = mid_below_ref[row : row + 2, :]
        for block in range(BLOCKS):
            bulk_ref[plane, PAD : PAD + ROWS, column_block(block)] = parts_ref[block, 2 * PLANES + plane]
    solute = [deep_ref[plane] for plane in range(PLANES)]
    potential = [
        2.0 * bulk_stiff * (solute[plane] - solute_mean) - bulk_ref[plane] - solute_kappa * lap
        for plane, lap in enumerate(laplace(solute))
    ]
    moved = [
        solute[plane] + time_step * solute_mobility * lap for plane, lap in enumerate(laplace(potential))
    ]
    for plane, lap in enumerate(laplace(moved)):
        part = 2.0 * bulk_stiff * (moved[plane] - solute_mean) - solute_kappa * lap
        out_ref[plane] = moved[plane][PAD : PAD + ROWS]
        part_ref[plane] = part[PAD : PAD + ROWS]


def call_solute_step(solute, parts, above, below, mid_above, mid_below):
    return pl.pallas_call(
        solute_step,
        out_shape=[hbm(*solute.shape)] * 2,
        scratch_shapes=[pltpu.VMEM((PLANES, DEEP, COLS), F32)] * 2,
        compiler_params=params(),
        name="solute_step",
    )(*from_hbm(solute), parts, *from_hbm(above, below, mid_above, mid_below))


def second_potential(part_ref, sums_ref, out_ref, next_ref, prev_ref):
    for plane in range(PLANES):
        for block in range(BLOCKS):
            columns = column_block(block)
            potential = part_ref[plane, :, columns] - sums_ref[block, PLANES + plane]
            out_ref[plane, :, columns] = potential
            prev_ref[plane : plane + 1, columns] = potential[:1]
            next_ref[plane : plane + 1, columns] = potential[ROWS - 1 :]


def call_second_potential(part, sums):
    return pl.pallas_call(
        second_potential,
        out_shape=[shape(*part.shape), shape(PLANES, COLS), shape(PLANES, COLS)],
        compiler_params=params(),
        name="second_potential",
    )(*from_hbm(part), sums)


def second_step(
    group_ref, mobility_ref, old_ref, solute_ref, sums_ref, above_ref, below_ref, eta_ref, base_ref, slope_ref
):
    grain = pl.program_id(0)

    @pl.when(grain == 0)
    def _():
        factors(sums_ref, solute_ref, base_ref, slope_ref)

    rate = time_step * mobility_ref[group_ref[grain]]
    planes = [old_ref[0, plane] for plane in range(PLANES)]
    out = stepped(planes, halo_rows(above_ref, grain), halo_rows(below_ref, grain), rate, base_ref, slope_ref)
    for plane in range(PLANES):
        eta_ref[0, plane] = out[plane]


def call_second_step(groups, mobility, eta, solute, sums, above, below):
    grain_block = pl.BlockSpec((1, PLANES, ROWS, COLS), lambda i: (i, 0, 0, 0))
    return pl.pallas_call(
        second_step,
        grid=(GRAINS,),
        in_specs=[
            smem(), smem(), grain_block, whole(*solute.shape), whole(*sums.shape),
            whole(*above.shape), whole(*below.shape),
        ],
        out_specs=grain_block,
        out_shape=shape(*eta.shape),
        scratch_shapes=[pltpu.VMEM(solute.shape, F32)] * 2,
        compiler_params=params(),
        cost_estimate=pl.CostEstimate(flops=20_000_000, bytes_accessed=10_000_000, transcendentals=0),
        name="second_step",
    )(groups, mobility, *from_hbm(eta, solute), sums, *from_hbm(above, below))


def solute_end(solute_ref, potential_ref, above_ref, below_ref, out_ref):
    rows = lax.broadcasted_iota(jnp.int32, (ROWS, COLS), 0)
    planes = [potential_ref[plane] for plane in range(PLANES)]
    for plane, across in enumerate(beside(planes)):
        value = planes[plane]
        up = jnp.where(rows == 0, above_ref[plane : plane + 1, :], pltpu.roll(value, 1, 0))
        down = jnp.where(rows == ROWS - 1, below_ref[plane : plane + 1, :], pltpu.roll(value, ROWS - 1, 0))
        lap = up + down + along_columns(value) + across - 6.0 * value
        out_ref[plane] = solute_ref[plane] + time_step * solute_mobility * lap


def call_solute_end(solute, potential, above, below):
    return pl.pallas_call(
        solute_end,
        out_shape=shape(*solute.shape),
        compiler_params=params(),
        name="solute_end",
    )(*from_hbm(solute), potential, above, below)


def exchange(to_next, to_prev, count):
    above = lax.ppermute(to_next, SPACE, [(i, (i + 1) % count) for i in range(count)])
    below = lax.ppermute(to_prev, SPACE, [((i + 1) % count, i) for i in range(count)])
    return above, below


def dealt(blocks):
    return lax.all_to_all(blocks, GRAIN, 0, 0, tiled=True)


def shards(grain_ids, group_of, group_mobility, seed_noise, concentration):
    count = lax.axis_size("yl") * lax.axis_size("z") * lax.axis_size("core")
    first = (lax.axis_index(GRAIN) * GRAINS).astype(jnp.int32).reshape(1)
    sums, to_next, to_prev = call_first_sums(first, seed_noise, grain_ids, concentration)
    above, below = exchange(to_next, to_prev, count)
    copies, bulk = call_first_owner(dealt(sums))
    eta, parts, eta_next, eta_prev = call_first_step(
        first, group_of, group_mobility, seed_noise, grain_ids, concentration, dealt(copies), bulk, above, below
    )
    parts = dealt(parts)
    copies, to_next, to_prev = call_second_owner(parts, eta_next, eta_prev)
    mid_above, mid_below = exchange(to_next, to_prev, count)
    sums = dealt(copies)
    solute, part = call_solute_step(concentration, parts, above, below, mid_above, mid_below)
    potential, to_next, to_prev = call_second_potential(part, sums)
    end_above, end_below = exchange(to_next, to_prev, count)
    eta = call_second_step(group_of, group_mobility, eta, solute, sums, mid_above, mid_below)
    solute = call_solute_end(solute, potential, end_above, end_below)
    return eta, solute


def solution(mesh):
    fine = Mesh(mesh.devices.reshape(2, 8, 2, 4, 4), SPACE + GRAIN)
    placed = (
        P(None, SPACE, None),
        P(GRAIN),
        P(),
        P(GRAIN, None, SPACE, None),
        P(None, SPACE, None),
    )
    return jax.shard_map(
        shards,
        mesh=fine,
        in_specs=placed,
        out_specs=(P(GRAIN, None, SPACE, None), P(None, SPACE, None)),
        check_vma=False,
    )
```

```python
import jax
import jax.numpy as jnp
from jax import lax
from jax.experimental import pallas as pl
from jax.experimental.pallas import tpu as pltpu
from jax.sharding import Mesh, PartitionSpec as P

GRAINS, PLANES, ROWS, COLS, LANES = 6, 3, 16, 2048, 128
BLOCKS = COLS // LANES
SPACE = ("yl", "z", "core")
GRAIN = ("x", "yh")

coef_quad = 1.0
coef_quart = 1.0
cross_gamma = 1.5
gradient_kappa = 0.5
solute_beta = 0.6
bulk_stiff = 1.0
solute_mean = 0.4
solute_kappa = 0.25
solute_mobility = 0.3
time_step = 0.1

F32 = jnp.float32
MIB = 1024 * 1024


def shape(*dims):
    return jax.ShapeDtypeStruct(dims, F32)


def hbm(*dims):
    return pltpu.HBM(dims, F32)


def params(mib=16):
    return pltpu.CompilerParams(vmem_limit_bytes=mib * MIB)


def whole(*dims):
    return pl.BlockSpec(dims, lambda *_: (0,) * len(dims))


def smem():
    return pl.BlockSpec(memory_space=pltpu.SMEM)


def along_columns(value):
    return pltpu.roll(value, 1, 1) + pltpu.roll(value, COLS - 1, 1)


def beside(planes):
    return (planes[0] + planes[1], planes[0] + planes[2], planes[1] + planes[2])


def column_block(block):
    return slice(block * LANES, (block + 1) * LANES)


def first_sums(first_ref, noise_ref, ids_ref, solute_ref, sums_ref, next_ref, prev_ref):
    for plane in range(PLANES):
        ids = ids_ref[plane]
        two = four = None
        for grain in range(GRAINS):
            seed = jnp.where(ids == first_ref[0] + grain, 0.9, 0.0).astype(F32)
            eta = seed + noise_ref[grain, plane]
            row = grain * PLANES + plane
            prev_ref[row : row + 1, :] = eta[:1]
            next_ref[row : row + 1, :] = eta[ROWS - 1 :]
            square = eta * eta
            two = square if two is None else two + square
            four = square * square if four is None else four + square * square
        for block in range(sums_ref.shape[0]):
            sums_ref[block, plane] = two[:, column_block(block)]
            sums_ref[block, PLANES + plane] = four[:, column_block(block)]
        row = GRAINS * PLANES + 3 * plane
        prev_ref[row : row + 3, :] = solute_ref[plane, :3]
        next_ref[row : row + 3, :] = solute_ref[plane, ROWS - 3 :]


def call_first_sums(first, noise, ids, solute):
    width = 512
    edge = GRAINS * PLANES + 3 * PLANES
    return pl.pallas_call(
        first_sums,
        grid=(COLS // width,),
        in_specs=[
            smem(),
            pl.BlockSpec((GRAINS, PLANES, ROWS, width), lambda i: (0, 0, 0, i)),
            pl.BlockSpec((PLANES, ROWS, width), lambda i: (0, 0, i)),
            pl.BlockSpec((PLANES, ROWS, width), lambda i: (0, 0, i)),
        ],
        out_specs=[
            pl.BlockSpec((width // LANES, 2 * PLANES, ROWS, LANES), lambda i: (i, 0, 0, 0)),
            pl.BlockSpec((edge, width), lambda i: (0, i)),
            pl.BlockSpec((edge, width), lambda i: (0, i)),
        ],
        out_shape=[
            shape(BLOCKS, 2 * PLANES, ROWS, LANES),
            shape(edge, COLS),
            shape(edge, COLS),
        ],
        compiler_params=params(60),
        name="first_sums",
    )(first, noise, ids, solute)


def factors(sums_ref, solute_ref, base_ref, slope_ref):
    for plane in range(PLANES):
        for block in range(BLOCKS):
            columns = column_block(block)
            cross = 2.0 * cross_gamma - 4.0 * solute_beta * solute_ref[plane, :, columns]
            base_ref[plane, :, columns] = (
                coef_quad - 6.0 * gradient_kappa - sums_ref[block, plane] * cross
            )
            slope_ref[plane, :, columns] = cross - coef_quart


def stepped(planes, above, below, rate, base_ref, slope_ref):
    rows = lax.broadcasted_iota(jnp.int32, (ROWS, COLS), 0)
    out = []
    for plane, across in zip(range(PLANES), beside(planes)):
        eta = planes[plane]
        up = jnp.where(rows == 0, above[plane], pltpu.roll(eta, 1, 0))
        down = jnp.where(rows == ROWS - 1, below[plane], pltpu.roll(eta, ROWS - 1, 0))
        around = up + down + along_columns(eta) + across
        bracket = base_ref[plane] + slope_ref[plane] * (eta * eta)
        out.append(eta + rate * (eta * bracket + gradient_kappa * around))
    return out


def halo_rows(ref, grain):
    return [ref[pl.ds(grain * PLANES + plane, 1), :] for plane in range(PLANES)]


def first_step(
    first_ref, group_ref, mobility_ref, noise_ref, ids_ref, solute_ref, sums_ref, above_ref, below_ref,
    eta_ref, next_sums_ref, next_ref, prev_ref, bulk_ref, rows_above_ref, rows_below_ref, base_ref, slope_ref,
):
    grain = pl.program_id(0)

    @pl.when(grain == 0)
    def _():
        factors(sums_ref, solute_ref, base_ref, slope_ref)
        for plane in range(PLANES):
            row = GRAINS * PLANES + 2 * plane
            for block in range(BLOCKS):
                columns = column_block(block)
                bulk = sums_ref[block, PLANES + plane]
                bulk_ref[plane, :, columns] = bulk
                prev_ref[row : row + 2, columns] = bulk[:2]
                next_ref[row : row + 2, columns] = bulk[ROWS - 2 :]
        rows_above_ref[...] = above_ref[GRAINS * PLANES :]
        rows_below_ref[...] = below_ref[GRAINS * PLANES :]

    rate = time_step * mobility_ref[group_ref[grain]]
    planes = [
        jnp.where(ids_ref[plane] == first_ref[0] + grain, 0.9, 0.0).astype(F32) + noise_ref[0, plane]
        for plane in range(PLANES)
    ]
    out = stepped(planes, halo_rows(above_ref, grain), halo_rows(below_ref, grain), rate, base_ref, slope_ref)
    for plane in range(PLANES):
        eta = out[plane]
        eta_ref[0, plane] = eta
        row = pl.ds(grain * PLANES + plane, 1)
        prev_ref[row, :] = eta[:1]
        next_ref[row, :] = eta[ROWS - 1 :]
    for plane in range(PLANES):
        square = out[plane] * out[plane]
        fourth = square * square

        @pl.when(grain == 0)
        def _():
            for block in range(BLOCKS):
                next_sums_ref[block, plane] = square[:, column_block(block)]
                next_sums_ref[block, PLANES + plane] = fourth[:, column_block(block)]

        @pl.when(grain != 0)
        def _():
            for block in range(BLOCKS):
                next_sums_ref[block, plane] += square[:, column_block(block)]
                next_sums_ref[block, PLANES + plane] += fourth[:, column_block(block)]


def call_first_step(first, groups, mobility, noise, ids, solute, sums, above, below):
    edge = GRAINS * PLANES + 2 * PLANES
    grain_block = pl.BlockSpec((1, PLANES, ROWS, COLS), lambda i: (i, 0, 0, 0))
    return pl.pallas_call(
        first_step,
        grid=(GRAINS,),
        in_specs=[
            smem(), smem(), smem(), grain_block,
            whole(*ids.shape), whole(*solute.shape), whole(*sums.shape),
            whole(*above.shape), whole(*below.shape),
        ],
        out_specs=[grain_block, whole(*sums.shape)]
        + [whole(edge, COLS)] * 2
        + [whole(*solute.shape)]
        + [whole(3 * PLANES, COLS)] * 2,
        out_shape=[hbm(*noise.shape), shape(*sums.shape)]
        + [shape(edge, COLS)] * 2
        + [hbm(*solute.shape)]
        + [hbm(3 * PLANES, COLS)] * 2,
        scratch_shapes=[pltpu.VMEM(solute.shape, F32)] * 2,
        compiler_params=params(),
        name="first_step",
    )(first, groups, mobility, noise, ids, solute, sums, above, below)


PAD = 8
DEEP = ROWS + 2 * PAD


def laplace(planes):
    height = planes[0].shape[0]
    return [
        pltpu.roll(value, 1, 0) + pltpu.roll(value, height - 1, 0) + along_columns(value) + across - 6.0 * value
        for value, across in zip(planes, beside(planes))
    ]


def solute_step(
    solute_ref, middle_ref, above_ref, below_ref, mid_above_ref, mid_below_ref,
    out_ref, part_ref, deep_ref, bulk_ref,
):
    for plane in range(PLANES):
        for ref in (deep_ref, bulk_ref):
            ref[plane, :PAD] = jnp.zeros((PAD, COLS), F32)
            ref[plane, PAD + ROWS :] = jnp.zeros((PAD, COLS), F32)
        row = 3 * plane
        deep_ref[plane, PAD - 3 : PAD] = above_ref[row : row + 3, :]
        deep_ref[plane, PAD : PAD + ROWS] = solute_ref[plane]
        deep_ref[plane, PAD + ROWS : PAD + ROWS + 3] = below_ref[row : row + 3, :]
        row = GRAINS * PLANES + 2 * plane
        bulk_ref[plane, PAD - 2 : PAD] = mid_above_ref[row : row + 2, :]
        bulk_ref[plane, PAD + ROWS : PAD + ROWS + 2] = mid_below_ref[row : row + 2, :]
        bulk_ref[plane, PAD : PAD + ROWS] = middle_ref[plane]
    solute = [deep_ref[plane] for plane in range(PLANES)]
    potential = [
        2.0 * bulk_stiff * (solute[plane] - solute_mean) - bulk_ref[plane] - solute_kappa * lap
        for plane, lap in enumerate(laplace(solute))
    ]
    moved = [
        solute[plane] + time_step * solute_mobility * lap for plane, lap in enumerate(laplace(potential))
    ]
    for plane, lap in enumerate(laplace(moved)):
        part = 2.0 * bulk_stiff * (moved[plane] - solute_mean) - solute_kappa * lap
        out_ref[plane] = moved[plane][PAD : PAD + ROWS]
        part_ref[plane] = part[PAD : PAD + ROWS]


def call_solute_step(solute, bulk, above, below, mid_above, mid_below):
    return pl.pallas_call(
        solute_step,
        out_shape=[shape(*solute.shape)] * 2,
        scratch_shapes=[pltpu.VMEM((PLANES, DEEP, COLS), F32)] * 2,
        compiler_params=params(),
        name="solute_step",
    )(solute, bulk, above, below, mid_above, mid_below)


def second_potential(part_ref, sums_ref, out_ref, next_ref, prev_ref):
    for plane in range(PLANES):
        for block in range(BLOCKS):
            columns = column_block(block)
            potential = part_ref[plane, :, columns] - sums_ref[block, PLANES + plane]
            out_ref[plane, :, columns] = potential
            prev_ref[plane : plane + 1, columns] = potential[:1]
            next_ref[plane : plane + 1, columns] = potential[ROWS - 1 :]


def call_second_potential(part, sums):
    return pl.pallas_call(
        second_potential,
        out_shape=[shape(*part.shape), shape(PLANES, COLS), shape(PLANES, COLS)],
        compiler_params=params(),
        name="second_potential",
    )(part, sums)


def second_step(
    group_ref, mobility_ref, old_ref, solute_ref, sums_ref, above_ref, below_ref, eta_ref, base_ref, slope_ref
):
    grain = pl.program_id(0)

    @pl.when(grain == 0)
    def _():
        factors(sums_ref, solute_ref, base_ref, slope_ref)

    rate = time_step * mobility_ref[group_ref[grain]]
    planes = [old_ref[0, plane] for plane in range(PLANES)]
    out = stepped(planes, halo_rows(above_ref, grain), halo_rows(below_ref, grain), rate, base_ref, slope_ref)
    for plane in range(PLANES):
        eta_ref[0, plane] = out[plane]


def call_second_step(groups, mobility, eta, solute, sums, above, below):
    grain_block = pl.BlockSpec((1, PLANES, ROWS, COLS), lambda i: (i, 0, 0, 0))
    return pl.pallas_call(
        second_step,
        grid=(GRAINS,),
        in_specs=[
            smem(), smem(), grain_block, whole(*solute.shape), whole(*sums.shape),
            whole(*above.shape), whole(*below.shape),
        ],
        out_specs=grain_block,
        out_shape=shape(*eta.shape),
        scratch_shapes=[pltpu.VMEM(solute.shape, F32)] * 2,
        compiler_params=params(),
        cost_estimate=pl.CostEstimate(flops=20_000_000, bytes_accessed=10_000_000, transcendentals=0),
        name="second_step",
    )(groups, mobility, eta, solute, sums, above, below)


def solute_end(solute_ref, potential_ref, above_ref, below_ref, out_ref):
    rows = lax.broadcasted_iota(jnp.int32, (ROWS, COLS), 0)
    planes = [potential_ref[plane] for plane in range(PLANES)]
    for plane, across in enumerate(beside(planes)):
        value = planes[plane]
        up = jnp.where(rows == 0, above_ref[plane : plane + 1, :], pltpu.roll(value, 1, 0))
        down = jnp.where(rows == ROWS - 1, below_ref[plane : plane + 1, :], pltpu.roll(value, ROWS - 1, 0))
        lap = up + down + along_columns(value) + across - 6.0 * value
        out_ref[plane] = solute_ref[plane] + time_step * solute_mobility * lap


def call_solute_end(solute, potential, above, below):
    return pl.pallas_call(
        solute_end,
        out_shape=shape(*solute.shape),
        compiler_params=params(),
        name="solute_end",
    )(solute, potential, above, below)


def exchange(to_next, to_prev, count):
    above = lax.ppermute(to_next, SPACE, [(i, (i + 1) % count) for i in range(count)])
    below = lax.ppermute(to_prev, SPACE, [((i + 1) % count, i) for i in range(count)])
    return above, below


def added(parts_ref, index):
    values = [parts_ref[(part,) + index] for part in range(parts_ref.shape[0])]
    while len(values) > 1:
        values = [left + right for left, right in zip(values[::2], values[1::2])]
    return values[0]


def add_parts(parts_ref, out_ref):
    for block in range(out_ref.shape[0]):
        for row in range(out_ref.shape[1]):
            out_ref[block, row] = added(parts_ref, (block, row))


def call_add_parts(parts):
    return pl.pallas_call(
        add_parts, out_shape=shape(*parts.shape[1:]), compiler_params=params(), name="add_parts"
    )(parts)


def owner(parts_ref, copies_ref):
    for plane in range(PLANES):
        two, four = added(parts_ref, (plane,)), added(parts_ref, (PLANES + plane,))
        bulk = solute_beta * (two * two - four)
        for copy in range(copies_ref.shape[0]):
            copies_ref[copy, plane] = two
            copies_ref[copy, PLANES + plane] = bulk


def call_owner(parts):
    return pl.pallas_call(
        owner, out_shape=shape(*parts.shape), compiler_params=params(), name="owner"
    )(parts)


def copies(value_ref, out_ref):
    for copy in range(out_ref.shape[0]):
        out_ref[copy] = value_ref[...]


def call_copies(value, count):
    return pl.pallas_call(
        copies, out_shape=shape(count, *value.shape), compiler_params=params(), name="copies"
    )(value)


def dealt(blocks, axis):
    return lax.all_to_all(blocks, axis, 0, 0, tiled=True)


def total(sums, to_next, to_prev):
    count = lax.axis_size("yl") * lax.axis_size("z") * lax.axis_size("core")
    along = lax.axis_size("x")
    parts = dealt(sums.reshape((along, BLOCKS // along) + sums.shape[1:]), "x")
    parts, above, below = lax.optimization_barrier((parts, *exchange(to_next, to_prev, count)))
    parts = dealt(call_add_parts(parts), "yh")
    parts = dealt(call_owner(parts), "yh")
    return dealt(call_copies(parts, along), "x").reshape(sums.shape), above, below


def shards(grain_ids, group_of, group_mobility, seed_noise, concentration):
    count = lax.axis_size("yl") * lax.axis_size("z") * lax.axis_size("core")
    first = (lax.axis_index(GRAIN) * GRAINS).astype(jnp.int32).reshape(1)
    sums, to_next, to_prev = call_first_sums(first, seed_noise, grain_ids, concentration)
    sums, above, below = total(sums, to_next, to_prev)
    eta, sums, to_next, to_prev, bulk, rows_above, rows_below = call_first_step(
        first, group_of, group_mobility, seed_noise, grain_ids, concentration, sums, above, below
    )
    sums, mid_above, mid_below = total(sums, to_next, to_prev)
    solute, part = call_solute_step(concentration, bulk, rows_above, rows_below, mid_above, mid_below)
    potential, to_next, to_prev = call_second_potential(part, sums)
    end_above, end_below = exchange(to_next, to_prev, count)
    eta = call_second_step(group_of, group_mobility, eta, solute, sums, mid_above, mid_below)
    solute = call_solute_end(solute, potential, end_above, end_below)
    return eta, solute


def solution(mesh):
    fine = Mesh(mesh.devices.reshape(2, 8, 2, 4, 4), SPACE + GRAIN)
    placed = (
        P(None, SPACE, None),
        P(GRAIN),
        P(),
        P(GRAIN, None, SPACE, None),
        P(None, SPACE, None),
    )
    return jax.shard_map(
        shards,
        mesh=fine,
        in_specs=placed,
        out_specs=(P(GRAIN, None, SPACE, None), P(None, SPACE, None)),
        check_vma=False,
    )
```

```python
import jax
import jax.numpy as jnp
from jax import lax
from jax.experimental import pallas as pl
from jax.experimental.pallas import tpu as pltpu
from jax.sharding import Mesh, PartitionSpec as P

GRAINS, PLANES, ROWS, COLS, LANES = 6, 3, 16, 2048, 128
BLOCKS = COLS // LANES
SPACE = ("yl", "z", "core")
GRAIN = ("x", "yh")

coef_quad = 1.0
coef_quart = 1.0
cross_gamma = 1.5
gradient_kappa = 0.5
solute_beta = 0.6
bulk_stiff = 1.0
solute_mean = 0.4
solute_kappa = 0.25
solute_mobility = 0.3
time_step = 0.1

F32 = jnp.float32
MIB = 1024 * 1024


def shape(*dims):
    return jax.ShapeDtypeStruct(dims, F32)


def hbm(*dims):
    return pltpu.HBM(dims, F32)


def from_hbm(*arrays):
    return [pltpu.with_memory_space_constraint(array, pltpu.HBM) for array in arrays]


def params(mib=16):
    return pltpu.CompilerParams(vmem_limit_bytes=mib * MIB)


def whole(*dims):
    return pl.BlockSpec(dims, lambda *_: (0,) * len(dims))


def smem():
    return pl.BlockSpec(memory_space=pltpu.SMEM)


def along_columns(value):
    return pltpu.roll(value, 1, 1) + pltpu.roll(value, COLS - 1, 1)


def beside(planes):
    return (planes[0] + planes[1], planes[0] + planes[2], planes[1] + planes[2])


def column_block(block):
    return slice(block * LANES, (block + 1) * LANES)


def first_sums(first_ref, noise_ref, ids_ref, solute_ref, sums_ref, next_ref, prev_ref):
    for plane in range(PLANES):
        ids = ids_ref[plane]
        two = four = None
        for grain in range(GRAINS):
            seed = jnp.where(ids == first_ref[0] + grain, 0.9, 0.0).astype(F32)
            eta = seed + noise_ref[grain, plane]
            row = grain * PLANES + plane
            prev_ref[row : row + 1, :] = eta[:1]
            next_ref[row : row + 1, :] = eta[ROWS - 1 :]
            square = eta * eta
            two = square if two is None else two + square
            four = square * square if four is None else four + square * square
        for block in range(sums_ref.shape[0]):
            sums_ref[block, plane] = two[:, column_block(block)]
            sums_ref[block, PLANES + plane] = four[:, column_block(block)]
        row = GRAINS * PLANES + 3 * plane
        prev_ref[row : row + 3, :] = solute_ref[plane, :3]
        next_ref[row : row + 3, :] = solute_ref[plane, ROWS - 3 :]


def call_first_sums(first, noise, ids, solute):
    width = 512
    edge = GRAINS * PLANES + 3 * PLANES
    return pl.pallas_call(
        first_sums,
        grid=(COLS // width,),
        in_specs=[
            smem(),
            pl.BlockSpec((GRAINS, PLANES, ROWS, width), lambda i: (0, 0, 0, i)),
            pl.BlockSpec((PLANES, ROWS, width), lambda i: (0, 0, i)),
            pl.BlockSpec((PLANES, ROWS, width), lambda i: (0, 0, i)),
        ],
        out_specs=[
            pl.BlockSpec((width // LANES, 2 * PLANES, ROWS, LANES), lambda i: (i, 0, 0, 0)),
            pl.BlockSpec((edge, width), lambda i: (0, i)),
            pl.BlockSpec((edge, width), lambda i: (0, i)),
        ],
        out_shape=[
            shape(BLOCKS, 2 * PLANES, ROWS, LANES),
            shape(edge, COLS),
            shape(edge, COLS),
        ],
        compiler_params=params(60),
        name="first_sums",
    )(first, noise, ids, solute)


def factors(sums_ref, solute_ref, base_ref, slope_ref):
    for plane in range(PLANES):
        for block in range(BLOCKS):
            columns = column_block(block)
            cross = 2.0 * cross_gamma - 4.0 * solute_beta * solute_ref[plane, :, columns]
            base_ref[plane, :, columns] = (
                coef_quad - 6.0 * gradient_kappa - sums_ref[block, plane] * cross
            )
            slope_ref[plane, :, columns] = cross - coef_quart


def stepped(planes, above, below, rate, base_ref, slope_ref):
    rows = lax.broadcasted_iota(jnp.int32, (ROWS, COLS), 0)
    out = []
    for plane, across in zip(range(PLANES), beside(planes)):
        eta = planes[plane]
        up = jnp.where(rows == 0, above[plane], pltpu.roll(eta, 1, 0))
        down = jnp.where(rows == ROWS - 1, below[plane], pltpu.roll(eta, ROWS - 1, 0))
        around = up + down + along_columns(eta) + across
        bracket = base_ref[plane] + slope_ref[plane] * (eta * eta)
        out.append(eta + rate * (eta * bracket + gradient_kappa * around))
    return out


def halo_rows(ref, grain):
    return [ref[pl.ds(grain * PLANES + plane, 1), :] for plane in range(PLANES)]


def first_step(
    first_ref, group_ref, mobility_ref, noise_ref, ids_ref, solute_ref, sums_ref, above_ref, below_ref,
    eta_ref, next_sums_ref, next_ref, prev_ref, bulk_ref, base_ref, slope_ref,
):
    grain = pl.program_id(0)

    @pl.when(grain == 0)
    def _():
        factors(sums_ref, solute_ref, base_ref, slope_ref)
        for plane in range(PLANES):
            row = GRAINS * PLANES + 2 * plane
            for block in range(BLOCKS):
                columns = column_block(block)
                bulk = sums_ref[block, PLANES + plane]
                bulk_ref[plane, :, columns] = bulk
                prev_ref[row : row + 2, columns] = bulk[:2]
                next_ref[row : row + 2, columns] = bulk[ROWS - 2 :]

    rate = time_step * mobility_ref[group_ref[grain]]
    planes = [
        jnp.where(ids_ref[plane] == first_ref[0] + grain, 0.9, 0.0).astype(F32) + noise_ref[0, plane]
        for plane in range(PLANES)
    ]
    out = stepped(planes, halo_rows(above_ref, grain), halo_rows(below_ref, grain), rate, base_ref, slope_ref)
    for plane in range(PLANES):
        eta = out[plane]
        eta_ref[0, plane] = eta
        row = pl.ds(grain * PLANES + plane, 1)
        prev_ref[row, :] = eta[:1]
        next_ref[row, :] = eta[ROWS - 1 :]
    for plane in range(PLANES):
        square = out[plane] * out[plane]
        fourth = square * square

        @pl.when(grain == 0)
        def _():
            for block in range(BLOCKS):
                next_sums_ref[block, plane] = square[:, column_block(block)]
                next_sums_ref[block, PLANES + plane] = fourth[:, column_block(block)]

        @pl.when(grain != 0)
        def _():
            for block in range(BLOCKS):
                next_sums_ref[block, plane] += square[:, column_block(block)]
                next_sums_ref[block, PLANES + plane] += fourth[:, column_block(block)]


def call_first_step(first, groups, mobility, noise, ids, solute, sums, above, below):
    edge = GRAINS * PLANES + 2 * PLANES
    grain_block = pl.BlockSpec((1, PLANES, ROWS, COLS), lambda i: (i, 0, 0, 0))
    return pl.pallas_call(
        first_step,
        grid=(GRAINS,),
        in_specs=[
            smem(), smem(), smem(), grain_block,
            whole(*ids.shape), whole(*solute.shape), whole(*sums.shape),
            whole(*above.shape), whole(*below.shape),
        ],
        out_specs=[grain_block, whole(*sums.shape)]
        + [whole(edge, COLS)] * 2
        + [whole(*solute.shape)],
        out_shape=[hbm(*noise.shape), shape(*sums.shape)]
        + [shape(edge, COLS)] * 2
        + [hbm(*solute.shape)],
        scratch_shapes=[pltpu.VMEM(solute.shape, F32)] * 2,
        compiler_params=params(),
        name="first_step",
    )(first, groups, mobility, *from_hbm(noise, ids, solute), sums, *from_hbm(above, below))


PAD = 8
DEEP = ROWS + 2 * PAD


def laplace(planes):
    height = planes[0].shape[0]
    return [
        pltpu.roll(value, 1, 0) + pltpu.roll(value, height - 1, 0) + along_columns(value) + across - 6.0 * value
        for value, across in zip(planes, beside(planes))
    ]


def solute_step(
    solute_ref, middle_ref, above_ref, below_ref, mid_above_ref, mid_below_ref,
    out_ref, part_ref, ends_ref, deep_ref, bulk_ref,
):
    for plane in range(PLANES):
        for ref in (deep_ref, bulk_ref):
            ref[plane, :PAD] = jnp.zeros((PAD, COLS), F32)
            ref[plane, PAD + ROWS :] = jnp.zeros((PAD, COLS), F32)
        row = GRAINS * PLANES + 3 * plane
        deep_ref[plane, PAD - 3 : PAD] = above_ref[row : row + 3, :]
        deep_ref[plane, PAD : PAD + ROWS] = solute_ref[plane]
        deep_ref[plane, PAD + ROWS : PAD + ROWS + 3] = below_ref[row : row + 3, :]
        row = GRAINS * PLANES + 2 * plane
        bulk_ref[plane, PAD - 2 : PAD] = mid_above_ref[row : row + 2, :]
        bulk_ref[plane, PAD + ROWS : PAD + ROWS + 2] = mid_below_ref[row : row + 2, :]
        bulk_ref[plane, PAD : PAD + ROWS] = middle_ref[plane]
    solute = [deep_ref[plane] for plane in range(PLANES)]
    potential = [
        2.0 * bulk_stiff * (solute[plane] - solute_mean) - bulk_ref[plane] - solute_kappa * lap
        for plane, lap in enumerate(laplace(solute))
    ]
    moved = [
        solute[plane] + time_step * solute_mobility * lap for plane, lap in enumerate(laplace(potential))
    ]
    for plane, lap in enumerate(laplace(moved)):
        part = 2.0 * bulk_stiff * (moved[plane] - solute_mean) - solute_kappa * lap
        out_ref[plane] = moved[plane][PAD : PAD + ROWS]
        part_ref[plane] = part[PAD : PAD + ROWS]
        ends_ref[plane : plane + 1, :] = part[PAD : PAD + 1]
        ends_ref[PLANES + plane : PLANES + plane + 1, :] = part[PAD + ROWS - 1 : PAD + ROWS]


def call_solute_step(solute, bulk, above, below, mid_above, mid_below):
    return pl.pallas_call(
        solute_step,
        out_shape=[hbm(*solute.shape)] * 2 + [hbm(2 * PLANES, COLS)],
        scratch_shapes=[pltpu.VMEM((PLANES, DEEP, COLS), F32)] * 2,
        compiler_params=params(),
        name="solute_step",
    )(*from_hbm(solute, bulk, above, below, mid_above, mid_below))


def end_rows(core_ref, ends_ref, sums_ref, inner_ref, outer_ref):
    for plane in range(PLANES):
        row = slice(plane, plane + 1)
        for block in range(BLOCKS):
            columns = column_block(block)
            bulk = sums_ref[block, PLANES + plane]
            top = ends_ref[plane : plane + 1, columns] - bulk[:1]
            bottom = ends_ref[PLANES + plane : PLANES + plane + 1, columns] - bulk[ROWS - 1 :]
            inner_ref[row, columns] = jnp.where(core_ref[0] == 0, bottom, top)
            outer_ref[row, columns] = jnp.where(core_ref[0] == 0, top, bottom)


def call_end_rows(core, ends, sums):
    return pl.pallas_call(
        end_rows,
        in_specs=[smem(), whole(*ends.shape), whole(*sums.shape)],
        out_shape=[shape(PLANES, COLS)] * 2,
        compiler_params=params(),
        name="end_rows",
    )(core, ends, sums)


def second_step(
    group_ref, mobility_ref, old_ref, solute_ref, sums_ref, above_ref, below_ref, eta_ref, base_ref, slope_ref
):
    grain = pl.program_id(0)

    @pl.when(grain == 0)
    def _():
        factors(sums_ref, solute_ref, base_ref, slope_ref)

    rate = time_step * mobility_ref[group_ref[grain]]
    planes = [old_ref[0, plane] for plane in range(PLANES)]
    out = stepped(planes, halo_rows(above_ref, grain), halo_rows(below_ref, grain), rate, base_ref, slope_ref)
    for plane in range(PLANES):
        eta_ref[0, plane] = out[plane]


def call_second_step(groups, mobility, eta, solute, sums, above, below):
    grain_block = pl.BlockSpec((1, PLANES, ROWS, COLS), lambda i: (i, 0, 0, 0))
    return pl.pallas_call(
        second_step,
        grid=(GRAINS,),
        in_specs=[
            smem(), smem(), grain_block, whole(*solute.shape), whole(*sums.shape),
            whole(*above.shape), whole(*below.shape),
        ],
        out_specs=grain_block,
        out_shape=shape(*eta.shape),
        scratch_shapes=[pltpu.VMEM(solute.shape, F32)] * 2,
        compiler_params=params(),
        cost_estimate=pl.CostEstimate(flops=20_000_000, bytes_accessed=10_000_000, transcendentals=0),
        name="second_step",
    )(groups, mobility, *from_hbm(eta, solute), sums, *from_hbm(above, below))


def solute_end(core_ref, solute_ref, part_ref, sums_ref, inner_ref, outer_ref, out_ref, potential_ref):
    rows = lax.broadcasted_iota(jnp.int32, (ROWS, COLS), 0)
    first_core = core_ref[0] == 0
    for plane in range(PLANES):
        for block in range(BLOCKS):
            columns = column_block(block)
            potential_ref[plane, :, columns] = part_ref[plane, :, columns] - sums_ref[block, PLANES + plane]
    planes = [potential_ref[plane] for plane in range(PLANES)]
    for plane, across in enumerate(beside(planes)):
        value = planes[plane]
        inner, outer = inner_ref[plane : plane + 1, :], outer_ref[plane : plane + 1, :]
        above, below = jnp.where(first_core, outer, inner), jnp.where(first_core, inner, outer)
        up = jnp.where(rows == 0, above, pltpu.roll(value, 1, 0))
        down = jnp.where(rows == ROWS - 1, below, pltpu.roll(value, ROWS - 1, 0))
        lap = up + down + along_columns(value) + across - 6.0 * value
        out_ref[plane] = solute_ref[plane] + time_step * solute_mobility * lap


def call_solute_end(core, solute, part, sums, inner, outer):
    return pl.pallas_call(
        solute_end,
        in_specs=[smem()] + [whole(*array.shape) for array in (solute, part, sums, inner, outer)],
        out_shape=shape(*solute.shape),
        scratch_shapes=[pltpu.VMEM(solute.shape, F32)],
        compiler_params=params(),
        name="solute_end",
    )(core, solute, part, sums, inner, outer)


def swapped(inner, outer, count):
    inner = lax.ppermute(inner, SPACE, [(i, i ^ 1) for i in range(count)])
    outer = lax.ppermute(outer, SPACE, [(i, (i + 2 * (i % 2) - 1) % count) for i in range(count)])
    return inner, outer


def exchange(to_next, to_prev, count):
    above = lax.ppermute(to_next, SPACE, [(i, (i + 1) % count) for i in range(count)])
    below = lax.ppermute(to_prev, SPACE, [((i + 1) % count, i) for i in range(count)])
    return above, below


def added(parts_ref, index):
    values = [parts_ref[(part,) + index] for part in range(parts_ref.shape[0])]
    while len(values) > 1:
        values = [left + right for left, right in zip(values[::2], values[1::2])]
    return values[0]


def add_parts(parts_ref, out_ref):
    for block in range(out_ref.shape[0]):
        for row in range(out_ref.shape[1]):
            out_ref[block, row] = added(parts_ref, (block, row))


def call_add_parts(parts):
    return pl.pallas_call(
        add_parts, out_shape=shape(*parts.shape[1:]), compiler_params=params(), name="add_parts"
    )(parts)


def owner(parts_ref, copies_ref):
    for plane in range(PLANES):
        two, four = added(parts_ref, (plane,)), added(parts_ref, (PLANES + plane,))
        bulk = solute_beta * (two * two - four)
        for copy in range(copies_ref.shape[0]):
            copies_ref[copy, plane] = two
            copies_ref[copy, PLANES + plane] = bulk


def call_owner(parts):
    return pl.pallas_call(
        owner, out_shape=hbm(BLOCKS, *parts.shape[1:]), compiler_params=params(), name="owner"
    )(parts)


def dealt(blocks, axis):
    return lax.all_to_all(blocks, axis, 0, 0, tiled=True)


def total(sums):
    along = lax.axis_size("x")
    parts = dealt(sums.reshape((along, BLOCKS // along) + sums.shape[1:]), "x")
    parts = dealt(call_add_parts(parts), "yh")
    return dealt(call_owner(parts), GRAIN)


def shards(grain_ids, group_of, group_mobility, seed_noise, concentration):
    count = lax.axis_size("yl") * lax.axis_size("z") * lax.axis_size("core")
    first = (lax.axis_index(GRAIN) * GRAINS).astype(jnp.int32).reshape(1)
    core = lax.axis_index("core").astype(jnp.int32).reshape(1)
    sums, to_next, to_prev = call_first_sums(first, seed_noise, grain_ids, concentration)
    above, below = exchange(to_next, to_prev, count)
    eta, sums, to_next, to_prev, bulk = call_first_step(
        first, group_of, group_mobility, seed_noise, grain_ids, concentration, total(sums), above, below
    )
    mid_above, mid_below = exchange(to_next, to_prev, count)
    sums = total(sums)
    solute, part, ends = call_solute_step(concentration, bulk, above, below, mid_above, mid_below)
    inner, outer = swapped(*call_end_rows(core, ends, sums), count)
    eta = call_second_step(group_of, group_mobility, eta, solute, sums, mid_above, mid_below)
    solute = call_solute_end(core, solute, part, sums, inner, outer)
    return eta, solute


def solution(mesh):
    fine = Mesh(mesh.devices.reshape(2, 8, 2, 4, 4), SPACE + GRAIN)
    placed = (
        P(None, SPACE, None),
        P(GRAIN),
        P(),
        P(GRAIN, None, SPACE, None),
        P(None, SPACE, None),
    )
    return jax.shard_map(
        shards,
        mesh=fine,
        in_specs=placed,
        out_specs=(P(GRAIN, None, SPACE, None), P(None, SPACE, None)),
        check_vma=False,
    )
```

```python
import jax
import jax.numpy as jnp
from jax import lax
from jax.experimental import pallas as pl
from jax.experimental.pallas import tpu as pltpu
from jax.sharding import Mesh, PartitionSpec as P

GRAINS, PLANES, ROWS, COLS, LANES = 6, 3, 16, 2048, 128
BLOCKS = COLS // LANES
SPACE = ("yl", "z", "core")
GRAIN = ("x", "yh")

coef_quad = 1.0
coef_quart = 1.0
cross_gamma = 1.5
gradient_kappa = 0.5
solute_beta = 0.6
bulk_stiff = 1.0
solute_mean = 0.4
solute_kappa = 0.25
solute_mobility = 0.3
time_step = 0.1

F32 = jnp.float32
MIB = 1024 * 1024


def shape(*dims):
    return jax.ShapeDtypeStruct(dims, F32)


def hbm(*dims):
    return pltpu.HBM(dims, F32)


def from_hbm(*arrays):
    return [pltpu.with_memory_space_constraint(array, pltpu.HBM) for array in arrays]


def params(mib=16):
    return pltpu.CompilerParams(vmem_limit_bytes=mib * MIB)


def whole(*dims):
    return pl.BlockSpec(dims, lambda *_: (0,) * len(dims))


def smem():
    return pl.BlockSpec(memory_space=pltpu.SMEM)


def along_columns(value):
    return pltpu.roll(value, 1, 1) + pltpu.roll(value, COLS - 1, 1)


def beside(planes):
    return (planes[0] + planes[1], planes[0] + planes[2], planes[1] + planes[2])


def column_block(block):
    return slice(block * LANES, (block + 1) * LANES)


def first_sums(first_ref, core_ref, noise_ref, more_ref, ids_ref, solute_ref, sums_ref, inner_ref, outer_ref):
    first_core = core_ref[0] == 0
    half = noise_ref.shape[0]
    for plane in range(PLANES):
        ids = ids_ref[plane]
        two = four = None
        for grain in range(GRAINS):
            seed = jnp.where(ids == first_ref[0] + grain, 0.9, 0.0).astype(F32)
            eta = seed + (noise_ref[grain, plane] if grain < half else more_ref[grain - half, plane])
            row = slice(grain * PLANES + plane, grain * PLANES + plane + 1)
            inner_ref[row, :] = jnp.where(first_core, eta[ROWS - 1 :], eta[:1])
            outer_ref[row, :] = jnp.where(first_core, eta[:1], eta[ROWS - 1 :])
            square = eta * eta
            two = square if two is None else two + square
            four = square * square if four is None else four + square * square
        for block in range(sums_ref.shape[0]):
            sums_ref[block, plane] = two[:, column_block(block)]
            sums_ref[block, PLANES + plane] = four[:, column_block(block)]
        row = slice(GRAINS * PLANES + 3 * plane, GRAINS * PLANES + 3 * plane + 3)
        top, bottom = solute_ref[plane, :3], solute_ref[plane, ROWS - 3 :]
        inner_ref[row, :] = jnp.where(first_core, bottom, top)
        outer_ref[row, :] = jnp.where(first_core, top, bottom)


def call_first_sums(first, core, noise, ids, solute):
    width = 512
    edge = GRAINS * PLANES + 3 * PLANES
    return pl.pallas_call(
        first_sums,
        grid=(COLS // width,),
        in_specs=[
            smem(),
            smem(),
            pl.BlockSpec((GRAINS // 2, PLANES, ROWS, width), lambda i: (0, 0, 0, i)),
            pl.BlockSpec((GRAINS // 2, PLANES, ROWS, width), lambda i: (1, 0, 0, i)),
            pl.BlockSpec((PLANES, ROWS, width), lambda i: (0, 0, i)),
            pl.BlockSpec((PLANES, ROWS, width), lambda i: (0, 0, i)),
        ],
        out_specs=[
            pl.BlockSpec((width // LANES, 2 * PLANES, ROWS, LANES), lambda i: (i, 0, 0, 0)),
            pl.BlockSpec((edge, width), lambda i: (0, i)),
            pl.BlockSpec((edge, width), lambda i: (0, i)),
        ],
        out_shape=[
            shape(BLOCKS, 2 * PLANES, ROWS, LANES),
            shape(edge, COLS),
            shape(edge, COLS),
        ],
        compiler_params=params(60),
        name="first_sums",
    )(first, core, noise, noise, ids, solute)


def factors(sums_ref, solute_ref, base_ref, slope_ref):
    for plane in range(PLANES):
        for block in range(BLOCKS):
            columns = column_block(block)
            cross = 2.0 * cross_gamma - 4.0 * solute_beta * solute_ref[plane, :, columns]
            base_ref[plane, :, columns] = (
                coef_quad - 6.0 * gradient_kappa - sums_ref[block, plane] * cross
            )
            slope_ref[plane, :, columns] = cross - coef_quart


def stepped(planes, above, below, rate, base_ref, slope_ref):
    rows = lax.broadcasted_iota(jnp.int32, (ROWS, COLS), 0)
    out = []
    for plane, across in zip(range(PLANES), beside(planes)):
        eta = planes[plane]
        up = jnp.where(rows == 0, above[plane], pltpu.roll(eta, 1, 0))
        down = jnp.where(rows == ROWS - 1, below[plane], pltpu.roll(eta, ROWS - 1, 0))
        around = up + down + along_columns(eta) + across
        bracket = base_ref[plane] + slope_ref[plane] * (eta * eta)
        out.append(eta + rate * (eta * bracket + gradient_kappa * around))
    return out


def halo_rows(core_ref, inner_ref, outer_ref, grain):
    above, below = [], []
    for plane in range(PLANES):
        row = pl.ds(grain * PLANES + plane, 1)
        inner, outer = inner_ref[row, :], outer_ref[row, :]
        above.append(jnp.where(core_ref[0] == 0, outer, inner))
        below.append(jnp.where(core_ref[0] == 0, inner, outer))
    return above, below


def first_step(
    first_ref, core_ref, group_ref, mobility_ref, noise_ref, ids_ref, solute_ref, sums_ref, inner_ref, outer_ref,
    eta_ref, next_sums_ref, next_inner_ref, next_outer_ref, bulk_ref, base_ref, slope_ref,
):
    grain = pl.program_id(0)
    first_core = core_ref[0] == 0

    @pl.when(grain == 0)
    def _():
        factors(sums_ref, solute_ref, base_ref, slope_ref)
        for plane in range(PLANES):
            row = GRAINS * PLANES + 2 * plane
            for block in range(BLOCKS):
                columns = column_block(block)
                bulk = sums_ref[block, PLANES + plane]
                bulk_ref[plane, :, columns] = bulk
                next_inner_ref[row : row + 2, columns] = jnp.where(first_core, bulk[ROWS - 2 :], bulk[:2])
                next_outer_ref[row : row + 2, columns] = jnp.where(first_core, bulk[:2], bulk[ROWS - 2 :])

    rate = time_step * mobility_ref[group_ref[grain]]
    planes = [
        jnp.where(ids_ref[plane] == first_ref[0] + grain, 0.9, 0.0).astype(F32) + noise_ref[0, plane]
        for plane in range(PLANES)
    ]
    out = stepped(planes, *halo_rows(core_ref, inner_ref, outer_ref, grain), rate, base_ref, slope_ref)
    for plane in range(PLANES):
        eta = out[plane]
        eta_ref[0, plane] = eta
        row = pl.ds(grain * PLANES + plane, 1)
        next_inner_ref[row, :] = jnp.where(first_core, eta[ROWS - 1 :], eta[:1])
        next_outer_ref[row, :] = jnp.where(first_core, eta[:1], eta[ROWS - 1 :])
    for plane in range(PLANES):
        square = out[plane] * out[plane]
        fourth = square * square

        @pl.when(grain == 0)
        def _():
            for block in range(BLOCKS):
                next_sums_ref[block, plane] = square[:, column_block(block)]
                next_sums_ref[block, PLANES + plane] = fourth[:, column_block(block)]

        @pl.when(grain != 0)
        def _():
            for block in range(BLOCKS):
                next_sums_ref[block, plane] += square[:, column_block(block)]
                next_sums_ref[block, PLANES + plane] += fourth[:, column_block(block)]


def call_first_step(first, core, groups, mobility, noise, ids, solute, sums, inner, outer):
    edge = GRAINS * PLANES + 2 * PLANES
    grain_block = pl.BlockSpec((1, PLANES, ROWS, COLS), lambda i: (i, 0, 0, 0))
    return pl.pallas_call(
        first_step,
        grid=(GRAINS,),
        in_specs=[
            smem(), smem(), smem(), smem(), grain_block,
            whole(*ids.shape), whole(*solute.shape), whole(*sums.shape),
            whole(*inner.shape), whole(*outer.shape),
        ],
        out_specs=[grain_block, whole(*sums.shape)]
        + [whole(edge, COLS)] * 2
        + [whole(*solute.shape)],
        out_shape=[hbm(*noise.shape), shape(*sums.shape)]
        + [shape(edge, COLS)] * 2
        + [hbm(*solute.shape)],
        scratch_shapes=[pltpu.VMEM(solute.shape, F32)] * 2,
        compiler_params=params(),
        name="first_step",
    )(first, core, groups, mobility, noise, ids, solute, sums, *from_hbm(inner, outer))


PAD = 8
DEEP = ROWS + 2 * PAD


def laplace(planes):
    height = planes[0].shape[0]
    return [
        pltpu.roll(value, 1, 0) + pltpu.roll(value, height - 1, 0) + along_columns(value) + across - 6.0 * value
        for value, across in zip(planes, beside(planes))
    ]


def solute_step(
    core_ref, solute_ref, middle_ref, inner_ref, outer_ref, mid_inner_ref, mid_outer_ref,
    out_ref, part_ref, ends_ref, deep_ref, bulk_ref,
):
    first_core = core_ref[0] == 0

    def sides(inner, outer):
        return jnp.where(first_core, outer, inner), jnp.where(first_core, inner, outer)

    for plane in range(PLANES):
        for ref in (deep_ref, bulk_ref):
            ref[plane, :PAD] = jnp.zeros((PAD, COLS), F32)
            ref[plane, PAD + ROWS :] = jnp.zeros((PAD, COLS), F32)
        row = GRAINS * PLANES + 3 * plane
        above, below = sides(inner_ref[row : row + 3, :], outer_ref[row : row + 3, :])
        deep_ref[plane, PAD - 3 : PAD] = above
        deep_ref[plane, PAD : PAD + ROWS] = solute_ref[plane]
        deep_ref[plane, PAD + ROWS : PAD + ROWS + 3] = below
        row = GRAINS * PLANES + 2 * plane
        above, below = sides(mid_inner_ref[row : row + 2, :], mid_outer_ref[row : row + 2, :])
        bulk_ref[plane, PAD - 2 : PAD] = above
        bulk_ref[plane, PAD + ROWS : PAD + ROWS + 2] = below
        bulk_ref[plane, PAD : PAD + ROWS] = middle_ref[plane]
    solute = [deep_ref[plane] for plane in range(PLANES)]
    potential = [
        2.0 * bulk_stiff * (solute[plane] - solute_mean) - bulk_ref[plane] - solute_kappa * lap
        for plane, lap in enumerate(laplace(solute))
    ]
    moved = [
        solute[plane] + time_step * solute_mobility * lap for plane, lap in enumerate(laplace(potential))
    ]
    for plane, lap in enumerate(laplace(moved)):
        part = 2.0 * bulk_stiff * (moved[plane] - solute_mean) - solute_kappa * lap
        out_ref[plane] = moved[plane][PAD : PAD + ROWS]
        part_ref[plane] = part[PAD : PAD + ROWS]
        ends_ref[plane : plane + 1, :] = part[PAD : PAD + 1]
        ends_ref[PLANES + plane : PLANES + plane + 1, :] = part[PAD + ROWS - 1 : PAD + ROWS]


def call_solute_step(core, *arrays):
    solute = arrays[0]
    return pl.pallas_call(
        solute_step,
        in_specs=[smem()] + [whole(*array.shape) for array in arrays],
        out_shape=[hbm(*solute.shape)] * 2 + [hbm(2 * PLANES, COLS)],
        scratch_shapes=[pltpu.VMEM((PLANES, DEEP, COLS), F32)] * 2,
        compiler_params=params(),
        name="solute_step",
    )(core, *from_hbm(*arrays))


def end_rows(core_ref, ends_ref, sums_ref, inner_ref, outer_ref):
    for plane in range(PLANES):
        row = slice(plane, plane + 1)
        for block in range(BLOCKS):
            columns = column_block(block)
            bulk = sums_ref[block, PLANES + plane]
            top = ends_ref[plane : plane + 1, columns] - bulk[:1]
            bottom = ends_ref[PLANES + plane : PLANES + plane + 1, columns] - bulk[ROWS - 1 :]
            inner_ref[row, columns] = jnp.where(core_ref[0] == 0, bottom, top)
            outer_ref[row, columns] = jnp.where(core_ref[0] == 0, top, bottom)


def call_end_rows(core, ends, sums):
    return pl.pallas_call(
        end_rows,
        in_specs=[smem(), whole(*ends.shape), whole(*sums.shape)],
        out_shape=[shape(PLANES, COLS)] * 2,
        compiler_params=params(),
        name="end_rows",
    )(core, ends, sums)


def second_step(
    core_ref, group_ref, mobility_ref, old_ref, solute_ref, sums_ref, inner_ref, outer_ref, eta_ref, base_ref, slope_ref
):
    grain = pl.program_id(0)

    @pl.when(grain == 0)
    def _():
        factors(sums_ref, solute_ref, base_ref, slope_ref)

    rate = time_step * mobility_ref[group_ref[grain]]
    planes = [old_ref[0, plane] for plane in range(PLANES)]
    out = stepped(planes, *halo_rows(core_ref, inner_ref, outer_ref, grain), rate, base_ref, slope_ref)
    for plane in range(PLANES):
        eta_ref[0, plane] = out[plane]


def call_second_step(core, groups, mobility, eta, solute, sums, inner, outer):
    grain_block = pl.BlockSpec((1, PLANES, ROWS, COLS), lambda i: (i, 0, 0, 0))
    return pl.pallas_call(
        second_step,
        grid=(GRAINS,),
        in_specs=[
            smem(), smem(), smem(), grain_block, whole(*solute.shape), whole(*sums.shape),
            whole(*inner.shape), whole(*outer.shape),
        ],
        out_specs=grain_block,
        out_shape=shape(*eta.shape),
        scratch_shapes=[pltpu.VMEM(solute.shape, F32)] * 2,
        compiler_params=params(),
        cost_estimate=pl.CostEstimate(flops=20_000_000, bytes_accessed=10_000_000, transcendentals=0),
        name="second_step",
    )(core, groups, mobility, eta, solute, sums, inner, outer)


def solute_end(core_ref, solute_ref, part_ref, sums_ref, inner_ref, outer_ref, out_ref, potential_ref):
    rows = lax.broadcasted_iota(jnp.int32, (ROWS, COLS), 0)
    first_core = core_ref[0] == 0
    for plane in range(PLANES):
        for block in range(BLOCKS):
            columns = column_block(block)
            potential_ref[plane, :, columns] = part_ref[plane, :, columns] - sums_ref[block, PLANES + plane]
    planes = [potential_ref[plane] for plane in range(PLANES)]
    for plane, across in enumerate(beside(planes)):
        value = planes[plane]
        inner, outer = inner_ref[plane : plane + 1, :], outer_ref[plane : plane + 1, :]
        above, below = jnp.where(first_core, outer, inner), jnp.where(first_core, inner, outer)
        up = jnp.where(rows == 0, above, pltpu.roll(value, 1, 0))
        down = jnp.where(rows == ROWS - 1, below, pltpu.roll(value, ROWS - 1, 0))
        lap = up + down + along_columns(value) + across - 6.0 * value
        out_ref[plane] = solute_ref[plane] + time_step * solute_mobility * lap


def call_solute_end(core, solute, part, sums, inner, outer):
    return pl.pallas_call(
        solute_end,
        in_specs=[smem()] + [whole(*array.shape) for array in (solute, part, sums, inner, outer)],
        out_shape=shape(*solute.shape),
        scratch_shapes=[pltpu.VMEM(solute.shape, F32)],
        compiler_params=params(),
        name="solute_end",
    )(core, solute, part, sums, inner, outer)


def swapped(inner, outer, count):
    inner = lax.ppermute(inner, SPACE, [(i, i ^ 1) for i in range(count)])
    outer = lax.ppermute(outer, SPACE, [(i, (i + 2 * (i % 2) - 1) % count) for i in range(count)])
    return inner, outer


def added(parts_ref, index):
    values = [parts_ref[(part,) + index] for part in range(parts_ref.shape[0])]
    while len(values) > 1:
        values = [left + right for left, right in zip(values[::2], values[1::2])]
    return values[0]


def add_parts(parts_ref, out_ref):
    for block in range(out_ref.shape[0]):
        for row in range(out_ref.shape[1]):
            out_ref[block, row] = added(parts_ref, (block, row))


def call_add_parts(parts):
    return pl.pallas_call(
        add_parts, out_shape=shape(*parts.shape[1:]), compiler_params=params(), name="add_parts"
    )(parts)


def owner(parts_ref, copies_ref):
    for plane in range(PLANES):
        two, four = added(parts_ref, (plane,)), added(parts_ref, (PLANES + plane,))
        bulk = solute_beta * (two * two - four)
        for copy in range(copies_ref.shape[0]):
            copies_ref[copy, plane] = two
            copies_ref[copy, PLANES + plane] = bulk


def call_owner(parts):
    return pl.pallas_call(
        owner, out_shape=shape(*parts.shape), compiler_params=params(), name="owner"
    )(parts)


def copies(value_ref, out_ref):
    for copy in range(out_ref.shape[0]):
        out_ref[copy] = value_ref[...]


def call_copies(value, count):
    return pl.pallas_call(
        copies, out_shape=shape(count, *value.shape), compiler_params=params(), name="copies"
    )(value)


def dealt(blocks, axis):
    return lax.all_to_all(blocks, axis, 0, 0, tiled=True)


def total(sums, beside_it):
    along = lax.axis_size("x")
    parts = dealt(sums.reshape((along, BLOCKS // along) + sums.shape[1:]), "x")
    parts, *beside_it = lax.optimization_barrier((parts, *beside_it))
    parts = dealt(call_add_parts(parts), "yh")
    parts = dealt(call_owner(parts), "yh")
    return dealt(call_copies(parts, along), "x").reshape(sums.shape), beside_it


def shards(grain_ids, group_of, group_mobility, seed_noise, concentration):
    count = lax.axis_size("yl") * lax.axis_size("z") * lax.axis_size("core")
    first = (lax.axis_index(GRAIN) * GRAINS).astype(jnp.int32).reshape(1)
    core = lax.axis_index("core").astype(jnp.int32).reshape(1)
    sums, inner, outer = call_first_sums(first, core, seed_noise, grain_ids, concentration)
    sums, (inner, outer) = total(sums, swapped(inner, outer, count))
    eta, sums, mid_inner, mid_outer, bulk = call_first_step(
        first, core, group_of, group_mobility, seed_noise, grain_ids, concentration, sums, inner, outer
    )
    mid_inner, mid_outer = swapped(mid_inner, mid_outer, count)
    later = call_solute_step(core, concentration, bulk, inner, outer, mid_inner, mid_outer)
    sums, (mid_inner, mid_outer, solute, part, ends) = total(sums, (mid_inner, mid_outer, *later))
    inner, outer = swapped(*call_end_rows(core, ends, sums), count)
    eta = call_second_step(core, group_of, group_mobility, eta, solute, sums, mid_inner, mid_outer)
    solute = call_solute_end(core, solute, part, sums, inner, outer)
    return eta, solute


def solution(mesh):
    fine = Mesh(mesh.devices.reshape(2, 8, 2, 4, 4), SPACE + GRAIN)
    placed = (
        P(None, SPACE, None),
        P(GRAIN),
        P(),
        P(GRAIN, None, SPACE, None),
        P(None, SPACE, None),
    )
    return jax.shard_map(
        shards,
        mesh=fine,
        in_specs=placed,
        out_specs=(P(GRAIN, None, SPACE, None), P(None, SPACE, None)),
        check_vma=False,
    )
```

```python
import jax
import jax.numpy as jnp
from jax import lax
from jax.experimental import pallas as pl
from jax.experimental.pallas import tpu as pltpu
from jax.sharding import Mesh, PartitionSpec as P

GRAINS, PLANES, ROWS, COLS, LANES = 6, 3, 16, 2048, 128
BLOCKS = COLS // LANES
SPACE = ("yl", "z", "core")
GRAIN = ("x", "yh")

coef_quad = 1.0
coef_quart = 1.0
cross_gamma = 1.5
gradient_kappa = 0.5
solute_beta = 0.6
bulk_stiff = 1.0
solute_mean = 0.4
solute_kappa = 0.25
solute_mobility = 0.3
time_step = 0.1

F32 = jnp.float32
MIB = 1024 * 1024


def shape(*dims):
    return jax.ShapeDtypeStruct(dims, F32)


def hbm(*dims):
    return pltpu.HBM(dims, F32)


def from_hbm(*arrays):
    return [pltpu.with_memory_space_constraint(array, pltpu.HBM) for array in arrays]


def params(mib=16):
    return pltpu.CompilerParams(vmem_limit_bytes=mib * MIB)


def whole(*dims):
    return pl.BlockSpec(dims, lambda *_: (0,) * len(dims))


def smem():
    return pl.BlockSpec(memory_space=pltpu.SMEM)


def along_columns(value):
    return pltpu.roll(value, 1, 1) + pltpu.roll(value, COLS - 1, 1)


def beside(planes):
    return (planes[0] + planes[1], planes[0] + planes[2], planes[1] + planes[2])


def column_block(block):
    return slice(block * LANES, (block + 1) * LANES)


def first_sums(first_ref, core_ref, noise_ref, ids_ref, sums_ref, inner_ref, outer_ref):
    first_core = core_ref[0] == 0
    for plane in range(PLANES):
        ids = ids_ref[plane]
        two = four = None
        for grain in range(GRAINS):
            seed = jnp.where(ids == first_ref[0] + grain, 0.9, 0.0).astype(F32)
            eta = seed + noise_ref[grain, plane]
            row = slice(grain * PLANES + plane, grain * PLANES + plane + 1)
            inner_ref[row, :] = jnp.where(first_core, eta[ROWS - 1 :], eta[:1])
            outer_ref[row, :] = jnp.where(first_core, eta[:1], eta[ROWS - 1 :])
            square = eta * eta
            two = square if two is None else two + square
            four = square * square if four is None else four + square * square
        for block in range(sums_ref.shape[0]):
            sums_ref[block, plane] = two[:, column_block(block)]
            sums_ref[block, PLANES + plane] = four[:, column_block(block)]


def call_first_sums(first, core, noise, ids):
    width = 512
    edge = GRAINS * PLANES
    return pl.pallas_call(
        first_sums,
        grid=(COLS // width,),
        in_specs=[
            smem(),
            smem(),
            pl.BlockSpec((GRAINS, PLANES, ROWS, width), lambda i: (0, 0, 0, i)),
            pl.BlockSpec((PLANES, ROWS, width), lambda i: (0, 0, i)),
        ],
        out_specs=[
            pl.BlockSpec((width // LANES, 2 * PLANES, ROWS, LANES), lambda i: (i, 0, 0, 0)),
            pl.BlockSpec((edge, width), lambda i: (0, i)),
            pl.BlockSpec((edge, width), lambda i: (0, i)),
        ],
        out_shape=[
            shape(BLOCKS, 2 * PLANES, ROWS, LANES),
            shape(edge, COLS),
            shape(edge, COLS),
        ],
        compiler_params=params(60),
        name="first_sums",
    )(first, core, noise, ids)


def factors(sums_ref, solute_ref, base_ref, slope_ref):
    for plane in range(PLANES):
        for block in range(BLOCKS):
            columns = column_block(block)
            cross = 2.0 * cross_gamma - 4.0 * solute_beta * solute_ref[plane, :, columns]
            base_ref[plane, :, columns] = (
                coef_quad - 6.0 * gradient_kappa - sums_ref[block, plane] * cross
            )
            slope_ref[plane, :, columns] = cross - coef_quart


def stepped(planes, above, below, rate, base_ref, slope_ref):
    rows = lax.broadcasted_iota(jnp.int32, (ROWS, COLS), 0)
    out = []
    for plane, across in zip(range(PLANES), beside(planes)):
        eta = planes[plane]
        up = jnp.where(rows == 0, above[plane], pltpu.roll(eta, 1, 0))
        down = jnp.where(rows == ROWS - 1, below[plane], pltpu.roll(eta, ROWS - 1, 0))
        around = up + down + along_columns(eta) + across
        bracket = base_ref[plane] + slope_ref[plane] * (eta * eta)
        out.append(eta + rate * (eta * bracket + gradient_kappa * around))
    return out


def halo_rows(core_ref, inner_ref, outer_ref, grain):
    above, below = [], []
    for plane in range(PLANES):
        row = pl.ds(grain * PLANES + plane, 1)
        inner, outer = inner_ref[row, :], outer_ref[row, :]
        above.append(jnp.where(core_ref[0] == 0, outer, inner))
        below.append(jnp.where(core_ref[0] == 0, inner, outer))
    return above, below


def first_step(
    first_ref, core_ref, group_ref, mobility_ref, noise_ref, ids_ref, solute_ref, sums_ref, inner_ref, outer_ref,
    eta_ref, next_sums_ref, next_inner_ref, next_outer_ref, bulk_ref, base_ref, slope_ref,
):
    grain = pl.program_id(0)
    first_core = core_ref[0] == 0

    @pl.when(grain == 0)
    def _():
        factors(sums_ref, solute_ref, base_ref, slope_ref)
        for plane in range(PLANES):
            row = GRAINS * PLANES + 2 * plane
            for block in range(BLOCKS):
                columns = column_block(block)
                bulk = sums_ref[block, PLANES + plane]
                bulk_ref[plane, :, columns] = bulk
                next_inner_ref[row : row + 2, columns] = jnp.where(first_core, bulk[ROWS - 2 :], bulk[:2])
                next_outer_ref[row : row + 2, columns] = jnp.where(first_core, bulk[:2], bulk[ROWS - 2 :])
            row = slice((GRAINS + 2 + plane) * PLANES, (GRAINS + 3 + plane) * PLANES)
            top, bottom = solute_ref[plane, :3], solute_ref[plane, ROWS - 3 :]
            next_inner_ref[row, :] = jnp.where(first_core, bottom, top)
            next_outer_ref[row, :] = jnp.where(first_core, top, bottom)

    rate = time_step * mobility_ref[group_ref[grain]]
    planes = [
        jnp.where(ids_ref[plane] == first_ref[0] + grain, 0.9, 0.0).astype(F32) + noise_ref[0, plane]
        for plane in range(PLANES)
    ]
    out = stepped(planes, *halo_rows(core_ref, inner_ref, outer_ref, grain), rate, base_ref, slope_ref)
    for plane in range(PLANES):
        eta = out[plane]
        eta_ref[0, plane] = eta
        row = pl.ds(grain * PLANES + plane, 1)
        next_inner_ref[row, :] = jnp.where(first_core, eta[ROWS - 1 :], eta[:1])
        next_outer_ref[row, :] = jnp.where(first_core, eta[:1], eta[ROWS - 1 :])
    for plane in range(PLANES):
        square = out[plane] * out[plane]
        fourth = square * square

        @pl.when(grain == 0)
        def _():
            for block in range(BLOCKS):
                next_sums_ref[block, plane] = square[:, column_block(block)]
                next_sums_ref[block, PLANES + plane] = fourth[:, column_block(block)]

        @pl.when(grain != 0)
        def _():
            for block in range(BLOCKS):
                next_sums_ref[block, plane] += square[:, column_block(block)]
                next_sums_ref[block, PLANES + plane] += fourth[:, column_block(block)]


def call_first_step(first, core, groups, mobility, noise, ids, solute, sums, inner, outer):
    edge = GRAINS * PLANES + 5 * PLANES
    grain_block = pl.BlockSpec((1, PLANES, ROWS, COLS), lambda i: (i, 0, 0, 0))
    return pl.pallas_call(
        first_step,
        grid=(GRAINS,),
        in_specs=[
            smem(), smem(), smem(), smem(), grain_block,
            whole(*ids.shape), whole(*solute.shape), whole(*sums.shape),
            whole(*inner.shape), whole(*outer.shape),
        ],
        out_specs=[grain_block, whole(*sums.shape)]
        + [whole(edge, COLS)] * 2
        + [whole(*solute.shape)],
        out_shape=[hbm(*noise.shape), shape(*sums.shape)]
        + [shape(edge, COLS)] * 2
        + [hbm(*solute.shape)],
        scratch_shapes=[pltpu.VMEM(solute.shape, F32)] * 2,
        compiler_params=params(),
        name="first_step",
    )(first, core, groups, mobility, noise, ids, solute, sums, *from_hbm(inner, outer))


PAD = 8
DEEP = ROWS + 2 * PAD


def laplace(planes):
    height = planes[0].shape[0]
    return [
        pltpu.roll(value, 1, 0) + pltpu.roll(value, height - 1, 0) + along_columns(value) + across - 6.0 * value
        for value, across in zip(planes, beside(planes))
    ]


def solute_step(
    core_ref, solute_ref, middle_ref, inner_ref, outer_ref,
    out_ref, part_ref, ends_ref, deep_ref, bulk_ref,
):
    first_core = core_ref[0] == 0

    def sides(inner, outer):
        return jnp.where(first_core, outer, inner), jnp.where(first_core, inner, outer)

    for plane in range(PLANES):
        for ref in (deep_ref, bulk_ref):
            ref[plane, :PAD] = jnp.zeros((PAD, COLS), F32)
            ref[plane, PAD + ROWS :] = jnp.zeros((PAD, COLS), F32)
        row = (GRAINS + 2 + plane) * PLANES
        above, below = sides(inner_ref[row : row + 3, :], outer_ref[row : row + 3, :])
        deep_ref[plane, PAD - 3 : PAD] = above
        deep_ref[plane, PAD : PAD + ROWS] = solute_ref[plane]
        deep_ref[plane, PAD + ROWS : PAD + ROWS + 3] = below
        row = GRAINS * PLANES + 2 * plane
        above, below = sides(inner_ref[row : row + 2, :], outer_ref[row : row + 2, :])
        bulk_ref[plane, PAD - 2 : PAD] = above
        bulk_ref[plane, PAD + ROWS : PAD + ROWS + 2] = below
        bulk_ref[plane, PAD : PAD + ROWS] = middle_ref[plane]
    solute = [deep_ref[plane] for plane in range(PLANES)]
    potential = [
        2.0 * bulk_stiff * (solute[plane] - solute_mean) - bulk_ref[plane] - solute_kappa * lap
        for plane, lap in enumerate(laplace(solute))
    ]
    moved = [
        solute[plane] + time_step * solute_mobility * lap for plane, lap in enumerate(laplace(potential))
    ]
    for plane, lap in enumerate(laplace(moved)):
        part = 2.0 * bulk_stiff * (moved[plane] - solute_mean) - solute_kappa * lap
        out_ref[plane] = moved[plane][PAD : PAD + ROWS]
        part_ref[plane] = part[PAD : PAD + ROWS]
        ends_ref[plane : plane + 1, :] = part[PAD : PAD + 1]
        ends_ref[PLANES + plane : PLANES + plane + 1, :] = part[PAD + ROWS - 1 : PAD + ROWS]


def call_solute_step(core, *arrays):
    solute = arrays[0]
    return pl.pallas_call(
        solute_step,
        in_specs=[smem()] + [whole(*array.shape) for array in arrays],
        out_shape=[shape(*solute.shape)] * 2 + [shape(2 * PLANES, COLS)],
        scratch_shapes=[pltpu.VMEM((PLANES, DEEP, COLS), F32)] * 2,
        compiler_params=params(),
        name="solute_step",
    )(core, *from_hbm(*arrays))


def end_rows(core_ref, ends_ref, sums_ref, inner_ref, outer_ref):
    for plane in range(PLANES):
        row = slice(plane, plane + 1)
        for block in range(BLOCKS):
            columns = column_block(block)
            bulk = sums_ref[block, PLANES + plane]
            top = ends_ref[plane : plane + 1, columns] - bulk[:1]
            bottom = ends_ref[PLANES + plane : PLANES + plane + 1, columns] - bulk[ROWS - 1 :]
            inner_ref[row, columns] = jnp.where(core_ref[0] == 0, bottom, top)
            outer_ref[row, columns] = jnp.where(core_ref[0] == 0, top, bottom)


def call_end_rows(core, ends, sums):
    return pl.pallas_call(
        end_rows,
        in_specs=[smem(), whole(*ends.shape), whole(*sums.shape)],
        out_shape=[shape(PLANES, COLS)] * 2,
        compiler_params=params(),
        name="end_rows",
    )(core, ends, sums)


def second_step(
    core_ref, group_ref, mobility_ref, old_ref, solute_ref, sums_ref, inner_ref, outer_ref, eta_ref, base_ref, slope_ref
):
    grain = pl.program_id(0)

    @pl.when(grain == 0)
    def _():
        factors(sums_ref, solute_ref, base_ref, slope_ref)

    rate = time_step * mobility_ref[group_ref[grain]]
    planes = [old_ref[0, plane] for plane in range(PLANES)]
    out = stepped(planes, *halo_rows(core_ref, inner_ref, outer_ref, grain), rate, base_ref, slope_ref)
    for plane in range(PLANES):
        eta_ref[0, plane] = out[plane]


def call_second_step(core, groups, mobility, eta, solute, sums, inner, outer):
    grain_block = pl.BlockSpec((1, PLANES, ROWS, COLS), lambda i: (i, 0, 0, 0))
    return pl.pallas_call(
        second_step,
        grid=(GRAINS,),
        in_specs=[
            smem(), smem(), smem(), grain_block, whole(*solute.shape), whole(*sums.shape),
            whole(*inner.shape), whole(*outer.shape),
        ],
        out_specs=grain_block,
        out_shape=shape(*eta.shape),
        scratch_shapes=[pltpu.VMEM(solute.shape, F32)] * 2,
        compiler_params=params(),
        cost_estimate=pl.CostEstimate(flops=20_000_000, bytes_accessed=10_000_000, transcendentals=0),
        name="second_step",
    )(core, groups, mobility, eta, solute, sums, *from_hbm(inner, outer))


def solute_end(core_ref, solute_ref, part_ref, sums_ref, inner_ref, outer_ref, out_ref, potential_ref):
    rows = lax.broadcasted_iota(jnp.int32, (ROWS, COLS), 0)
    first_core = core_ref[0] == 0
    for plane in range(PLANES):
        for block in range(BLOCKS):
            columns = column_block(block)
            potential_ref[plane, :, columns] = part_ref[plane, :, columns] - sums_ref[block, PLANES + plane]
    planes = [potential_ref[plane] for plane in range(PLANES)]
    for plane, across in enumerate(beside(planes)):
        value = planes[plane]
        inner, outer = inner_ref[plane : plane + 1, :], outer_ref[plane : plane + 1, :]
        above, below = jnp.where(first_core, outer, inner), jnp.where(first_core, inner, outer)
        up = jnp.where(rows == 0, above, pltpu.roll(value, 1, 0))
        down = jnp.where(rows == ROWS - 1, below, pltpu.roll(value, ROWS - 1, 0))
        lap = up + down + along_columns(value) + across - 6.0 * value
        out_ref[plane] = solute_ref[plane] + time_step * solute_mobility * lap


def call_solute_end(core, solute, part, sums, inner, outer):
    return pl.pallas_call(
        solute_end,
        in_specs=[smem()] + [whole(*array.shape) for array in (solute, part, sums, inner, outer)],
        out_shape=shape(*solute.shape),
        scratch_shapes=[pltpu.VMEM(solute.shape, F32)],
        compiler_params=params(),
        name="solute_end",
    )(core, solute, part, sums, inner, outer)


def swapped(inner, outer, count):
    inner = lax.ppermute(inner, SPACE, [(i, i ^ 1) for i in range(count)])
    outer = lax.ppermute(outer, SPACE, [(i, (i + 2 * (i % 2) - 1) % count) for i in range(count)])
    return inner, outer


def added(parts_ref, index):
    values = [parts_ref[(part,) + index] for part in range(parts_ref.shape[0])]
    while len(values) > 1:
        values = [left + right for left, right in zip(values[::2], values[1::2])]
    return values[0]


def add_parts(parts_ref, out_ref):
    for block in range(out_ref.shape[0]):
        for row in range(out_ref.shape[1]):
            out_ref[block, row] = added(parts_ref, (block, row))


def call_add_parts(parts):
    return pl.pallas_call(
        add_parts, out_shape=shape(*parts.shape[1:]), compiler_params=params(), name="add_parts"
    )(parts)


def owner(parts_ref, copies_ref):
    for plane in range(PLANES):
        two, four = added(parts_ref, (plane,)), added(parts_ref, (PLANES + plane,))
        bulk = solute_beta * (two * two - four)
        for copy in range(copies_ref.shape[0]):
            copies_ref[copy, plane] = two
            copies_ref[copy, PLANES + plane] = bulk


def call_owner(parts):
    return pl.pallas_call(
        owner, out_shape=shape(*parts.shape), compiler_params=params(), name="owner"
    )(parts)


def copies(value_ref, out_ref):
    for copy in range(out_ref.shape[0]):
        out_ref[copy] = value_ref[...]


def call_copies(value, count):
    return pl.pallas_call(
        copies, out_shape=shape(count, *value.shape), compiler_params=params(), name="copies"
    )(value)


def dealt(blocks, axis):
    return lax.all_to_all(blocks, axis, 0, 0, tiled=True)


def total(sums, beside_it):
    along = lax.axis_size("x")
    parts = dealt(sums.reshape((along, BLOCKS // along) + sums.shape[1:]), "x")
    parts, *beside_it = lax.optimization_barrier((parts, *beside_it))
    parts = dealt(call_add_parts(parts), "yh")
    parts = dealt(call_owner(parts), "yh")
    return dealt(call_copies(parts, along), "x").reshape(sums.shape), beside_it


def shards(grain_ids, group_of, group_mobility, seed_noise, concentration):
    count = lax.axis_size("yl") * lax.axis_size("z") * lax.axis_size("core")
    first = (lax.axis_index(GRAIN) * GRAINS).astype(jnp.int32).reshape(1)
    core = lax.axis_index("core").astype(jnp.int32).reshape(1)
    sums, inner, outer = call_first_sums(first, core, seed_noise, grain_ids)
    sums, (inner, outer) = total(sums, swapped(inner, outer, count))
    eta, sums, inner, outer, bulk = call_first_step(
        first, core, group_of, group_mobility, seed_noise, grain_ids, concentration, sums, inner, outer
    )
    sums, (mid_inner, mid_outer) = total(sums, swapped(inner, outer, count))
    solute, part, ends = call_solute_step(core, concentration, bulk, mid_inner, mid_outer)
    inner, outer = swapped(*call_end_rows(core, ends, sums), count)
    eta = call_second_step(core, group_of, group_mobility, eta, solute, sums, mid_inner, mid_outer)
    solute = call_solute_end(core, solute, part, sums, inner, outer)
    return eta, solute


def solution(mesh):
    fine = Mesh(mesh.devices.reshape(2, 8, 2, 4, 4), SPACE + GRAIN)
    placed = (
        P(None, SPACE, None),
        P(GRAIN),
        P(),
        P(GRAIN, None, SPACE, None),
        P(None, SPACE, None),
    )
    return jax.shard_map(
        shards,
        mesh=fine,
        in_specs=placed,
        out_specs=(P(GRAIN, None, SPACE, None), P(None, SPACE, None)),
        check_vma=False,
    )
```

```python
import jax
import jax.numpy as jnp
from jax import lax
from jax.experimental import pallas as pl
from jax.experimental.pallas import tpu as pltpu
from jax.sharding import Mesh, PartitionSpec as P

GRAINS, PLANES, ROWS, COLS, LANES = 6, 3, 16, 2048, 128
BLOCKS = COLS // LANES
SPACE = ("yl", "z", "core")
GRAIN = ("x", "yh")

coef_quad = 1.0
coef_quart = 1.0
cross_gamma = 1.5
gradient_kappa = 0.5
solute_beta = 0.6
bulk_stiff = 1.0
solute_mean = 0.4
solute_kappa = 0.25
solute_mobility = 0.3
time_step = 0.1

F32 = jnp.float32
MIB = 1024 * 1024


def shape(*dims):
    return jax.ShapeDtypeStruct(dims, F32)


def hbm(*dims):
    return pltpu.HBM(dims, F32)


def from_hbm(*arrays):
    return [pltpu.with_memory_space_constraint(array, pltpu.HBM) for array in arrays]


def params(mib=16):
    return pltpu.CompilerParams(vmem_limit_bytes=mib * MIB)


def whole(*dims):
    return pl.BlockSpec(dims, lambda *_: (0,) * len(dims))


def smem():
    return pl.BlockSpec(memory_space=pltpu.SMEM)


def along_columns(value):
    return pltpu.roll(value, 1, 1) + pltpu.roll(value, COLS - 1, 1)


def beside(planes):
    return (planes[0] + planes[1], planes[0] + planes[2], planes[1] + planes[2])


def column_block(block):
    return slice(block * LANES, (block + 1) * LANES)


def first_sums(first_ref, noise_ref, ids_ref, solute_ref, sums_ref, next_ref, prev_ref):
    for plane in range(PLANES):
        ids = ids_ref[plane]
        two = four = None
        for grain in range(GRAINS):
            seed = jnp.where(ids == first_ref[0] + grain, 0.9, 0.0).astype(F32)
            eta = seed + noise_ref[grain, plane]
            row = grain * PLANES + plane
            prev_ref[row : row + 1, :] = eta[:1]
            next_ref[row : row + 1, :] = eta[ROWS - 1 :]
            square = eta * eta
            two = square if two is None else two + square
            four = square * square if four is None else four + square * square
        for block in range(sums_ref.shape[0]):
            sums_ref[block, plane] = two[:, column_block(block)]
            sums_ref[block, PLANES + plane] = four[:, column_block(block)]
        row = GRAINS * PLANES + 3 * plane
        prev_ref[row : row + 3, :] = solute_ref[plane, :3]
        next_ref[row : row + 3, :] = solute_ref[plane, ROWS - 3 :]


def call_first_sums(first, noise, ids, solute):
    width = 512
    edge = GRAINS * PLANES + 3 * PLANES
    return pl.pallas_call(
        first_sums,
        grid=(COLS // width,),
        in_specs=[
            smem(),
            pl.BlockSpec((GRAINS, PLANES, ROWS, width), lambda i: (0, 0, 0, i)),
            pl.BlockSpec((PLANES, ROWS, width), lambda i: (0, 0, i)),
            pl.BlockSpec((PLANES, ROWS, width), lambda i: (0, 0, i)),
        ],
        out_specs=[
            pl.BlockSpec((width // LANES, 2 * PLANES, ROWS, LANES), lambda i: (i, 0, 0, 0)),
            pl.BlockSpec((edge, width), lambda i: (0, i)),
            pl.BlockSpec((edge, width), lambda i: (0, i)),
        ],
        out_shape=[
            shape(BLOCKS, 2 * PLANES, ROWS, LANES),
            shape(edge, COLS),
            shape(edge, COLS),
        ],
        compiler_params=params(60),
        name="first_sums",
    )(first, noise, ids, solute)


def factors(sums_ref, solute_ref, base_ref, slope_ref):
    for plane in range(PLANES):
        for block in range(BLOCKS):
            columns = column_block(block)
            cross = 2.0 * cross_gamma - 4.0 * solute_beta * solute_ref[plane, :, columns]
            base_ref[plane, :, columns] = (
                coef_quad - 6.0 * gradient_kappa - sums_ref[block, plane] * cross
            )
            slope_ref[plane, :, columns] = cross - coef_quart


def stepped(planes, above, below, rate, base_ref, slope_ref):
    rows = lax.broadcasted_iota(jnp.int32, (ROWS, COLS), 0)
    out = []
    for plane, across in zip(range(PLANES), beside(planes)):
        eta = planes[plane]
        up = jnp.where(rows == 0, above[plane], pltpu.roll(eta, 1, 0))
        down = jnp.where(rows == ROWS - 1, below[plane], pltpu.roll(eta, ROWS - 1, 0))
        around = up + down + along_columns(eta) + across
        bracket = base_ref[plane] + slope_ref[plane] * (eta * eta)
        out.append(eta + rate * (eta * bracket + gradient_kappa * around))
    return out


def halo_rows(ref, grain):
    return [ref[pl.ds(grain * PLANES + plane, 1), :] for plane in range(PLANES)]


def first_step(
    first_ref, group_ref, mobility_ref, noise_ref, ids_ref, solute_ref, sums_ref, above_ref, below_ref,
    eta_ref, next_sums_ref, next_ref, prev_ref, bulk_ref, rows_above_ref, rows_below_ref, base_ref, slope_ref,
):
    grain = pl.program_id(0)

    @pl.when(grain == 0)
    def _():
        factors(sums_ref, solute_ref, base_ref, slope_ref)
        for plane in range(PLANES):
            row = GRAINS * PLANES + 2 * plane
            for block in range(BLOCKS):
                columns = column_block(block)
                bulk = sums_ref[block, PLANES + plane]
                bulk_ref[plane, :, columns] = bulk
                prev_ref[row : row + 2, columns] = bulk[:2]
                next_ref[row : row + 2, columns] = bulk[ROWS - 2 :]
        rows_above_ref[...] = above_ref[GRAINS * PLANES :]
        rows_below_ref[...] = below_ref[GRAINS * PLANES :]

    rate = time_step * mobility_ref[group_ref[grain]]
    planes = [
        jnp.where(ids_ref[plane] == first_ref[0] + grain, 0.9, 0.0).astype(F32) + noise_ref[0, plane]
        for plane in range(PLANES)
    ]
    out = stepped(planes, halo_rows(above_ref, grain), halo_rows(below_ref, grain), rate, base_ref, slope_ref)
    for plane in range(PLANES):
        eta = out[plane]
        eta_ref[0, plane] = eta
        row = pl.ds(grain * PLANES + plane, 1)
        prev_ref[row, :] = eta[:1]
        next_ref[row, :] = eta[ROWS - 1 :]
    for plane in range(PLANES):
        square = out[plane] * out[plane]
        fourth = square * square

        @pl.when(grain == 0)
        def _():
            for block in range(BLOCKS):
                next_sums_ref[block, plane] = square[:, column_block(block)]
                next_sums_ref[block, PLANES + plane] = fourth[:, column_block(block)]

        @pl.when(grain != 0)
        def _():
            for block in range(BLOCKS):
                next_sums_ref[block, plane] += square[:, column_block(block)]
                next_sums_ref[block, PLANES + plane] += fourth[:, column_block(block)]


def call_first_step(first, groups, mobility, noise, ids, solute, sums, above, below):
    edge = GRAINS * PLANES + 2 * PLANES
    grain_block = pl.BlockSpec((1, PLANES, ROWS, COLS), lambda i: (i, 0, 0, 0))
    return pl.pallas_call(
        first_step,
        grid=(GRAINS,),
        in_specs=[
            smem(), smem(), smem(), grain_block,
            whole(*ids.shape), whole(*solute.shape), whole(*sums.shape),
            whole(*above.shape), whole(*below.shape),
        ],
        out_specs=[grain_block, whole(*sums.shape)]
        + [whole(edge, COLS)] * 2
        + [whole(*solute.shape)]
        + [whole(3 * PLANES, COLS)] * 2,
        out_shape=[hbm(*noise.shape), shape(*sums.shape)]
        + [shape(edge, COLS)] * 2
        + [hbm(*solute.shape)]
        + [hbm(3 * PLANES, COLS)] * 2,
        scratch_shapes=[pltpu.VMEM(solute.shape, F32)] * 2,
        compiler_params=params(),
        name="first_step",
    )(first, groups, mobility, noise, ids, solute, sums, above, below)


PAD = 8
DEEP = ROWS + 2 * PAD


def laplace(planes):
    height = planes[0].shape[0]
    return [
        pltpu.roll(value, 1, 0) + pltpu.roll(value, height - 1, 0) + along_columns(value) + across - 6.0 * value
        for value, across in zip(planes, beside(planes))
    ]


def solute_step(
    solute_ref, middle_ref, above_ref, below_ref, mid_above_ref, mid_below_ref,
    out_ref, part_ref, ends_ref, deep_ref, bulk_ref,
):
    for plane in range(PLANES):
        for ref in (deep_ref, bulk_ref):
            ref[plane, :PAD] = jnp.zeros((PAD, COLS), F32)
            ref[plane, PAD + ROWS :] = jnp.zeros((PAD, COLS), F32)
        row = 3 * plane
        deep_ref[plane, PAD - 3 : PAD] = above_ref[row : row + 3, :]
        deep_ref[plane, PAD : PAD + ROWS] = solute_ref[plane]
        deep_ref[plane, PAD + ROWS : PAD + ROWS + 3] = below_ref[row : row + 3, :]
        row = GRAINS * PLANES + 2 * plane
        bulk_ref[plane, PAD - 2 : PAD] = mid_above_ref[row : row + 2, :]
        bulk_ref[plane, PAD + ROWS : PAD + ROWS + 2] = mid_below_ref[row : row + 2, :]
        bulk_ref[plane, PAD : PAD + ROWS] = middle_ref[plane]
    solute = [deep_ref[plane] for plane in range(PLANES)]
    potential = [
        2.0 * bulk_stiff * (solute[plane] - solute_mean) - bulk_ref[plane] - solute_kappa * lap
        for plane, lap in enumerate(laplace(solute))
    ]
    moved = [
        solute[plane] + time_step * solute_mobility * lap for plane, lap in enumerate(laplace(potential))
    ]
    for plane, lap in enumerate(laplace(moved)):
        part = 2.0 * bulk_stiff * (moved[plane] - solute_mean) - solute_kappa * lap
        out_ref[plane] = moved[plane][PAD : PAD + ROWS]
        part_ref[plane] = part[PAD : PAD + ROWS]
        ends_ref[plane : plane + 1, :] = part[PAD : PAD + 1]
        ends_ref[PLANES + plane : PLANES + plane + 1, :] = part[PAD + ROWS - 1 : PAD + ROWS]


def call_solute_step(solute, bulk, above, below, mid_above, mid_below):
    return pl.pallas_call(
        solute_step,
        out_shape=[shape(*solute.shape)] * 2 + [hbm(2 * PLANES, COLS)],
        scratch_shapes=[pltpu.VMEM((PLANES, DEEP, COLS), F32)] * 2,
        compiler_params=params(),
        name="solute_step",
    )(solute, bulk, above, below, mid_above, mid_below)


def end_rows(core_ref, ends_ref, sums_ref, inner_ref, outer_ref):
    for plane in range(PLANES):
        row = slice(plane, plane + 1)
        for block in range(BLOCKS):
            columns = column_block(block)
            bulk = sums_ref[block, PLANES + plane]
            top = ends_ref[plane : plane + 1, columns] - bulk[:1]
            bottom = ends_ref[PLANES + plane : PLANES + plane + 1, columns] - bulk[ROWS - 1 :]
            inner_ref[row, columns] = jnp.where(core_ref[0] == 0, bottom, top)
            outer_ref[row, columns] = jnp.where(core_ref[0] == 0, top, bottom)


def call_end_rows(core, ends, sums):
    return pl.pallas_call(
        end_rows,
        in_specs=[smem(), whole(*ends.shape), whole(*sums.shape)],
        out_shape=[shape(PLANES, COLS)] * 2,
        compiler_params=params(),
        name="end_rows",
    )(core, *from_hbm(ends), sums)


def second_step(
    group_ref, mobility_ref, old_ref, solute_ref, sums_ref, above_ref, below_ref, eta_ref, base_ref, slope_ref
):
    grain = pl.program_id(0)

    @pl.when(grain == 0)
    def _():
        factors(sums_ref, solute_ref, base_ref, slope_ref)

    rate = time_step * mobility_ref[group_ref[grain]]
    planes = [old_ref[0, plane] for plane in range(PLANES)]
    out = stepped(planes, halo_rows(above_ref, grain), halo_rows(below_ref, grain), rate, base_ref, slope_ref)
    for plane in range(PLANES):
        eta_ref[0, plane] = out[plane]


def call_second_step(groups, mobility, eta, solute, sums, above, below):
    grain_block = pl.BlockSpec((1, PLANES, ROWS, COLS), lambda i: (i, 0, 0, 0))
    return pl.pallas_call(
        second_step,
        grid=(GRAINS,),
        in_specs=[
            smem(), smem(), grain_block, whole(*solute.shape), whole(*sums.shape),
            whole(*above.shape), whole(*below.shape),
        ],
        out_specs=grain_block,
        out_shape=shape(*eta.shape),
        scratch_shapes=[pltpu.VMEM(solute.shape, F32)] * 2,
        compiler_params=params(),
        cost_estimate=pl.CostEstimate(flops=20_000_000, bytes_accessed=10_000_000, transcendentals=0),
        name="second_step",
    )(groups, mobility, eta, solute, sums, above, below)


def solute_end(core_ref, solute_ref, part_ref, sums_ref, inner_ref, outer_ref, out_ref, potential_ref):
    rows = lax.broadcasted_iota(jnp.int32, (ROWS, COLS), 0)
    first_core = core_ref[0] == 0
    for plane in range(PLANES):
        for block in range(BLOCKS):
            columns = column_block(block)
            potential_ref[plane, :, columns] = part_ref[plane, :, columns] - sums_ref[block, PLANES + plane]
    planes = [potential_ref[plane] for plane in range(PLANES)]
    for plane, across in enumerate(beside(planes)):
        value = planes[plane]
        inner, outer = inner_ref[plane : plane + 1, :], outer_ref[plane : plane + 1, :]
        above, below = jnp.where(first_core, outer, inner), jnp.where(first_core, inner, outer)
        up = jnp.where(rows == 0, above, pltpu.roll(value, 1, 0))
        down = jnp.where(rows == ROWS - 1, below, pltpu.roll(value, ROWS - 1, 0))
        lap = up + down + along_columns(value) + across - 6.0 * value
        out_ref[plane] = solute_ref[plane] + time_step * solute_mobility * lap


def call_solute_end(core, solute, part, sums, inner, outer):
    return pl.pallas_call(
        solute_end,
        in_specs=[smem()] + [whole(*array.shape) for array in (solute, part, sums, inner, outer)],
        out_shape=shape(*solute.shape),
        scratch_shapes=[pltpu.VMEM(solute.shape, F32)],
        compiler_params=params(),
        name="solute_end",
    )(core, solute, part, sums, inner, outer)


def swapped(inner, outer, count):
    outer = lax.ppermute(outer, SPACE, [(i, (i + 2 * (i % 2) - 1) % count) for i in range(count)])
    inner = lax.ppermute(inner, SPACE, [(i, i ^ 1) for i in range(count)])
    return inner, outer


def exchange(to_next, to_prev, count):
    above = lax.ppermute(to_next, SPACE, [(i, (i + 1) % count) for i in range(count)])
    below = lax.ppermute(to_prev, SPACE, [((i + 1) % count, i) for i in range(count)])
    return above, below


def added(parts_ref, index):
    values = [parts_ref[(part,) + index] for part in range(parts_ref.shape[0])]
    while len(values) > 1:
        values = [left + right for left, right in zip(values[::2], values[1::2])]
    return values[0]


def add_parts(parts_ref, out_ref):
    for block in range(out_ref.shape[0]):
        for row in range(out_ref.shape[1]):
            out_ref[block, row] = added(parts_ref, (block, row))


def call_add_parts(parts):
    return pl.pallas_call(
        add_parts, out_shape=shape(*parts.shape[1:]), compiler_params=params(), name="add_parts"
    )(parts)


def owner(parts_ref, copies_ref):
    for plane in range(PLANES):
        two, four = added(parts_ref, (plane,)), added(parts_ref, (PLANES + plane,))
        bulk = solute_beta * (two * two - four)
        for copy in range(copies_ref.shape[0]):
            copies_ref[copy, plane] = two
            copies_ref[copy, PLANES + plane] = bulk


def call_owner(parts):
    return pl.pallas_call(
        owner, out_shape=shape(*parts.shape), compiler_params=params(), name="owner"
    )(parts)


def copies(value_ref, out_ref):
    for copy in range(out_ref.shape[0]):
        out_ref[copy] = value_ref[...]


def call_copies(value, count):
    return pl.pallas_call(
        copies, out_shape=shape(count, *value.shape), compiler_params=params(), name="copies"
    )(value)


def dealt(blocks, axis):
    return lax.all_to_all(blocks, axis, 0, 0, tiled=True)


def total(sums, to_next, to_prev):
    count = lax.axis_size("yl") * lax.axis_size("z") * lax.axis_size("core")
    along = lax.axis_size("x")
    parts = dealt(sums.reshape((along, BLOCKS // along) + sums.shape[1:]), "x")
    parts, above, below = lax.optimization_barrier((parts, *exchange(to_next, to_prev, count)))
    parts = dealt(call_add_parts(parts), "yh")
    parts = dealt(call_owner(parts), "yh")
    return dealt(call_copies(parts, along), "x").reshape(sums.shape), above, below


def shards(grain_ids, group_of, group_mobility, seed_noise, concentration):
    count = lax.axis_size("yl") * lax.axis_size("z") * lax.axis_size("core")
    first = (lax.axis_index(GRAIN) * GRAINS).astype(jnp.int32).reshape(1)
    sums, to_next, to_prev = call_first_sums(first, seed_noise, grain_ids, concentration)
    sums, above, below = total(sums, to_next, to_prev)
    eta, sums, to_next, to_prev, bulk, rows_above, rows_below = call_first_step(
        first, group_of, group_mobility, seed_noise, grain_ids, concentration, sums, above, below
    )
    sums, mid_above, mid_below = total(sums, to_next, to_prev)
    solute, part, ends = call_solute_step(concentration, bulk, rows_above, rows_below, mid_above, mid_below)
    core = lax.axis_index("core").astype(jnp.int32).reshape(1)
    inner, outer = swapped(*call_end_rows(core, ends, sums), count)
    eta = call_second_step(group_of, group_mobility, eta, solute, sums, mid_above, mid_below)
    solute = call_solute_end(core, solute, part, sums, inner, outer)
    return eta, solute


def solution(mesh):
    fine = Mesh(mesh.devices.reshape(2, 8, 2, 4, 4), SPACE + GRAIN)
    placed = (
        P(None, SPACE, None),
        P(GRAIN),
        P(),
        P(GRAIN, None, SPACE, None),
        P(None, SPACE, None),
    )
    return jax.shard_map(
        shards,
        mesh=fine,
        in_specs=placed,
        out_specs=(P(GRAIN, None, SPACE, None), P(None, SPACE, None)),
        check_vma=False,
    )
```

```python
import jax
import jax.numpy as jnp
from jax import lax
from jax.experimental import pallas as pl
from jax.experimental.pallas import tpu as pltpu
from jax.sharding import Mesh, PartitionSpec as P

GRAINS, PLANES, ROWS, COLS, LANES = 6, 3, 16, 2048, 128
BLOCKS = COLS // LANES
SPACE = ("yl", "z", "core")
GRAIN = ("x", "yh")

coef_quad = 1.0
coef_quart = 1.0
cross_gamma = 1.5
gradient_kappa = 0.5
solute_beta = 0.6
bulk_stiff = 1.0
solute_mean = 0.4
solute_kappa = 0.25
solute_mobility = 0.3
time_step = 0.1

F32 = jnp.float32
MIB = 1024 * 1024


def shape(*dims):
    return jax.ShapeDtypeStruct(dims, F32)


def hbm(*dims):
    return pltpu.HBM(dims, F32)


def from_hbm(*arrays):
    return [pltpu.with_memory_space_constraint(array, pltpu.HBM) for array in arrays]


def params(mib=16):
    return pltpu.CompilerParams(vmem_limit_bytes=mib * MIB)


def whole(*dims):
    return pl.BlockSpec(dims, lambda *_: (0,) * len(dims))


def smem():
    return pl.BlockSpec(memory_space=pltpu.SMEM)


def along_columns(value):
    return pltpu.roll(value, 1, 1) + pltpu.roll(value, COLS - 1, 1)


def beside(planes):
    return (planes[0] + planes[1], planes[0] + planes[2], planes[1] + planes[2])


def column_block(block):
    return slice(block * LANES, (block + 1) * LANES)


def first_sums(first_ref, noise_ref, ids_ref, solute_ref, sums_ref, next_ref, prev_ref):
    for plane in range(PLANES):
        ids = ids_ref[plane]
        two = four = None
        for grain in range(GRAINS):
            seed = jnp.where(ids == first_ref[0] + grain, 0.9, 0.0).astype(F32)
            eta = seed + noise_ref[grain, plane]
            row = grain * PLANES + plane
            prev_ref[row : row + 1, :] = eta[:1]
            next_ref[row : row + 1, :] = eta[ROWS - 1 :]
            square = eta * eta
            two = square if two is None else two + square
            four = square * square if four is None else four + square * square
        for block in range(sums_ref.shape[0]):
            sums_ref[block, plane] = two[:, column_block(block)]
            sums_ref[block, PLANES + plane] = four[:, column_block(block)]
        row = GRAINS * PLANES + 3 * plane
        prev_ref[row : row + 3, :] = solute_ref[plane, :3]
        next_ref[row : row + 3, :] = solute_ref[plane, ROWS - 3 :]


def call_first_sums(first, noise, ids, solute):
    width = 512
    edge = GRAINS * PLANES + 3 * PLANES
    return pl.pallas_call(
        first_sums,
        grid=(COLS // width,),
        in_specs=[
            smem(),
            pl.BlockSpec((GRAINS, PLANES, ROWS, width), lambda i: (0, 0, 0, i)),
            pl.BlockSpec((PLANES, ROWS, width), lambda i: (0, 0, i)),
            pl.BlockSpec((PLANES, ROWS, width), lambda i: (0, 0, i)),
        ],
        out_specs=[
            pl.BlockSpec((width // LANES, 2 * PLANES, ROWS, LANES), lambda i: (i, 0, 0, 0)),
            pl.BlockSpec((edge, width), lambda i: (0, i)),
            pl.BlockSpec((edge, width), lambda i: (0, i)),
        ],
        out_shape=[
            shape(BLOCKS, 2 * PLANES, ROWS, LANES),
            shape(edge, COLS),
            shape(edge, COLS),
        ],
        compiler_params=params(60),
        name="first_sums",
    )(first, noise, ids, solute)


def factors(sums_ref, solute_ref, base_ref, slope_ref):
    for plane in range(PLANES):
        for block in range(BLOCKS):
            columns = column_block(block)
            cross = 2.0 * cross_gamma - 4.0 * solute_beta * solute_ref[plane, :, columns]
            base_ref[plane, :, columns] = (
                coef_quad - 6.0 * gradient_kappa - sums_ref[block, plane] * cross
            )
            slope_ref[plane, :, columns] = cross - coef_quart


def stepped(planes, above, below, rate, base_ref, slope_ref):
    rows = lax.broadcasted_iota(jnp.int32, (ROWS, COLS), 0)
    out = []
    for plane, across in zip(range(PLANES), beside(planes)):
        eta = planes[plane]
        up = jnp.where(rows == 0, above[plane], pltpu.roll(eta, 1, 0))
        down = jnp.where(rows == ROWS - 1, below[plane], pltpu.roll(eta, ROWS - 1, 0))
        around = up + down + along_columns(eta) + across
        bracket = base_ref[plane] + slope_ref[plane] * (eta * eta)
        out.append(eta + rate * (eta * bracket + gradient_kappa * around))
    return out


def halo_rows(ref, grain):
    return [ref[pl.ds(grain * PLANES + plane, 1), :] for plane in range(PLANES)]


def first_step(
    first_ref, group_ref, mobility_ref, noise_ref, ids_ref, solute_ref, sums_ref, above_ref, below_ref,
    eta_ref, next_sums_ref, next_ref, prev_ref, bulk_ref, base_ref, slope_ref,
):
    grain = pl.program_id(0)

    @pl.when(grain == 0)
    def _():
        factors(sums_ref, solute_ref, base_ref, slope_ref)
        for plane in range(PLANES):
            row = GRAINS * PLANES + 2 * plane
            for block in range(BLOCKS):
                columns = column_block(block)
                bulk = sums_ref[block, PLANES + plane]
                bulk_ref[plane, :, columns] = bulk
                prev_ref[row : row + 2, columns] = bulk[:2]
                next_ref[row : row + 2, columns] = bulk[ROWS - 2 :]

    rate = time_step * mobility_ref[group_ref[grain]]
    planes = [
        jnp.where(ids_ref[plane] == first_ref[0] + grain, 0.9, 0.0).astype(F32) + noise_ref[0, plane]
        for plane in range(PLANES)
    ]
    out = stepped(planes, halo_rows(above_ref, grain), halo_rows(below_ref, grain), rate, base_ref, slope_ref)
    for plane in range(PLANES):
        eta = out[plane]
        eta_ref[0, plane] = eta
        row = pl.ds(grain * PLANES + plane, 1)
        prev_ref[row, :] = eta[:1]
        next_ref[row, :] = eta[ROWS - 1 :]
    for plane in range(PLANES):
        square = out[plane] * out[plane]
        fourth = square * square

        @pl.when(grain == 0)
        def _():
            for block in range(BLOCKS):
                next_sums_ref[block, plane] = square[:, column_block(block)]
                next_sums_ref[block, PLANES + plane] = fourth[:, column_block(block)]

        @pl.when(grain != 0)
        def _():
            for block in range(BLOCKS):
                next_sums_ref[block, plane] += square[:, column_block(block)]
                next_sums_ref[block, PLANES + plane] += fourth[:, column_block(block)]


def call_first_step(first, groups, mobility, noise, ids, solute, sums, above, below):
    edge = GRAINS * PLANES + 2 * PLANES
    grain_block = pl.BlockSpec((1, PLANES, ROWS, COLS), lambda i: (i, 0, 0, 0))
    return pl.pallas_call(
        first_step,
        grid=(GRAINS,),
        in_specs=[
            smem(), smem(), smem(), grain_block,
            whole(*ids.shape), whole(*solute.shape), whole(*sums.shape),
            whole(*above.shape), whole(*below.shape),
        ],
        out_specs=[grain_block, whole(*sums.shape)]
        + [whole(edge, COLS)] * 2
        + [whole(*solute.shape)],
        out_shape=[hbm(*noise.shape), shape(*sums.shape)]
        + [shape(edge, COLS)] * 2
        + [hbm(*solute.shape)],
        scratch_shapes=[pltpu.VMEM(solute.shape, F32)] * 2,
        compiler_params=params(),
        name="first_step",
    )(first, groups, mobility, noise, *from_hbm(ids), solute, sums, *from_hbm(above, below))


PAD = 8
DEEP = ROWS + 2 * PAD


def laplace(planes):
    height = planes[0].shape[0]
    return [
        pltpu.roll(value, 1, 0) + pltpu.roll(value, height - 1, 0) + along_columns(value) + across - 6.0 * value
        for value, across in zip(planes, beside(planes))
    ]


def solute_step(
    solute_ref, middle_ref, above_ref, below_ref, mid_above_ref, mid_below_ref,
    out_ref, part_ref, deep_ref, bulk_ref,
):
    for plane in range(PLANES):
        for ref in (deep_ref, bulk_ref):
            ref[plane, :PAD] = jnp.zeros((PAD, COLS), F32)
            ref[plane, PAD + ROWS :] = jnp.zeros((PAD, COLS), F32)
        row = GRAINS * PLANES + 3 * plane
        deep_ref[plane, PAD - 3 : PAD] = above_ref[row : row + 3, :]
        deep_ref[plane, PAD : PAD + ROWS] = solute_ref[plane]
        deep_ref[plane, PAD + ROWS : PAD + ROWS + 3] = below_ref[row : row + 3, :]
        row = GRAINS * PLANES + 2 * plane
        bulk_ref[plane, PAD - 2 : PAD] = mid_above_ref[row : row + 2, :]
        bulk_ref[plane, PAD + ROWS : PAD + ROWS + 2] = mid_below_ref[row : row + 2, :]
        bulk_ref[plane, PAD : PAD + ROWS] = middle_ref[plane]
    solute = [deep_ref[plane] for plane in range(PLANES)]
    potential = [
        2.0 * bulk_stiff * (solute[plane] - solute_mean) - bulk_ref[plane] - solute_kappa * lap
        for plane, lap in enumerate(laplace(solute))
    ]
    moved = [
        solute[plane] + time_step * solute_mobility * lap for plane, lap in enumerate(laplace(potential))
    ]
    for plane, lap in enumerate(laplace(moved)):
        part = 2.0 * bulk_stiff * (moved[plane] - solute_mean) - solute_kappa * lap
        out_ref[plane] = moved[plane][PAD : PAD + ROWS]
        part_ref[plane] = part[PAD : PAD + ROWS]


def call_solute_step(solute, bulk, above, below, mid_above, mid_below):
    return pl.pallas_call(
        solute_step,
        out_shape=[shape(*solute.shape)] * 2,
        scratch_shapes=[pltpu.VMEM((PLANES, DEEP, COLS), F32)] * 2,
        compiler_params=params(),
        name="solute_step",
    )(*from_hbm(solute, bulk, above, below, mid_above, mid_below))


def second_potential(part_ref, sums_ref, out_ref, next_ref, prev_ref):
    for plane in range(PLANES):
        for block in range(BLOCKS):
            columns = column_block(block)
            potential = part_ref[plane, :, columns] - sums_ref[block, PLANES + plane]
            out_ref[plane, :, columns] = potential
            prev_ref[plane : plane + 1, columns] = potential[:1]
            next_ref[plane : plane + 1, columns] = potential[ROWS - 1 :]


def call_second_potential(part, sums):
    return pl.pallas_call(
        second_potential,
        out_shape=[shape(*part.shape), shape(PLANES, COLS), shape(PLANES, COLS)],
        compiler_params=params(),
        name="second_potential",
    )(part, sums)


def second_step(
    group_ref, mobility_ref, old_ref, solute_ref, sums_ref, above_ref, below_ref, eta_ref, base_ref, slope_ref
):
    grain = pl.program_id(0)

    @pl.when(grain == 0)
    def _():
        factors(sums_ref, solute_ref, base_ref, slope_ref)

    rate = time_step * mobility_ref[group_ref[grain]]
    planes = [old_ref[0, plane] for plane in range(PLANES)]
    out = stepped(planes, halo_rows(above_ref, grain), halo_rows(below_ref, grain), rate, base_ref, slope_ref)
    for plane in range(PLANES):
        eta_ref[0, plane] = out[plane]


def call_second_step(groups, mobility, eta, solute, sums, above, below):
    grain_block = pl.BlockSpec((1, PLANES, ROWS, COLS), lambda i: (i, 0, 0, 0))
    return pl.pallas_call(
        second_step,
        grid=(GRAINS,),
        in_specs=[
            smem(), smem(), grain_block, whole(*solute.shape), whole(*sums.shape),
            whole(*above.shape), whole(*below.shape),
        ],
        out_specs=grain_block,
        out_shape=shape(*eta.shape),
        scratch_shapes=[pltpu.VMEM(solute.shape, F32)] * 2,
        compiler_params=params(),
        cost_estimate=pl.CostEstimate(flops=20_000_000, bytes_accessed=10_000_000, transcendentals=0),
        name="second_step",
    )(groups, mobility, eta, solute, sums, *from_hbm(above, below))


def solute_end(solute_ref, potential_ref, above_ref, below_ref, out_ref):
    rows = lax.broadcasted_iota(jnp.int32, (ROWS, COLS), 0)
    planes = [potential_ref[plane] for plane in range(PLANES)]
    for plane, across in enumerate(beside(planes)):
        value = planes[plane]
        up = jnp.where(rows == 0, above_ref[plane : plane + 1, :], pltpu.roll(value, 1, 0))
        down = jnp.where(rows == ROWS - 1, below_ref[plane : plane + 1, :], pltpu.roll(value, ROWS - 1, 0))
        lap = up + down + along_columns(value) + across - 6.0 * value
        out_ref[plane] = solute_ref[plane] + time_step * solute_mobility * lap


def call_solute_end(solute, potential, above, below):
    return pl.pallas_call(
        solute_end,
        out_shape=shape(*solute.shape),
        compiler_params=params(),
        name="solute_end",
    )(solute, potential, above, below)


def exchange(to_next, to_prev, count):
    above = lax.ppermute(to_next, SPACE, [(i, (i + 1) % count) for i in range(count)])
    below = lax.ppermute(to_prev, SPACE, [((i + 1) % count, i) for i in range(count)])
    return above, below


def added(parts_ref, index):
    values = [parts_ref[(part,) + index] for part in range(parts_ref.shape[0])]
    while len(values) > 1:
        values = [left + right for left, right in zip(values[::2], values[1::2])]
    return values[0]


def add_parts(parts_ref, out_ref):
    for block in range(out_ref.shape[0]):
        for row in range(out_ref.shape[1]):
            out_ref[block, row] = added(parts_ref, (block, row))


def call_add_parts(parts):
    return pl.pallas_call(
        add_parts, out_shape=shape(*parts.shape[1:]), compiler_params=params(), name="add_parts"
    )(parts)


def owner(parts_ref, copies_ref):
    for plane in range(PLANES):
        two, four = added(parts_ref, (plane,)), added(parts_ref, (PLANES + plane,))
        bulk = solute_beta * (two * two - four)
        for copy in range(copies_ref.shape[0]):
            copies_ref[copy, plane] = two
            copies_ref[copy, PLANES + plane] = bulk


def call_owner(parts):
    return pl.pallas_call(
        owner, out_shape=shape(*parts.shape), compiler_params=params(), name="owner"
    )(parts)


def copies(value_ref, out_ref):
    for copy in range(out_ref.shape[0]):
        out_ref[copy] = value_ref[...]


def call_copies(value, count):
    return pl.pallas_call(
        copies, out_shape=shape(count, *value.shape), compiler_params=params(), name="copies"
    )(value)


def dealt(blocks, axis):
    return lax.all_to_all(blocks, axis, 0, 0, tiled=True)


def total(sums):
    along = lax.axis_size("x")
    parts = dealt(sums.reshape((along, BLOCKS // along) + sums.shape[1:]), "x")
    parts = dealt(call_add_parts(parts), "yh")
    parts = dealt(call_owner(parts), "yh")
    return dealt(call_copies(parts, along), "x").reshape(sums.shape)


def shards(grain_ids, group_of, group_mobility, seed_noise, concentration):
    count = lax.axis_size("yl") * lax.axis_size("z") * lax.axis_size("core")
    first = (lax.axis_index(GRAIN) * GRAINS).astype(jnp.int32).reshape(1)
    sums, to_next, to_prev = call_first_sums(first, seed_noise, grain_ids, concentration)
    above, below = exchange(to_next, to_prev, count)
    eta, sums, to_next, to_prev, bulk = call_first_step(
        first, group_of, group_mobility, seed_noise, grain_ids, concentration, total(sums), above, below
    )
    mid_above, mid_below = exchange(to_next, to_prev, count)
    sums = total(sums)
    solute, part = call_solute_step(concentration, bulk, above, below, mid_above, mid_below)
    potential, to_next, to_prev = call_second_potential(part, sums)
    end_above, end_below = exchange(to_next, to_prev, count)
    eta = call_second_step(group_of, group_mobility, eta, solute, sums, mid_above, mid_below)
    solute = call_solute_end(solute, potential, end_above, end_below)
    return eta, solute


def solution(mesh):
    fine = Mesh(mesh.devices.reshape(2, 8, 2, 4, 4), SPACE + GRAIN)
    placed = (
        P(None, SPACE, None),
        P(GRAIN),
        P(),
        P(GRAIN, None, SPACE, None),
        P(None, SPACE, None),
    )
    return jax.shard_map(
        shards,
        mesh=fine,
        in_specs=placed,
        out_specs=(P(GRAIN, None, SPACE, None), P(None, SPACE, None)),
        check_vma=False,
    )
```

```python
import jax
import jax.numpy as jnp
from jax import lax
from jax.experimental import pallas as pl
from jax.experimental.pallas import tpu as pltpu
from jax.sharding import Mesh, PartitionSpec as P

GRAINS, PLANES, ROWS, COLS, LANES = 6, 3, 16, 2048, 128
BLOCKS = COLS // LANES
SPACE = ("yl", "z", "core")
GRAIN = ("x", "yh")

coef_quad = 1.0
coef_quart = 1.0
cross_gamma = 1.5
gradient_kappa = 0.5
solute_beta = 0.6
bulk_stiff = 1.0
solute_mean = 0.4
solute_kappa = 0.25
solute_mobility = 0.3
time_step = 0.1

F32 = jnp.float32
MIB = 1024 * 1024


def shape(*dims):
    return jax.ShapeDtypeStruct(dims, F32)


def hbm(*dims):
    return pltpu.HBM(dims, F32)


def from_hbm(*arrays):
    return [pltpu.with_memory_space_constraint(array, pltpu.HBM) for array in arrays]


def params(mib=16):
    return pltpu.CompilerParams(vmem_limit_bytes=mib * MIB)


def whole(*dims):
    return pl.BlockSpec(dims, lambda *_: (0,) * len(dims))


def smem():
    return pl.BlockSpec(memory_space=pltpu.SMEM)


def along_columns(value):
    return pltpu.roll(value, 1, 1) + pltpu.roll(value, COLS - 1, 1)


def beside(planes):
    return (planes[0] + planes[1], planes[0] + planes[2], planes[1] + planes[2])


def column_block(block):
    return slice(block * LANES, (block + 1) * LANES)


def first_sums(first_ref, noise_ref, ids_ref, solute_ref, sums_ref, next_ref, prev_ref):
    for plane in range(PLANES):
        ids = ids_ref[plane]
        two = four = None
        for grain in range(GRAINS):
            seed = jnp.where(ids == first_ref[0] + grain, 0.9, 0.0).astype(F32)
            eta = seed + noise_ref[grain, plane]
            row = grain * PLANES + plane
            prev_ref[row : row + 1, :] = eta[:1]
            next_ref[row : row + 1, :] = eta[ROWS - 1 :]
            square = eta * eta
            two = square if two is None else two + square
            four = square * square if four is None else four + square * square
        for block in range(sums_ref.shape[0]):
            sums_ref[block, plane] = two[:, column_block(block)]
            sums_ref[block, PLANES + plane] = four[:, column_block(block)]
        row = GRAINS * PLANES + 3 * plane
        prev_ref[row : row + 3, :] = solute_ref[plane, :3]
        next_ref[row : row + 3, :] = solute_ref[plane, ROWS - 3 :]


def call_first_sums(first, noise, ids, solute):
    width = 512
    edge = GRAINS * PLANES + 3 * PLANES
    return pl.pallas_call(
        first_sums,
        grid=(COLS // width,),
        in_specs=[
            smem(),
            pl.BlockSpec((GRAINS, PLANES, ROWS, width), lambda i: (0, 0, 0, i)),
            pl.BlockSpec((PLANES, ROWS, width), lambda i: (0, 0, i)),
            pl.BlockSpec((PLANES, ROWS, width), lambda i: (0, 0, i)),
        ],
        out_specs=[
            pl.BlockSpec((width // LANES, 2 * PLANES, ROWS, LANES), lambda i: (i, 0, 0, 0)),
            pl.BlockSpec((edge, width), lambda i: (0, i)),
            pl.BlockSpec((edge, width), lambda i: (0, i)),
        ],
        out_shape=[
            shape(BLOCKS, 2 * PLANES, ROWS, LANES),
            shape(edge, COLS),
            shape(edge, COLS),
        ],
        compiler_params=params(60),
        name="first_sums",
    )(first, noise, ids, solute)


def factors(sums_ref, solute_ref, base_ref, slope_ref):
    for plane in range(PLANES):
        for block in range(BLOCKS):
            columns = column_block(block)
            cross = 2.0 * cross_gamma - 4.0 * solute_beta * solute_ref[plane, :, columns]
            base_ref[plane, :, columns] = (
                coef_quad - 6.0 * gradient_kappa - sums_ref[block, plane] * cross
            )
            slope_ref[plane, :, columns] = cross - coef_quart


def stepped(planes, above, below, rate, base_ref, slope_ref):
    rows = lax.broadcasted_iota(jnp.int32, (ROWS, COLS), 0)
    out = []
    for plane, across in zip(range(PLANES), beside(planes)):
        eta = planes[plane]
        up = jnp.where(rows == 0, above[plane], pltpu.roll(eta, 1, 0))
        down = jnp.where(rows == ROWS - 1, below[plane], pltpu.roll(eta, ROWS - 1, 0))
        around = up + down + along_columns(eta) + across
        bracket = base_ref[plane] + slope_ref[plane] * (eta * eta)
        out.append(eta + rate * (eta * bracket + gradient_kappa * around))
    return out


def halo_rows(ref, grain):
    return [ref[pl.ds(grain * PLANES + plane, 1), :] for plane in range(PLANES)]


def first_step(
    first_ref, group_ref, mobility_ref, noise_ref, ids_ref, solute_ref, sums_ref, above_ref, below_ref,
    eta_ref, next_sums_ref, next_ref, prev_ref, bulk_ref, rows_above_ref, rows_below_ref, base_ref, slope_ref,
):
    grain = pl.program_id(0)

    @pl.when(grain == 0)
    def _():
        factors(sums_ref, solute_ref, base_ref, slope_ref)
        for plane in range(PLANES):
            row = GRAINS * PLANES + 2 * plane
            for block in range(BLOCKS):
                columns = column_block(block)
                bulk = sums_ref[block, PLANES + plane]
                bulk_ref[plane, :, columns] = bulk
                prev_ref[row : row + 2, columns] = bulk[:2]
                next_ref[row : row + 2, columns] = bulk[ROWS - 2 :]
        rows_above_ref[...] = above_ref[GRAINS * PLANES :]
        rows_below_ref[...] = below_ref[GRAINS * PLANES :]

    rate = time_step * mobility_ref[group_ref[grain]]
    planes = [
        jnp.where(ids_ref[plane] == first_ref[0] + grain, 0.9, 0.0).astype(F32) + noise_ref[0, plane]
        for plane in range(PLANES)
    ]
    out = stepped(planes, halo_rows(above_ref, grain), halo_rows(below_ref, grain), rate, base_ref, slope_ref)
    for plane in range(PLANES):
        eta = out[plane]
        eta_ref[0, plane] = eta
        row = pl.ds(grain * PLANES + plane, 1)
        prev_ref[row, :] = eta[:1]
        next_ref[row, :] = eta[ROWS - 1 :]
    for plane in range(PLANES):
        square = out[plane] * out[plane]
        fourth = square * square

        @pl.when(grain == 0)
        def _():
            for block in range(BLOCKS):
                next_sums_ref[block, plane] = square[:, column_block(block)]
                next_sums_ref[block, PLANES + plane] = fourth[:, column_block(block)]

        @pl.when(grain != 0)
        def _():
            for block in range(BLOCKS):
                next_sums_ref[block, plane] += square[:, column_block(block)]
                next_sums_ref[block, PLANES + plane] += fourth[:, column_block(block)]


def call_first_step(first, groups, mobility, noise, ids, solute, sums, above, below):
    edge = GRAINS * PLANES + 2 * PLANES
    grain_block = pl.BlockSpec((1, PLANES, ROWS, COLS), lambda i: (i, 0, 0, 0))
    return pl.pallas_call(
        first_step,
        grid=(GRAINS,),
        in_specs=[
            smem(), smem(), smem(), grain_block,
            whole(*ids.shape), whole(*solute.shape), whole(*sums.shape),
            whole(*above.shape), whole(*below.shape),
        ],
        out_specs=[grain_block, whole(*sums.shape)]
        + [whole(edge, COLS)] * 2
        + [whole(*solute.shape)]
        + [whole(3 * PLANES, COLS)] * 2,
        out_shape=[hbm(*noise.shape), shape(*sums.shape)]
        + [shape(edge, COLS)] * 2
        + [hbm(*solute.shape)]
        + [hbm(3 * PLANES, COLS)] * 2,
        scratch_shapes=[pltpu.VMEM(solute.shape, F32)] * 2,
        compiler_params=params(),
        name="first_step",
    )(first, groups, mobility, noise, *from_hbm(ids), solute, sums, *from_hbm(above, below))


PAD = 8
DEEP = ROWS + 2 * PAD


def laplace(planes):
    height = planes[0].shape[0]
    return [
        pltpu.roll(value, 1, 0) + pltpu.roll(value, height - 1, 0) + along_columns(value) + across - 6.0 * value
        for value, across in zip(planes, beside(planes))
    ]


def solute_step(
    solute_ref, middle_ref, above_ref, below_ref, mid_above_ref, mid_below_ref,
    out_ref, part_ref, deep_ref, bulk_ref,
):
    for plane in range(PLANES):
        for ref in (deep_ref, bulk_ref):
            ref[plane, :PAD] = jnp.zeros((PAD, COLS), F32)
            ref[plane, PAD + ROWS :] = jnp.zeros((PAD, COLS), F32)
        row = 3 * plane
        deep_ref[plane, PAD - 3 : PAD] = above_ref[row : row + 3, :]
        deep_ref[plane, PAD : PAD + ROWS] = solute_ref[plane]
        deep_ref[plane, PAD + ROWS : PAD + ROWS + 3] = below_ref[row : row + 3, :]
        row = GRAINS * PLANES + 2 * plane
        bulk_ref[plane, PAD - 2 : PAD] = mid_above_ref[row : row + 2, :]
        bulk_ref[plane, PAD + ROWS : PAD + ROWS + 2] = mid_below_ref[row : row + 2, :]
        bulk_ref[plane, PAD : PAD + ROWS] = middle_ref[plane]
    solute = [deep_ref[plane] for plane in range(PLANES)]
    potential = [
        2.0 * bulk_stiff * (solute[plane] - solute_mean) - bulk_ref[plane] - solute_kappa * lap
        for plane, lap in enumerate(laplace(solute))
    ]
    moved = [
        solute[plane] + time_step * solute_mobility * lap for plane, lap in enumerate(laplace(potential))
    ]
    for plane, lap in enumerate(laplace(moved)):
        part = 2.0 * bulk_stiff * (moved[plane] - solute_mean) - solute_kappa * lap
        out_ref[plane] = moved[plane][PAD : PAD + ROWS]
        part_ref[plane] = part[PAD : PAD + ROWS]


def call_solute_step(solute, bulk, above, below, mid_above, mid_below):
    return pl.pallas_call(
        solute_step,
        out_shape=[shape(*solute.shape)] * 2,
        scratch_shapes=[pltpu.VMEM((PLANES, DEEP, COLS), F32)] * 2,
        compiler_params=params(),
        name="solute_step",
    )(solute, bulk, above, below, mid_above, mid_below)


def second_potential(part_ref, sums_ref, out_ref, next_ref, prev_ref):
    for plane in range(PLANES):
        for block in range(BLOCKS):
            columns = column_block(block)
            potential = part_ref[plane, :, columns] - sums_ref[block, PLANES + plane]
            out_ref[plane, :, columns] = potential
            prev_ref[plane : plane + 1, columns] = potential[:1]
            next_ref[plane : plane + 1, columns] = potential[ROWS - 1 :]


def call_second_potential(part, sums):
    return pl.pallas_call(
        second_potential,
        out_shape=[shape(*part.shape), shape(PLANES, COLS), shape(PLANES, COLS)],
        compiler_params=params(),
        name="second_potential",
    )(part, sums)


def second_step(
    group_ref, mobility_ref, old_ref, solute_ref, sums_ref, above_ref, below_ref, eta_ref, base_ref, slope_ref
):
    grain = pl.program_id(0)

    @pl.when(grain == 0)
    def _():
        factors(sums_ref, solute_ref, base_ref, slope_ref)

    rate = time_step * mobility_ref[group_ref[grain]]
    planes = [old_ref[0, plane] for plane in range(PLANES)]
    out = stepped(planes, halo_rows(above_ref, grain), halo_rows(below_ref, grain), rate, base_ref, slope_ref)
    for plane in range(PLANES):
        eta_ref[0, plane] = out[plane]


def call_second_step(groups, mobility, eta, solute, sums, above, below):
    grain_block = pl.BlockSpec((1, PLANES, ROWS, COLS), lambda i: (i, 0, 0, 0))
    return pl.pallas_call(
        second_step,
        grid=(GRAINS,),
        in_specs=[
            smem(), smem(), grain_block, whole(*solute.shape), whole(*sums.shape),
            whole(*above.shape), whole(*below.shape),
        ],
        out_specs=grain_block,
        out_shape=shape(*eta.shape),
        scratch_shapes=[pltpu.VMEM(solute.shape, F32)] * 2,
        compiler_params=params(),
        cost_estimate=pl.CostEstimate(flops=20_000_000, bytes_accessed=10_000_000, transcendentals=0),
        name="second_step",
    )(groups, mobility, eta, solute, sums, above, below)


def solute_end(solute_ref, potential_ref, above_ref, below_ref, out_ref):
    rows = lax.broadcasted_iota(jnp.int32, (ROWS, COLS), 0)
    planes = [potential_ref[plane] for plane in range(PLANES)]
    for plane, across in enumerate(beside(planes)):
        value = planes[plane]
        up = jnp.where(rows == 0, above_ref[plane : plane + 1, :], pltpu.roll(value, 1, 0))
        down = jnp.where(rows == ROWS - 1, below_ref[plane : plane + 1, :], pltpu.roll(value, ROWS - 1, 0))
        lap = up + down + along_columns(value) + across - 6.0 * value
        out_ref[plane] = solute_ref[plane] + time_step * solute_mobility * lap


def call_solute_end(solute, potential, above, below):
    return pl.pallas_call(
        solute_end,
        out_shape=shape(*solute.shape),
        compiler_params=params(),
        name="solute_end",
    )(solute, potential, above, below)


def exchange(to_next, to_prev, count):
    above = lax.ppermute(to_next, SPACE, [(i, (i + 1) % count) for i in range(count)])
    below = lax.ppermute(to_prev, SPACE, [((i + 1) % count, i) for i in range(count)])
    return above, below


def added(parts_ref, index):
    values = [parts_ref[(part,) + index] for part in range(parts_ref.shape[0])]
    while len(values) > 1:
        values = [left + right for left, right in zip(values[::2], values[1::2])]
    return values[0]


def add_parts(parts_ref, out_ref):
    for block in range(out_ref.shape[0]):
        for row in range(out_ref.shape[1]):
            out_ref[block, row] = added(parts_ref, (block, row))


def call_add_parts(parts):
    return pl.pallas_call(
        add_parts, out_shape=shape(*parts.shape[1:]), compiler_params=params(), name="add_parts"
    )(parts)


def owner(parts_ref, copies_ref):
    for plane in range(PLANES):
        two, four = added(parts_ref, (plane,)), added(parts_ref, (PLANES + plane,))
        bulk = solute_beta * (two * two - four)
        for copy in range(copies_ref.shape[0]):
            copies_ref[copy, plane] = two
            copies_ref[copy, PLANES + plane] = bulk


def call_owner(parts):
    return pl.pallas_call(
        owner, out_shape=shape(*parts.shape), compiler_params=params(), name="owner"
    )(parts)


def copies(value_ref, out_ref):
    for copy in range(out_ref.shape[0]):
        out_ref[copy] = value_ref[...]


def call_copies(value, count):
    return pl.pallas_call(
        copies, out_shape=shape(count, *value.shape), compiler_params=params(), name="copies"
    )(value)


def dealt(blocks, axis):
    return lax.all_to_all(blocks, axis, 0, 0, tiled=True)


def total(sums, *beside_it):
    along = lax.axis_size("x")
    parts = dealt(sums.reshape((along, BLOCKS // along) + sums.shape[1:]), "x")
    parts, *beside_it = lax.optimization_barrier((parts, *beside_it))
    parts = dealt(call_add_parts(parts), "yh")
    parts = dealt(call_owner(parts), "yh")
    return dealt(call_copies(parts, along), "x").reshape(sums.shape), *beside_it


def shards(grain_ids, group_of, group_mobility, seed_noise, concentration):
    count = lax.axis_size("yl") * lax.axis_size("z") * lax.axis_size("core")
    first = (lax.axis_index(GRAIN) * GRAINS).astype(jnp.int32).reshape(1)
    sums, to_next, to_prev = call_first_sums(first, seed_noise, grain_ids, concentration)
    above, below = exchange(to_next, to_prev, count)
    (sums,) = total(sums)
    eta, sums, to_next, to_prev, bulk, rows_above, rows_below = call_first_step(
        first, group_of, group_mobility, seed_noise, grain_ids, concentration, sums, above, below
    )
    sums, mid_above, mid_below = total(sums, *exchange(to_next, to_prev, count))
    solute, part = call_solute_step(concentration, bulk, rows_above, rows_below, mid_above, mid_below)
    potential, to_next, to_prev = call_second_potential(part, sums)
    end_above, end_below = exchange(to_next, to_prev, count)
    eta = call_second_step(group_of, group_mobility, eta, solute, sums, mid_above, mid_below)
    solute = call_solute_end(solute, potential, end_above, end_below)
    return eta, solute


def solution(mesh):
    fine = Mesh(mesh.devices.reshape(2, 8, 2, 4, 4), SPACE + GRAIN)
    placed = (
        P(None, SPACE, None),
        P(GRAIN),
        P(),
        P(GRAIN, None, SPACE, None),
        P(None, SPACE, None),
    )
    return jax.shard_map(
        shards,
        mesh=fine,
        in_specs=placed,
        out_specs=(P(GRAIN, None, SPACE, None), P(None, SPACE, None)),
        check_vma=False,
    )
```

```python
import jax
import jax.numpy as jnp
from jax import lax
from jax.experimental import pallas as pl
from jax.experimental.pallas import tpu as pltpu
from jax.sharding import Mesh, PartitionSpec as P

GRAINS, PLANES, ROWS, COLS, LANES = 6, 3, 16, 2048, 128
BLOCKS = COLS // LANES
SPACE = ("yl", "z", "core")
GRAIN = ("x", "yh")

coef_quad = 1.0
coef_quart = 1.0
cross_gamma = 1.5
gradient_kappa = 0.5
solute_beta = 0.6
bulk_stiff = 1.0
solute_mean = 0.4
solute_kappa = 0.25
solute_mobility = 0.3
time_step = 0.1

F32 = jnp.float32
MIB = 1024 * 1024


def shape(*dims):
    return jax.ShapeDtypeStruct(dims, F32)


def hbm(*dims):
    return pltpu.HBM(dims, F32)


def from_hbm(*arrays):
    return [pltpu.with_memory_space_constraint(array, pltpu.HBM) for array in arrays]


def params(mib=16):
    return pltpu.CompilerParams(vmem_limit_bytes=mib * MIB)


def whole(*dims):
    return pl.BlockSpec(dims, lambda *_: (0,) * len(dims))


def smem():
    return pl.BlockSpec(memory_space=pltpu.SMEM)


def along_columns(value):
    return pltpu.roll(value, 1, 1) + pltpu.roll(value, COLS - 1, 1)


def beside(planes):
    return (planes[0] + planes[1], planes[0] + planes[2], planes[1] + planes[2])


def column_block(block):
    return slice(block * LANES, (block + 1) * LANES)


def first_sums(first_ref, noise_ref, ids_ref, solute_ref, sums_ref, next_ref, prev_ref):
    for plane in range(PLANES):
        ids = ids_ref[plane]
        two = four = None
        for grain in range(GRAINS):
            seed = jnp.where(ids == first_ref[0] + grain, 0.9, 0.0).astype(F32)
            eta = seed + noise_ref[grain, plane]
            row = grain * PLANES + plane
            prev_ref[row : row + 1, :] = eta[:1]
            next_ref[row : row + 1, :] = eta[ROWS - 1 :]
            square = eta * eta
            two = square if two is None else two + square
            four = square * square if four is None else four + square * square
        for block in range(sums_ref.shape[0]):
            sums_ref[block, plane] = two[:, column_block(block)]
            sums_ref[block, PLANES + plane] = four[:, column_block(block)]
        row = GRAINS * PLANES + 3 * plane
        prev_ref[row : row + 3, :] = solute_ref[plane, :3]
        next_ref[row : row + 3, :] = solute_ref[plane, ROWS - 3 :]


def call_first_sums(first, noise, ids, solute):
    width = 512
    edge = GRAINS * PLANES + 3 * PLANES
    return pl.pallas_call(
        first_sums,
        grid=(COLS // width,),
        in_specs=[
            smem(),
            pl.BlockSpec((GRAINS, PLANES, ROWS, width), lambda i: (0, 0, 0, i)),
            pl.BlockSpec((PLANES, ROWS, width), lambda i: (0, 0, i)),
            pl.BlockSpec((PLANES, ROWS, width), lambda i: (0, 0, i)),
        ],
        out_specs=[
            pl.BlockSpec((width // LANES, 2 * PLANES, ROWS, LANES), lambda i: (i, 0, 0, 0)),
            pl.BlockSpec((edge, width), lambda i: (0, i)),
            pl.BlockSpec((edge, width), lambda i: (0, i)),
        ],
        out_shape=[
            shape(BLOCKS, 2 * PLANES, ROWS, LANES),
            shape(edge, COLS),
            shape(edge, COLS),
        ],
        compiler_params=params(60),
        name="first_sums",
    )(first, noise, ids, solute)


def factors(sums_ref, solute_ref, base_ref, slope_ref):
    for plane in range(PLANES):
        for block in range(BLOCKS):
            columns = column_block(block)
            cross = 2.0 * cross_gamma - 4.0 * solute_beta * solute_ref[plane, :, columns]
            base_ref[plane, :, columns] = (
                coef_quad - 6.0 * gradient_kappa - sums_ref[block, plane] * cross
            )
            slope_ref[plane, :, columns] = cross - coef_quart


def stepped(planes, above, below, rate, base_ref, slope_ref):
    rows = lax.broadcasted_iota(jnp.int32, (ROWS, COLS), 0)
    out = []
    for plane, across in zip(range(PLANES), beside(planes)):
        eta = planes[plane]
        up = jnp.where(rows == 0, above[plane], pltpu.roll(eta, 1, 0))
        down = jnp.where(rows == ROWS - 1, below[plane], pltpu.roll(eta, ROWS - 1, 0))
        around = up + down + along_columns(eta) + across
        bracket = base_ref[plane] + slope_ref[plane] * (eta * eta)
        out.append(eta + rate * (eta * bracket + gradient_kappa * around))
    return out


def halo_rows(ref, grain):
    return [ref[pl.ds(grain * PLANES + plane, 1), :] for plane in range(PLANES)]


def first_step(
    first_ref, group_ref, mobility_ref, noise_ref, ids_ref, solute_ref, sums_ref, above_ref, below_ref,
    eta_ref, next_sums_ref, next_ref, prev_ref, bulk_ref, rows_above_ref, rows_below_ref, base_ref, slope_ref,
):
    grain = pl.program_id(0)

    @pl.when(grain == 0)
    def _():
        factors(sums_ref, solute_ref, base_ref, slope_ref)
        for plane in range(PLANES):
            row = GRAINS * PLANES + 2 * plane
            for block in range(BLOCKS):
                columns = column_block(block)
                bulk = sums_ref[block, PLANES + plane]
                bulk_ref[plane, :, columns] = bulk
                prev_ref[row : row + 2, columns] = bulk[:2]
                next_ref[row : row + 2, columns] = bulk[ROWS - 2 :]
        rows_above_ref[...] = above_ref[GRAINS * PLANES :]
        rows_below_ref[...] = below_ref[GRAINS * PLANES :]

    rate = time_step * mobility_ref[group_ref[grain]]
    planes = [
        jnp.where(ids_ref[plane] == first_ref[0] + grain, 0.9, 0.0).astype(F32) + noise_ref[0, plane]
        for plane in range(PLANES)
    ]
    out = stepped(planes, halo_rows(above_ref, grain), halo_rows(below_ref, grain), rate, base_ref, slope_ref)
    for plane in range(PLANES):
        eta = out[plane]
        eta_ref[0, plane] = eta
        row = pl.ds(grain * PLANES + plane, 1)
        prev_ref[row, :] = eta[:1]
        next_ref[row, :] = eta[ROWS - 1 :]
    for plane in range(PLANES):
        square = out[plane] * out[plane]
        fourth = square * square

        @pl.when(grain == 0)
        def _():
            for block in range(BLOCKS):
                next_sums_ref[block, plane] = square[:, column_block(block)]
                next_sums_ref[block, PLANES + plane] = fourth[:, column_block(block)]

        @pl.when(grain != 0)
        def _():
            for block in range(BLOCKS):
                next_sums_ref[block, plane] += square[:, column_block(block)]
                next_sums_ref[block, PLANES + plane] += fourth[:, column_block(block)]


def call_first_step(first, groups, mobility, noise, ids, solute, sums, above, below):
    edge = GRAINS * PLANES + 2 * PLANES
    grain_block = pl.BlockSpec((1, PLANES, ROWS, COLS), lambda i: (i, 0, 0, 0))
    return pl.pallas_call(
        first_step,
        grid=(GRAINS,),
        in_specs=[
            smem(), smem(), smem(), grain_block,
            whole(*ids.shape), whole(*solute.shape), whole(*sums.shape),
            whole(*above.shape), whole(*below.shape),
        ],
        out_specs=[grain_block, whole(*sums.shape)]
        + [whole(edge, COLS)] * 2
        + [whole(*solute.shape)]
        + [whole(3 * PLANES, COLS)] * 2,
        out_shape=[hbm(*noise.shape), hbm(*sums.shape)]
        + [hbm(edge, COLS)] * 2
        + [hbm(*solute.shape)]
        + [hbm(3 * PLANES, COLS)] * 2,
        scratch_shapes=[pltpu.VMEM(solute.shape, F32)] * 2,
        compiler_params=params(),
        name="first_step",
    )(first, groups, mobility, noise, *from_hbm(ids), solute, sums, *from_hbm(above, below))


PAD = 8
DEEP = ROWS + 2 * PAD


def laplace(planes):
    height = planes[0].shape[0]
    return [
        pltpu.roll(value, 1, 0) + pltpu.roll(value, height - 1, 0) + along_columns(value) + across - 6.0 * value
        for value, across in zip(planes, beside(planes))
    ]


def solute_step(
    solute_ref, middle_ref, above_ref, below_ref, mid_above_ref, mid_below_ref,
    out_ref, part_ref, deep_ref, bulk_ref,
):
    for plane in range(PLANES):
        for ref in (deep_ref, bulk_ref):
            ref[plane, :PAD] = jnp.zeros((PAD, COLS), F32)
            ref[plane, PAD + ROWS :] = jnp.zeros((PAD, COLS), F32)
        row = 3 * plane
        deep_ref[plane, PAD - 3 : PAD] = above_ref[row : row + 3, :]
        deep_ref[plane, PAD : PAD + ROWS] = solute_ref[plane]
        deep_ref[plane, PAD + ROWS : PAD + ROWS + 3] = below_ref[row : row + 3, :]
        row = GRAINS * PLANES + 2 * plane
        bulk_ref[plane, PAD - 2 : PAD] = mid_above_ref[row : row + 2, :]
        bulk_ref[plane, PAD + ROWS : PAD + ROWS + 2] = mid_below_ref[row : row + 2, :]
        bulk_ref[plane, PAD : PAD + ROWS] = middle_ref[plane]
    solute = [deep_ref[plane] for plane in range(PLANES)]
    potential = [
        2.0 * bulk_stiff * (solute[plane] - solute_mean) - bulk_ref[plane] - solute_kappa * lap
        for plane, lap in enumerate(laplace(solute))
    ]
    moved = [
        solute[plane] + time_step * solute_mobility * lap for plane, lap in enumerate(laplace(potential))
    ]
    for plane, lap in enumerate(laplace(moved)):
        part = 2.0 * bulk_stiff * (moved[plane] - solute_mean) - solute_kappa * lap
        out_ref[plane] = moved[plane][PAD : PAD + ROWS]
        part_ref[plane] = part[PAD : PAD + ROWS]


def call_solute_step(solute, bulk, above, below, mid_above, mid_below):
    return pl.pallas_call(
        solute_step,
        out_shape=[shape(*solute.shape)] * 2,
        scratch_shapes=[pltpu.VMEM((PLANES, DEEP, COLS), F32)] * 2,
        compiler_params=params(),
        name="solute_step",
    )(solute, bulk, above, below, mid_above, mid_below)


def second_potential(part_ref, sums_ref, out_ref, next_ref, prev_ref):
    for plane in range(PLANES):
        for block in range(BLOCKS):
            columns = column_block(block)
            potential = part_ref[plane, :, columns] - sums_ref[block, PLANES + plane]
            out_ref[plane, :, columns] = potential
            prev_ref[plane : plane + 1, columns] = potential[:1]
            next_ref[plane : plane + 1, columns] = potential[ROWS - 1 :]


def call_second_potential(part, sums):
    return pl.pallas_call(
        second_potential,
        out_shape=[shape(*part.shape), shape(PLANES, COLS), shape(PLANES, COLS)],
        compiler_params=params(),
        name="second_potential",
    )(part, sums)


def second_step(
    group_ref, mobility_ref, old_ref, solute_ref, sums_ref, above_ref, below_ref, eta_ref, base_ref, slope_ref
):
    grain = pl.program_id(0)

    @pl.when(grain == 0)
    def _():
        factors(sums_ref, solute_ref, base_ref, slope_ref)

    rate = time_step * mobility_ref[group_ref[grain]]
    planes = [old_ref[0, plane] for plane in range(PLANES)]
    out = stepped(planes, halo_rows(above_ref, grain), halo_rows(below_ref, grain), rate, base_ref, slope_ref)
    for plane in range(PLANES):
        eta_ref[0, plane] = out[plane]


def call_second_step(groups, mobility, eta, solute, sums, above, below):
    grain_block = pl.BlockSpec((1, PLANES, ROWS, COLS), lambda i: (i, 0, 0, 0))
    return pl.pallas_call(
        second_step,
        grid=(GRAINS,),
        in_specs=[
            smem(), smem(), grain_block, whole(*solute.shape), whole(*sums.shape),
            whole(*above.shape), whole(*below.shape),
        ],
        out_specs=grain_block,
        out_shape=shape(*eta.shape),
        scratch_shapes=[pltpu.VMEM(solute.shape, F32)] * 2,
        compiler_params=params(),
        cost_estimate=pl.CostEstimate(flops=20_000_000, bytes_accessed=10_000_000, transcendentals=0),
        name="second_step",
    )(groups, mobility, eta, solute, sums, above, below)


def solute_end(solute_ref, potential_ref, above_ref, below_ref, out_ref):
    rows = lax.broadcasted_iota(jnp.int32, (ROWS, COLS), 0)
    planes = [potential_ref[plane] for plane in range(PLANES)]
    for plane, across in enumerate(beside(planes)):
        value = planes[plane]
        up = jnp.where(rows == 0, above_ref[plane : plane + 1, :], pltpu.roll(value, 1, 0))
        down = jnp.where(rows == ROWS - 1, below_ref[plane : plane + 1, :], pltpu.roll(value, ROWS - 1, 0))
        lap = up + down + along_columns(value) + across - 6.0 * value
        out_ref[plane] = solute_ref[plane] + time_step * solute_mobility * lap


def call_solute_end(solute, potential, above, below):
    return pl.pallas_call(
        solute_end,
        out_shape=shape(*solute.shape),
        compiler_params=params(),
        name="solute_end",
    )(solute, potential, above, below)


def exchange(to_next, to_prev, count):
    above = lax.ppermute(to_next, SPACE, [(i, (i + 1) % count) for i in range(count)])
    below = lax.ppermute(to_prev, SPACE, [((i + 1) % count, i) for i in range(count)])
    return above, below


def added(parts_ref, index):
    values = [parts_ref[(part,) + index] for part in range(parts_ref.shape[0])]
    while len(values) > 1:
        values = [left + right for left, right in zip(values[::2], values[1::2])]
    return values[0]


def add_parts(parts_ref, out_ref):
    for block in range(out_ref.shape[0]):
        for row in range(out_ref.shape[1]):
            out_ref[block, row] = added(parts_ref, (block, row))


def call_add_parts(parts):
    return pl.pallas_call(
        add_parts, out_shape=shape(*parts.shape[1:]), compiler_params=params(), name="add_parts"
    )(parts)


def owner(parts_ref, copies_ref):
    for plane in range(PLANES):
        two, four = added(parts_ref, (plane,)), added(parts_ref, (PLANES + plane,))
        bulk = solute_beta * (two * two - four)
        for copy in range(copies_ref.shape[0]):
            copies_ref[copy, plane] = two
            copies_ref[copy, PLANES + plane] = bulk


def call_owner(parts):
    return pl.pallas_call(
        owner, out_shape=shape(*parts.shape), compiler_params=params(), name="owner"
    )(parts)


def copies(value_ref, out_ref):
    for copy in range(out_ref.shape[0]):
        out_ref[copy] = value_ref[...]


def call_copies(value, count):
    return pl.pallas_call(
        copies, out_shape=shape(count, *value.shape), compiler_params=params(), name="copies"
    )(value)


def dealt(blocks, axis):
    return lax.all_to_all(blocks, axis, 0, 0, tiled=True)


def total(sums, *beside_it):
    along = lax.axis_size("x")
    parts = dealt(sums.reshape((along, BLOCKS // along) + sums.shape[1:]), "x")
    parts, *beside_it = lax.optimization_barrier((parts, *beside_it))
    parts = dealt(call_add_parts(parts), "yh")
    parts = dealt(call_owner(parts), "yh")
    return dealt(call_copies(parts, along), "x").reshape(sums.shape), *beside_it


def shards(grain_ids, group_of, group_mobility, seed_noise, concentration):
    count = lax.axis_size("yl") * lax.axis_size("z") * lax.axis_size("core")
    first = (lax.axis_index(GRAIN) * GRAINS).astype(jnp.int32).reshape(1)
    sums, to_next, to_prev = call_first_sums(first, seed_noise, grain_ids, concentration)
    above, below = exchange(to_next, to_prev, count)
    (sums,) = total(sums)
    eta, sums, to_next, to_prev, bulk, rows_above, rows_below = call_first_step(
        first, group_of, group_mobility, seed_noise, grain_ids, concentration, sums, above, below
    )
    sums, mid_above, mid_below = total(sums, *exchange(to_next, to_prev, count))
    solute, part = call_solute_step(concentration, bulk, rows_above, rows_below, mid_above, mid_below)
    potential, to_next, to_prev = call_second_potential(part, sums)
    end_above, end_below = exchange(to_next, to_prev, count)
    eta = call_second_step(group_of, group_mobility, eta, solute, sums, mid_above, mid_below)
    solute = call_solute_end(solute, potential, end_above, end_below)
    return eta, solute


def solution(mesh):
    fine = Mesh(mesh.devices.reshape(2, 8, 2, 4, 4), SPACE + GRAIN)
    placed = (
        P(None, SPACE, None),
        P(GRAIN),
        P(),
        P(GRAIN, None, SPACE, None),
        P(None, SPACE, None),
    )
    return jax.shard_map(
        shards,
        mesh=fine,
        in_specs=placed,
        out_specs=(P(GRAIN, None, SPACE, None), P(None, SPACE, None)),
        check_vma=False,
    )
```

```python
import jax
import jax.numpy as jnp
from jax import lax
from jax.experimental import pallas as pl
from jax.experimental.pallas import tpu as pltpu
from jax.sharding import Mesh, PartitionSpec as P

GRAINS, PLANES, ROWS, COLS, LANES = 6, 3, 16, 2048, 128
BLOCKS = COLS // LANES
SPACE = ("yl", "z", "core")
GRAIN = ("x", "yh")

coef_quad = 1.0
coef_quart = 1.0
cross_gamma = 1.5
gradient_kappa = 0.5
solute_beta = 0.6
bulk_stiff = 1.0
solute_mean = 0.4
solute_kappa = 0.25
solute_mobility = 0.3
time_step = 0.1

F32 = jnp.float32
MIB = 1024 * 1024


def shape(*dims):
    return jax.ShapeDtypeStruct(dims, F32)


def hbm(*dims):
    return pltpu.HBM(dims, F32)


def from_hbm(*arrays):
    return [pltpu.with_memory_space_constraint(array, pltpu.HBM) for array in arrays]


def params(mib=16):
    return pltpu.CompilerParams(vmem_limit_bytes=mib * MIB)


def whole(*dims):
    return pl.BlockSpec(dims, lambda *_: (0,) * len(dims))


def smem():
    return pl.BlockSpec(memory_space=pltpu.SMEM)


def along_columns(value):
    return pltpu.roll(value, 1, 1) + pltpu.roll(value, COLS - 1, 1)


def beside(planes):
    return (planes[0] + planes[1], planes[0] + planes[2], planes[1] + planes[2])


def column_block(block):
    return slice(block * LANES, (block + 1) * LANES)


def first_sums(first_ref, noise_ref, ids_ref, solute_ref, sums_ref, next_ref, prev_ref):
    for plane in range(PLANES):
        ids = ids_ref[plane]
        two = four = None
        for grain in range(GRAINS):
            seed = jnp.where(ids == first_ref[0] + grain, 0.9, 0.0).astype(F32)
            eta = seed + noise_ref[grain, plane]
            row = grain * PLANES + plane
            prev_ref[row : row + 1, :] = eta[:1]
            next_ref[row : row + 1, :] = eta[ROWS - 1 :]
            square = eta * eta
            two = square if two is None else two + square
            four = square * square if four is None else four + square * square
        for block in range(sums_ref.shape[0]):
            sums_ref[block, plane] = two[:, column_block(block)]
            sums_ref[block, PLANES + plane] = four[:, column_block(block)]
        row = GRAINS * PLANES + 3 * plane
        prev_ref[row : row + 3, :] = solute_ref[plane, :3]
        next_ref[row : row + 3, :] = solute_ref[plane, ROWS - 3 :]


def call_first_sums(first, noise, ids, solute):
    width = 512
    edge = GRAINS * PLANES + 3 * PLANES
    return pl.pallas_call(
        first_sums,
        grid=(COLS // width,),
        in_specs=[
            smem(),
            pl.BlockSpec((GRAINS, PLANES, ROWS, width), lambda i: (0, 0, 0, i)),
            pl.BlockSpec((PLANES, ROWS, width), lambda i: (0, 0, i)),
            pl.BlockSpec((PLANES, ROWS, width), lambda i: (0, 0, i)),
        ],
        out_specs=[
            pl.BlockSpec((width // LANES, 2 * PLANES, ROWS, LANES), lambda i: (i, 0, 0, 0)),
            pl.BlockSpec((edge, width), lambda i: (0, i)),
            pl.BlockSpec((edge, width), lambda i: (0, i)),
        ],
        out_shape=[
            shape(BLOCKS, 2 * PLANES, ROWS, LANES),
            shape(edge, COLS),
            shape(edge, COLS),
        ],
        compiler_params=params(60),
        name="first_sums",
    )(first, noise, ids, solute)


def factors(sums_ref, solute_ref, base_ref, slope_ref):
    for plane in range(PLANES):
        for block in range(BLOCKS):
            columns = column_block(block)
            cross = 2.0 * cross_gamma - 4.0 * solute_beta * solute_ref[plane, :, columns]
            base_ref[plane, :, columns] = (
                coef_quad - 6.0 * gradient_kappa - sums_ref[block, plane] * cross
            )
            slope_ref[plane, :, columns] = cross - coef_quart


def stepped(planes, above, below, rate, base_ref, slope_ref):
    rows = lax.broadcasted_iota(jnp.int32, (ROWS, COLS), 0)
    out = []
    for plane, across in zip(range(PLANES), beside(planes)):
        eta = planes[plane]
        up = jnp.where(rows == 0, above[plane], pltpu.roll(eta, 1, 0))
        down = jnp.where(rows == ROWS - 1, below[plane], pltpu.roll(eta, ROWS - 1, 0))
        around = up + down + along_columns(eta) + across
        bracket = base_ref[plane] + slope_ref[plane] * (eta * eta)
        out.append(eta + rate * (eta * bracket + gradient_kappa * around))
    return out


def halo_rows(ref, grain):
    return [ref[pl.ds(grain * PLANES + plane, 1), :] for plane in range(PLANES)]


def first_step(
    first_ref, group_ref, mobility_ref, noise_ref, ids_ref, solute_ref, sums_ref, above_ref, below_ref,
    eta_ref, next_sums_ref, next_ref, prev_ref, bulk_ref, rows_above_ref, rows_below_ref, base_ref, slope_ref,
):
    grain = pl.program_id(0)

    @pl.when(grain == 0)
    def _():
        factors(sums_ref, solute_ref, base_ref, slope_ref)
        for plane in range(PLANES):
            row = GRAINS * PLANES + 2 * plane
            for block in range(BLOCKS):
                columns = column_block(block)
                bulk = sums_ref[block, PLANES + plane]
                bulk_ref[plane, :, columns] = bulk
                prev_ref[row : row + 2, columns] = bulk[:2]
                next_ref[row : row + 2, columns] = bulk[ROWS - 2 :]
        rows_above_ref[...] = above_ref[GRAINS * PLANES :]
        rows_below_ref[...] = below_ref[GRAINS * PLANES :]

    rate = time_step * mobility_ref[group_ref[grain]]
    planes = [
        jnp.where(ids_ref[plane] == first_ref[0] + grain, 0.9, 0.0).astype(F32) + noise_ref[0, plane]
        for plane in range(PLANES)
    ]
    out = stepped(planes, halo_rows(above_ref, grain), halo_rows(below_ref, grain), rate, base_ref, slope_ref)
    for plane in range(PLANES):
        eta = out[plane]
        eta_ref[0, plane] = eta
        row = pl.ds(grain * PLANES + plane, 1)
        prev_ref[row, :] = eta[:1]
        next_ref[row, :] = eta[ROWS - 1 :]
    for plane in range(PLANES):
        square = out[plane] * out[plane]
        fourth = square * square

        @pl.when(grain == 0)
        def _():
            for block in range(BLOCKS):
                next_sums_ref[block, plane] = square[:, column_block(block)]
                next_sums_ref[block, PLANES + plane] = fourth[:, column_block(block)]

        @pl.when(grain != 0)
        def _():
            for block in range(BLOCKS):
                next_sums_ref[block, plane] += square[:, column_block(block)]
                next_sums_ref[block, PLANES + plane] += fourth[:, column_block(block)]


def call_first_step(first, groups, mobility, noise, ids, solute, sums, above, below):
    edge = GRAINS * PLANES + 2 * PLANES
    grain_block = pl.BlockSpec((1, PLANES, ROWS, COLS), lambda i: (i, 0, 0, 0))
    return pl.pallas_call(
        first_step,
        grid=(GRAINS,),
        in_specs=[
            smem(), smem(), smem(), grain_block,
            whole(*ids.shape), whole(*solute.shape), whole(*sums.shape),
            whole(*above.shape), whole(*below.shape),
        ],
        out_specs=[grain_block, whole(*sums.shape)]
        + [whole(edge, COLS)] * 2
        + [whole(*solute.shape)]
        + [whole(3 * PLANES, COLS)] * 2,
        out_shape=[hbm(*noise.shape), hbm(*sums.shape)]
        + [hbm(edge, COLS)] * 2
        + [hbm(*solute.shape)]
        + [hbm(3 * PLANES, COLS)] * 2,
        scratch_shapes=[pltpu.VMEM(solute.shape, F32)] * 2,
        compiler_params=params(),
        name="first_step",
    )(first, groups, mobility, noise, *from_hbm(ids), solute, sums, *from_hbm(above, below))


PAD = 8
DEEP = ROWS + 2 * PAD


def laplace(planes):
    height = planes[0].shape[0]
    return [
        pltpu.roll(value, 1, 0) + pltpu.roll(value, height - 1, 0) + along_columns(value) + across - 6.0 * value
        for value, across in zip(planes, beside(planes))
    ]


def solute_step(
    solute_ref, middle_ref, above_ref, below_ref, mid_above_ref, mid_below_ref,
    out_ref, part_ref, deep_ref, bulk_ref,
):
    for plane in range(PLANES):
        for ref in (deep_ref, bulk_ref):
            ref[plane, :PAD] = jnp.zeros((PAD, COLS), F32)
            ref[plane, PAD + ROWS :] = jnp.zeros((PAD, COLS), F32)
        row = 3 * plane
        deep_ref[plane, PAD - 3 : PAD] = above_ref[row : row + 3, :]
        deep_ref[plane, PAD : PAD + ROWS] = solute_ref[plane]
        deep_ref[plane, PAD + ROWS : PAD + ROWS + 3] = below_ref[row : row + 3, :]
        row = GRAINS * PLANES + 2 * plane
        bulk_ref[plane, PAD - 2 : PAD] = mid_above_ref[row : row + 2, :]
        bulk_ref[plane, PAD + ROWS : PAD + ROWS + 2] = mid_below_ref[row : row + 2, :]
        bulk_ref[plane, PAD : PAD + ROWS] = middle_ref[plane]
    solute = [deep_ref[plane] for plane in range(PLANES)]
    potential = [
        2.0 * bulk_stiff * (solute[plane] - solute_mean) - bulk_ref[plane] - solute_kappa * lap
        for plane, lap in enumerate(laplace(solute))
    ]
    moved = [
        solute[plane] + time_step * solute_mobility * lap for plane, lap in enumerate(laplace(potential))
    ]
    for plane, lap in enumerate(laplace(moved)):
        part = 2.0 * bulk_stiff * (moved[plane] - solute_mean) - solute_kappa * lap
        out_ref[plane] = moved[plane][PAD : PAD + ROWS]
        part_ref[plane] = part[PAD : PAD + ROWS]


def call_solute_step(solute, bulk, above, below, mid_above, mid_below):
    return pl.pallas_call(
        solute_step,
        out_shape=[shape(*solute.shape)] * 2,
        scratch_shapes=[pltpu.VMEM((PLANES, DEEP, COLS), F32)] * 2,
        compiler_params=params(),
        name="solute_step",
    )(solute, bulk, above, below, mid_above, mid_below)


def second_potential(part_ref, sums_ref, out_ref, next_ref, prev_ref):
    for plane in range(PLANES):
        for block in range(BLOCKS):
            columns = column_block(block)
            potential = part_ref[plane, :, columns] - sums_ref[block, PLANES + plane]
            out_ref[plane, :, columns] = potential
            prev_ref[plane : plane + 1, columns] = potential[:1]
            next_ref[plane : plane + 1, columns] = potential[ROWS - 1 :]


def call_second_potential(part, sums):
    return pl.pallas_call(
        second_potential,
        out_shape=[shape(*part.shape), shape(PLANES, COLS), shape(PLANES, COLS)],
        compiler_params=params(),
        name="second_potential",
    )(part, sums)


def second_step(
    group_ref, mobility_ref, old_ref, solute_ref, sums_ref, above_ref, below_ref, eta_ref, base_ref, slope_ref
):
    grain = pl.program_id(0)

    @pl.when(grain == 0)
    def _():
        factors(sums_ref, solute_ref, base_ref, slope_ref)

    rate = time_step * mobility_ref[group_ref[grain]]
    planes = [old_ref[0, plane] for plane in range(PLANES)]
    out = stepped(planes, halo_rows(above_ref, grain), halo_rows(below_ref, grain), rate, base_ref, slope_ref)
    for plane in range(PLANES):
        eta_ref[0, plane] = out[plane]


def call_second_step(groups, mobility, eta, solute, sums, above, below):
    grain_block = pl.BlockSpec((1, PLANES, ROWS, COLS), lambda i: (i, 0, 0, 0))
    return pl.pallas_call(
        second_step,
        grid=(GRAINS,),
        in_specs=[
            smem(), smem(), grain_block, whole(*solute.shape), whole(*sums.shape),
            whole(*above.shape), whole(*below.shape),
        ],
        out_specs=grain_block,
        out_shape=shape(*eta.shape),
        scratch_shapes=[pltpu.VMEM(solute.shape, F32)] * 2,
        compiler_params=params(),
        cost_estimate=pl.CostEstimate(flops=20_000_000, bytes_accessed=10_000_000, transcendentals=0),
        name="second_step",
    )(groups, mobility, *from_hbm(eta), solute, sums, above, below)


def solute_end(solute_ref, potential_ref, above_ref, below_ref, out_ref):
    rows = lax.broadcasted_iota(jnp.int32, (ROWS, COLS), 0)
    planes = [potential_ref[plane] for plane in range(PLANES)]
    for plane, across in enumerate(beside(planes)):
        value = planes[plane]
        up = jnp.where(rows == 0, above_ref[plane : plane + 1, :], pltpu.roll(value, 1, 0))
        down = jnp.where(rows == ROWS - 1, below_ref[plane : plane + 1, :], pltpu.roll(value, ROWS - 1, 0))
        lap = up + down + along_columns(value) + across - 6.0 * value
        out_ref[plane] = solute_ref[plane] + time_step * solute_mobility * lap


def call_solute_end(solute, potential, above, below):
    return pl.pallas_call(
        solute_end,
        out_shape=shape(*solute.shape),
        compiler_params=params(),
        name="solute_end",
    )(solute, potential, above, below)


def exchange(to_next, to_prev, count):
    above = lax.ppermute(to_next, SPACE, [(i, (i + 1) % count) for i in range(count)])
    below = lax.ppermute(to_prev, SPACE, [((i + 1) % count, i) for i in range(count)])
    return above, below


def added(parts_ref, index):
    values = [parts_ref[(part,) + index] for part in range(parts_ref.shape[0])]
    while len(values) > 1:
        values = [left + right for left, right in zip(values[::2], values[1::2])]
    return values[0]


def add_parts(parts_ref, out_ref):
    for block in range(out_ref.shape[0]):
        for row in range(out_ref.shape[1]):
            out_ref[block, row] = added(parts_ref, (block, row))


def call_add_parts(parts):
    return pl.pallas_call(
        add_parts, out_shape=shape(*parts.shape[1:]), compiler_params=params(), name="add_parts"
    )(parts)


def owner(parts_ref, copies_ref):
    for plane in range(PLANES):
        two, four = added(parts_ref, (plane,)), added(parts_ref, (PLANES + plane,))
        bulk = solute_beta * (two * two - four)
        for copy in range(copies_ref.shape[0]):
            copies_ref[copy, plane] = two
            copies_ref[copy, PLANES + plane] = bulk


def call_owner(parts):
    return pl.pallas_call(
        owner, out_shape=shape(*parts.shape), compiler_params=params(), name="owner"
    )(parts)


def copies(value_ref, out_ref):
    for copy in range(out_ref.shape[0]):
        out_ref[copy] = value_ref[...]


def call_copies(value, count):
    return pl.pallas_call(
        copies, out_shape=shape(count, *value.shape), compiler_params=params(), name="copies"
    )(value)


def dealt(blocks, axis):
    return lax.all_to_all(blocks, axis, 0, 0, tiled=True)


def total(sums, *beside_it):
    along = lax.axis_size("x")
    parts = dealt(sums.reshape((along, BLOCKS // along) + sums.shape[1:]), "x")
    parts, *beside_it = lax.optimization_barrier((parts, *beside_it))
    parts = dealt(call_add_parts(parts), "yh")
    parts = dealt(call_owner(parts), "yh")
    return dealt(call_copies(parts, along), "x").reshape(sums.shape), *beside_it


def shards(grain_ids, group_of, group_mobility, seed_noise, concentration):
    count = lax.axis_size("yl") * lax.axis_size("z") * lax.axis_size("core")
    first = (lax.axis_index(GRAIN) * GRAINS).astype(jnp.int32).reshape(1)
    sums, to_next, to_prev = call_first_sums(first, seed_noise, grain_ids, concentration)
    above, below = exchange(to_next, to_prev, count)
    (sums,) = total(sums)
    eta, sums, to_next, to_prev, bulk, rows_above, rows_below = call_first_step(
        first, group_of, group_mobility, seed_noise, grain_ids, concentration, sums, above, below
    )
    sums, mid_above, mid_below = total(sums, *exchange(to_next, to_prev, count))
    solute, part = call_solute_step(concentration, bulk, rows_above, rows_below, mid_above, mid_below)
    potential, to_next, to_prev = call_second_potential(part, sums)
    end_above, end_below = exchange(to_next, to_prev, count)
    eta = call_second_step(group_of, group_mobility, eta, solute, sums, mid_above, mid_below)
    solute = call_solute_end(solute, potential, end_above, end_below)
    return eta, solute


def solution(mesh):
    fine = Mesh(mesh.devices.reshape(2, 8, 2, 4, 4), SPACE + GRAIN)
    placed = (
        P(None, SPACE, None),
        P(GRAIN),
        P(),
        P(GRAIN, None, SPACE, None),
        P(None, SPACE, None),
    )
    return jax.shard_map(
        shards,
        mesh=fine,
        in_specs=placed,
        out_specs=(P(GRAIN, None, SPACE, None), P(None, SPACE, None)),
        check_vma=False,
    )
```
